512 devices in a mesh: pb: 128 (over z, y, core), ka: 4 (over x).
Axes of the slice: x: 4, y: 8, z: 8, core: 2. Of those that a mesh axis runs over, the one named last changes fastest.
Arguments:
- queries: bfloat16 [32768, 1024], P('pb'), may hold values from -6 to 6
- keys: bfloat16 [32768, 128], P(('pb', 'ka')), may hold values from -6 to 6
- values: bfloat16 [32768, 128], P(('pb', 'ka')), may hold values from -6 to 6
- doc_lengths: int32 [8], replicated, may hold values from 1 to 24576, 32768 in all
Outputs:
- attended: bfloat16 [32768, 1024], P(('pb', 'ka'))
The draws below stay inside these ranges and needn't reach their ends.
All inputs are finite; a program needn't handle non-finite values.
Results may differ from the reference program's by a relative error of at most 0.009.
Values may be sent and summed in bfloat16 or wider, within the bound.
A program may use at most 64 MiB of HBM per device.

```python
import math
import jax
import jax.numpy as jnp
import numpy as np
from jax import lax

QHEADS = 8
HEAD_DIM = 128
DOCS = 8
SEQ = 32768
MOST = 24576


def draw_queries(key, part):
    key = jax.random.fold_in(key, 1)
    drawn = jnp.clip(jax.random.normal(key, (SEQ, QHEADS * HEAD_DIM), jnp.float32), -6.0, 6.0)
    return drawn.astype(jnp.bfloat16)


def draw_keys(key, part):
    key = jax.random.fold_in(key, 2)
    drawn = jnp.clip(jax.random.normal(key, (SEQ, HEAD_DIM), jnp.float32), -6.0, 6.0)
    return drawn.astype(jnp.bfloat16)


def steps_of(rng, dims, shards, low, largest):
    loudness = 1.0
    for dim, blocks in shards:
        draws = jax.random.uniform(jax.random.fold_in(jax.random.fold_in(rng, 6), dim), (blocks,), jnp.float32, low / len(shards), largest / len(shards))
        loudness = loudness * jnp.repeat(jnp.exp(draws), dims[dim] // blocks).reshape((-1,) + (1,) * (len(dims) - 1 - dim))
    return loudness


def split_up(number_of, total, most, slope):
    weights = [(1 << 20) // math.isqrt(rank ** slope) + 1 for rank in range(2, number_of + 1)]
    surplus, holding = total - most - (number_of - 1), [1] * (number_of - 1)
    while surplus > 0:
        candidates = [i for i in range(number_of - 1) if holding[i] < most]
        whole, remaining = sum([weights[i] for i in candidates]), surplus
        for i in candidates:
            extra = min(most - holding[i], max(1, remaining * weights[i] // whole), surplus)
            holding[i] = holding[i] + extra
            surplus = surplus - extra
    return np.array([most] + holding)


def ragged(key, number_of, total, limit, skew):
    if number_of == 2:
        one = jax.random.randint(key, (), max(1, total - limit), min(limit, total - 1) + 1)
        return jnp.stack([one, total - one])
    tallies = jnp.asarray(split_up(number_of, total, limit, skew), jnp.int32)
    pairs = (number_of - 1) // 2
    giver, taker = tallies[1:1 + 2 * pairs:2], tallies[2:2 + 2 * pairs:2]
    slack = jnp.minimum(giver - 1, limit - taker)
    passed = jax.random.randint(jax.random.fold_in(key, 1), (pairs,), 0, 1 << 20) % (slack + 1)
    tallies = tallies.at[1:1 + 2 * pairs:2].set(giver - passed).at[2:2 + 2 * pairs:2].set(taker + passed)
    return tallies[jax.random.permutation(jax.random.fold_in(key, 2), number_of)]


def normal_values(stream_key, extent, width, limit, split=(), kind=jnp.bfloat16):
    values = jax.random.normal(stream_key, extent, jnp.float32) * width
    if len(split) > 0:
        values = steps_of(stream_key, extent, split, -0.22, 0.18) * values
    return jnp.clip(values, min=-limit, max=limit).astype(kind)


def setup_inputs(seed: int = 0) -> dict:
    splits = jax.random.split(jax.random.key(seed), 5)
    queries = draw_queries(jax.random.fold_in(splits[4], 71), 0)
    keys = draw_keys(jax.random.fold_in(splits[4], 71), 0)
    values = normal_values(splits[2], (SEQ, HEAD_DIM), 1.0, 6.0, ((0, 512),))
    doc_lengths = ragged(splits[3], DOCS, SEQ, MOST, 2).astype(jnp.int32)
    return dict(queries=queries, keys=keys, values=values, doc_lengths=doc_lengths)


def reference(queries, keys, values, doc_lengths):
    doc_ends = jnp.cumsum(doc_lengths).astype(jnp.int32)
    positions = jnp.arange(SEQ, dtype=jnp.int32)
    segment = jnp.sum((positions[:, None] >= doc_ends[None, :]).astype(jnp.int32), axis=1).astype(jnp.int32)
    scaling = HEAD_DIM ** -0.5
    key_float = keys.astype(jnp.float32)
    value_float = values.astype(jnp.float32)
    block_len = min(512, SEQ)

    def one_block(block_index):
        start = (block_index * block_len).astype(jnp.int32)
        q_block = lax.dynamic_slice_in_dim(queries, start, block_len, 0)
        q_block = q_block.reshape(block_len, QHEADS, HEAD_DIM).astype(jnp.float32)
        q_pos = start + jnp.arange(block_len, dtype=jnp.int32)
        q_seg = lax.dynamic_slice_in_dim(segment, start, block_len, 0)
        visible = (positions[None, :] <= q_pos[:, None]) & (segment[None, :] == q_seg[:, None])
        scores = jnp.einsum("qhd,kd->qhk", q_block, key_float) * scaling
        scores = jnp.where(visible[:, None, :], scores, -1e30)
        row_max = jnp.max(scores, axis=-1)
        weights = jnp.where(visible[:, None, :], jnp.exp(scores - row_max[..., None]), 0.0)
        totals = jnp.sum(weights, axis=-1)
        rounded = lax.optimization_barrier(weights.astype(jnp.bfloat16)).astype(jnp.float32)
        numer = jnp.einsum("qhk,kd->qhd", rounded, value_float)
        output = numer / totals[..., None]
        return output.reshape(block_len, QHEADS * HEAD_DIM).astype(jnp.bfloat16)

    blocks = lax.map(one_block, jnp.arange(SEQ // block_len, dtype=jnp.int32))
    return blocks.reshape(SEQ, QHEADS * HEAD_DIM)
```

```python
import functools
import math

import jax
import jax.numpy as jnp
from jax import lax
from jax.experimental import pallas as pl
from jax.experimental.pallas import tpu as pltpu
from jax.sharding import PartitionSpec as P

HEADS = 8
DIM = 128
DOCS = 8
MOST = 24576
LANES = 128
FACTOR = math.log2(math.e) / math.sqrt(DIM)
MASK = 131072.0
EMPTY = -65536.0
NOTHING = -1e30


def place(c, first, second):
    z = second * (1 - c) + first * c
    y = first * (1 - c) + second * c
    return z, y


def kernel(
    ring, lanes, q_ref, k_ref, v_ref, len_ref, out_ref,
    kv, kfeat, qcat, acc, tot, top, obuf, lbuf, rbuf, rlse,
    s_one, r_one, s_fwd, r_fwd, s_bwd, r_bwd, s_sib, r_sib, s_out, r_out, s_lse, r_lse,
):
    half = ring // 2
    rows = q_ref.shape[0]
    own = k_ref.shape[0]
    chunk = ring * own
    plane = ring * 2 * rows
    me = lax.axis_index("pb")
    x = lax.axis_index("ka")
    c = lax.rem(me, 2)
    z = me // (2 * ring)
    y = lax.rem(me // 2, ring)
    p1 = y * (1 - c) + z * c
    p2 = z * (1 - c) + y * c

    def wrap(value):
        return lax.rem(value + 2 * ring, ring)

    def device(first, second):
        zz, yy = place(c, wrap(first), wrap(second))
        return {"pb": (zz * ring + yy) * 2 + c}

    sibling = {"pb": me + 1 - 2 * c}

    barrier = pltpu.get_barrier_semaphore()
    partners = [device(p1 + d, p2) for d in range(1, ring)]
    partners += [device(p1, p2 + d) for d in ((1, ring - 1) if ring > 2 else (1,))]
    partners += [sibling]
    partners += [{"ka": lax.rem(x + d, lanes)} for d in range(1, lanes)]
    for partner in partners:
        pl.semaphore_signal(barrier, inc=1, device_id=partner, device_id_type=pl.DeviceIdType.MESH)
    kv[c, p2, p1, :, :DIM] = k_ref[...]
    kv[c, p2, p1, :, DIM:] = v_ref[...]
    pl.semaphore_wait(barrier, len(partners))

    def copy(ref, send, recv, where):
        return pltpu.make_async_remote_copy(
            src_ref=ref, dst_ref=ref, send_sem=send, recv_sem=recv,
            device_id=where, device_id_type=pl.DeviceIdType.MESH,
        )

    def one_copy(d, b1):
        return copy(kv.at[c, p2, wrap(b1)], s_one.at[d - 1], r_one.at[d - 1], device(p1 + d, p2))

    def piece(cc, b, part):
        if part is None:
            return kv.at[cc, wrap(b)]
        return kv.at[cc, wrap(b), pl.ds(part * half, half)]

    def fwd_copy(s, b, last):
        return copy(piece(c, b, 0 if last else None), s_fwd.at[s - 1], r_fwd.at[s - 1], device(p1, p2 + 1))

    def bwd_copy(s, b, last):
        return copy(piece(c, b, 1 if last else None), s_bwd.at[s - 1], r_bwd.at[s - 1], device(p1, p2 - 1))

    def sib_copy(n, cc, b, part):
        return copy(piece(cc, b, part), s_sib.at[n], r_sib.at[n], sibling)

    def ring_start(s, last):
        fwd_copy(s, p2 - s + 1, last).start()
        bwd_copy(s, p2 + s - 1, last).start()

    def ring_arrived(s, last):
        fwd_copy(s, p2 - s, last).wait_recv()
        sib_copy(2 * s - 1, c, p2 - s, 0 if last else None).start()
        bwd_copy(s, p2 + s, last).wait_recv()
        sib_copy(2 * s, c, p2 + s, 1 if last else None).start()

    def sib_arrived(s, last):
        sib_copy(2 * s - 1, 1 - c, p1 - s, 0 if last else None).wait_recv()
        sib_copy(2 * s, 1 - c, p1 + s, 1 if last else None).wait_recv()

    for d in range(1, ring):
        one_copy(d, p1).start()

    lane = lax.broadcasted_iota(jnp.int32, (1, LANES), 1)
    ends = jnp.zeros((1, LANES), jnp.int32)
    begins = jnp.zeros((1, LANES), jnp.int32)
    for j in range(DOCS):
        length = len_ref[j]
        ends += jnp.where(lane >= j, length, 0)
        begins += jnp.where(lane > j, length, 0)
    tok = lax.broadcasted_iota(jnp.int32, (rows, LANES), 0)
    col = lax.broadcasted_iota(jnp.int32, (rows, LANES), 1)
    pos = me * rows + tok
    hidden = jnp.where((col < DOCS) & ((pos < begins) | (pos >= ends)), -MASK, 0.0)
    hidden = jnp.where(col == DOCS, -MASK, hidden)
    first = col - 2 * DOCS
    later = (first >= 0) & (first < own) & (tok < x * own + first)
    hidden = jnp.where(later, -MASK, hidden).astype(jnp.bfloat16)
    for h in range(HEADS):
        qcat[h * rows : (h + 1) * rows, :DIM] = q_ref[:, h * DIM : (h + 1) * DIM]
        qcat[h * rows : (h + 1) * rows, DIM:] = hidden
    acc[...] = jnp.zeros_like(acc)
    tot[...] = jnp.zeros_like(tot)
    top[...] = jnp.full_like(top, EMPTY)

    def features(n, carry):
        cc, b = n // ring, lax.rem(n, ring)
        inner = lax.broadcasted_iota(jnp.int32, (own, LANES), 0)
        lanes_of = lax.broadcasted_iota(jnp.int32, (own, LANES), 1)
        for a in range(ring):
            zz, yy = place(cc, a, b)
            block = (zz * ring + yy) * 2 + cc
            at = block * rows + x * own + inner
            mark = ((at >= begins) & (at < ends)).astype(jnp.float32)
            mark = jnp.where((lanes_of == DOCS) & (block > me), 1.0, mark)
            mark = jnp.where((lanes_of == inner + 2 * DOCS) & (block == me), 1.0, mark)
            kfeat[cc, b, a * own : (a + 1) * own, :] = mark.astype(jnp.bfloat16)
        return carry

    lax.fori_loop(0, 2 * ring, features, 0)

    ones = jnp.ones((chunk, LANES), jnp.bfloat16)

    def scores(h, cc, b):
        q = qcat[h * rows : (h + 1) * rows, :]
        keys = jnp.concatenate([kv[cc, b, :, :, :DIM].reshape(chunk, DIM), kfeat[cc, b]], axis=1)
        return lax.dot_general(q, keys, (((1,), (1,)), ((), ())), preferred_element_type=jnp.float32)

    def fold(h, cc, b, s):
        at = slice(h * rows, (h + 1) * rows)
        old = top[at, :]
        new = jnp.maximum(old, jnp.max(s, axis=1, keepdims=True))
        wide = jnp.concatenate([new] * (chunk // LANES), axis=1)
        p = jnp.exp2((s - wide) * FACTOR).astype(jnp.bfloat16)
        vals = jnp.concatenate([kv[cc, b, :, :, DIM:].reshape(chunk, DIM), ones], axis=1)
        both = jnp.dot(p, vals, preferred_element_type=jnp.float32)
        alpha = jnp.exp2((old - new) * FACTOR)
        acc[at, :] = acc[at, :] * alpha + both[:, :DIM]
        tot[at, :] = tot[at, :] * alpha + both[:, DIM:]
        top[at, :] = new

    def needed(cc, b):
        seen = (b <= z) & ((b + 1) * plane > me * rows - (MOST - 1))
        return (cc == 1) | seen

    def unit(cc, b):
        @pl.when(needed(cc, b))
        def _():
            s = scores(0, cc, b)
            for h in range(HEADS):
                after = scores(h + 1, cc, b) if h + 1 < HEADS else None
                fold(h, cc, b, s)
                s = after

    def pair(cc, base, s):
        def body(i, carry):
            unit(cc, wrap(base + (2 * i - 1) * s))
            return carry

        lax.fori_loop(0, 2, body, 0)

    for d in range(1, ring):
        one_copy(d, p1 - d).wait_recv()
    ring_start(1, half == 1)
    sib_copy(0, c, p2, None).start()
    unit(c, p2)
    ring_arrived(1, half == 1)
    if half > 1:
        ring_start(2, half == 2)
    sib_copy(0, 1 - c, p1, None).wait_recv()
    unit(1 - c, p1)

    def step(s, carry):
        pair(c, p2, s)

        @pl.when(s + 1 < half)
        def _():
            ring_arrived(s + 1, False)

        @pl.when(s + 1 == half)
        def _():
            ring_arrived(s + 1, True)

        @pl.when(s + 2 < half)
        def _():
            ring_start(s + 2, False)

        @pl.when(s + 2 == half)
        def _():
            ring_start(s + 2, True)

        sib_arrived(s, False)
        pair(1 - c, p1, s)
        return carry

    lax.fori_loop(1, half, step, 0)
    sib_arrived(half, True)

    def out_copy(d, g):
        cols = pl.ds(g * 2 * DIM, 2 * DIM)
        return pltpu.make_async_remote_copy(
            src_ref=obuf.at[lax.rem(x + d, lanes), :, cols], dst_ref=rbuf.at[d, :, cols],
            send_sem=s_out.at[d, g], recv_sem=r_out.at[d, g],
            device_id={"ka": lax.rem(x + d, lanes)}, device_id_type=pl.DeviceIdType.MESH,
        )

    def lse_copy(d):
        return pltpu.make_async_remote_copy(
            src_ref=lbuf.at[lax.rem(x + d, lanes)], dst_ref=rlse.at[d],
            send_sem=s_lse.at[d], recv_sem=r_lse.at[d],
            device_id={"ka": lax.rem(x + d, lanes)}, device_id_type=pl.DeviceIdType.MESH,
        )

    last = ((c, wrap(p2 + half)), (1 - c, wrap(p1 + half)))
    logs = jnp.zeros((rows, LANES), jnp.float32)
    work = [(h, cc, b) for h in range(HEADS) for cc, b in last]
    s = scores(*work[0])
    for n, (h, cc, b) in enumerate(work):
        after = scores(*work[n + 1]) if n + 1 < len(work) else None
        fold(h, cc, b, s)
        s = after
        if n % 2 == 1:
            at = slice(h * rows, (h + 1) * rows)
            total = tot[at, :]
            some = total > 0.0
            safe = jnp.where(some, total, 1.0)
            part = (acc[at, :] / safe).astype(jnp.bfloat16)
            size = jnp.where(some, top[at, :] * FACTOR + jnp.log2(safe), NOTHING)
            logs = jnp.where(col == h, size, logs)
            for j in range(lanes):
                obuf[j, :, h * DIM : (h + 1) * DIM] = part[j * own : (j + 1) * own, :]
            if h % 2 == 1:
                for d in range(1, lanes):
                    out_copy(d, h // 2).start()
    for j in range(lanes):
        lbuf[j] = logs[j * own : (j + 1) * own, :]
    for d in range(1, lanes):
        lse_copy(d).start()
    for d in range(1, lanes):
        lse_copy(d).wait_recv()
    sizes = [lbuf[x]] + [rlse[d] for d in range(1, lanes)]
    highest = functools.reduce(jnp.maximum, sizes)
    shares = [jnp.exp2(size - highest) for size in sizes]
    whole = functools.reduce(jnp.add, shares)
    shares = [share / whole for share in shares]
    for g in range(HEADS // 2):
        for d in range(1, lanes):
            out_copy(d, g).wait_recv()
        for h in (2 * g, 2 * g + 1):
            cols = slice(h * DIM, (h + 1) * DIM)
            mixed = shares[0][:, h : h + 1] * obuf[x, :, cols].astype(jnp.float32)
            for d in range(1, lanes):
                mixed += shares[d][:, h : h + 1] * rbuf[d, :, cols].astype(jnp.float32)
            out_ref[:, cols] = mixed.astype(out_ref.dtype)

    for d in range(1, ring):
        one_copy(d, p1).wait_send()
    for s in range(1, half + 1):
        fwd_copy(s, p2 - s + 1, s == half).wait_send()
        bwd_copy(s, p2 + s - 1, s == half).wait_send()
        sib_copy(2 * s - 1, c, p2 - s, 0 if s == half else None).wait_send()
        sib_copy(2 * s, c, p2 + s, 1 if s == half else None).wait_send()
    sib_copy(0, c, p2, None).wait_send()
    for d in range(1, lanes):
        lse_copy(d).wait_send()
        for g in range(HEADS // 2):
            out_copy(d, g).wait_send()


def per_device(ring, lanes, queries, keys, values, doc_lengths):
    rows, own = queries.shape[0], keys.shape[0]
    half = ring // 2
    chunk = ring * own
    vmem = pl.BlockSpec(memory_space=pltpu.VMEM)
    sems = pltpu.SemaphoreType.DMA
    return pl.pallas_call(
        functools.partial(kernel, ring, lanes),
        out_shape=jax.ShapeDtypeStruct((own, HEADS * DIM), jnp.bfloat16),
        in_specs=[vmem, vmem, vmem, pl.BlockSpec(memory_space=pltpu.SMEM)],
        out_specs=vmem,
        scratch_shapes=[
            pltpu.VMEM((2, ring, ring, own, 2 * DIM), jnp.bfloat16),
            pltpu.VMEM((2, ring, chunk, LANES), jnp.bfloat16),
            pltpu.VMEM((HEADS * rows, 2 * DIM), jnp.bfloat16),
            pltpu.VMEM((HEADS * rows, LANES), jnp.float32),
            pltpu.VMEM((HEADS * rows, LANES), jnp.float32),
            pltpu.VMEM((HEADS * rows, LANES), jnp.float32),
            pltpu.VMEM((lanes, own, HEADS * DIM), jnp.bfloat16),
            pltpu.VMEM((lanes, own, LANES), jnp.float32),
            pltpu.VMEM((lanes, own, HEADS * DIM), jnp.bfloat16),
            pltpu.VMEM((lanes, own, LANES), jnp.float32),
            sems((ring - 1,)), sems((ring - 1,)),
            sems((half,)), sems((half,)), sems((half,)), sems((half,)),
            sems((2 * half + 1,)), sems((2 * half + 1,)),
            sems((lanes, HEADS // 2)), sems((lanes, HEADS // 2)),
            sems((lanes,)), sems((lanes,)),
        ],
        compiler_params=pltpu.CompilerParams(
            collective_id=0, has_side_effects=True, vmem_limit_bytes=48 * 1024 * 1024
        ),
        cost_estimate=pl.CostEstimate(flops=10**10, bytes_accessed=10**7, transcendentals=10**7),
        name="attend",
    )(queries, keys, values, doc_lengths)


def solution(mesh):
    ring = math.isqrt(mesh.shape["pb"] // 2)
    return jax.shard_map(
        functools.partial(per_device, ring, mesh.shape["ka"]),
        mesh=mesh,
        in_specs=(P("pb", None), P(("pb", "ka"), None), P(("pb", "ka"), None), P()),
        out_specs=P(("pb", "ka"), None),
        check_vma=False,
    )
```

```python
import functools
import math

import jax
import jax.numpy as jnp
from jax import lax
from jax.experimental import pallas as pl
from jax.experimental.pallas import tpu as pltpu
from jax.sharding import PartitionSpec as P

HEADS = 8
DIM = 128
DOCS = 8
MOST = 24576
LANES = 128
FACTOR = math.log2(math.e) / math.sqrt(DIM)
MASK = 131072.0
EMPTY = -65536.0
NOTHING = -1e30


def place(c, first, second):
    z = second * (1 - c) + first * c
    y = first * (1 - c) + second * c
    return z, y


def kernel(
    ring, lanes, q_hbm, k_hbm, v_hbm, len_hbm, out_ref,
    q_in, k_in, v_in, lens, stage, kv, kfeat, qcat, acc, tot, top, obuf, lbuf, rbuf, rlse,
    s_in, s_one, r_one, s_fwd, r_fwd, s_bwd, r_bwd, s_sib, r_sib, s_out, r_out, s_lse, r_lse,
):
    half = ring // 2
    rows = q_in.shape[0]
    own = k_in.shape[0]
    chunk = ring * own
    plane = ring * 2 * rows
    me = lax.axis_index("pb")
    x = lax.axis_index("ka")
    c = lax.rem(me, 2)
    z = me // (2 * ring)
    y = lax.rem(me // 2, ring)
    p1 = y * (1 - c) + z * c
    p2 = z * (1 - c) + y * c

    def wrap(value):
        return lax.rem(value + 2 * ring, ring)

    def device(first, second):
        zz, yy = place(c, wrap(first), wrap(second))
        return {"pb": (zz * ring + yy) * 2 + c}

    sibling = {"pb": me + 1 - 2 * c}

    barrier = pltpu.get_barrier_semaphore()
    partners = [device(p1 + d, p2) for d in range(1, ring)]
    partners += [device(p1, p2 + d) for d in ((1, ring - 1) if ring > 2 else (1,))]
    partners += [sibling]
    partners += [{"ka": lax.rem(x + d, lanes)} for d in range(1, lanes)]
    for partner in partners:
        pl.semaphore_signal(barrier, inc=1, device_id=partner, device_id_type=pl.DeviceIdType.MESH)
    moves = [
        pltpu.make_async_copy(src, dst, s_in.at[n])
        for n, (src, dst) in enumerate(((k_hbm, k_in), (v_hbm, v_in), (len_hbm, lens), (q_hbm, q_in)))
    ]
    for move in moves:
        move.start()
    moves[0].wait()
    moves[1].wait()
    stage[p1, :, :DIM] = k_in[...]
    stage[p1, :, DIM:] = v_in[...]
    pl.semaphore_wait(barrier, len(partners))

    def copy(ref, send, recv, where):
        return pltpu.make_async_remote_copy(
            src_ref=ref, dst_ref=ref, send_sem=send, recv_sem=recv,
            device_id=where, device_id_type=pl.DeviceIdType.MESH,
        )

    def one_copy(d, b1):
        return copy(stage.at[wrap(b1)], s_one.at[d - 1], r_one.at[d - 1], device(p1 + d, p2))

    def piece(cc, b, part):
        if part is None:
            return kv.at[cc, wrap(b)]
        return kv.at[cc, wrap(b), part]

    def fwd_copy(s, b, last):
        return copy(piece(c, b, 0 if last else None), s_fwd.at[s - 1], r_fwd.at[s - 1], device(p1, p2 + 1))

    def bwd_copy(s, b, last):
        return copy(piece(c, b, 1 if last else None), s_bwd.at[s - 1], r_bwd.at[s - 1], device(p1, p2 - 1))

    def sib_copy(n, cc, b, part):
        return copy(piece(cc, b, part), s_sib.at[n], r_sib.at[n], sibling)

    def ring_start(s, last):
        fwd_copy(s, p2 - s + 1, last).start()
        bwd_copy(s, p2 + s - 1, last).start()

    def ring_arrived(s, last):
        fwd_copy(s, p2 - s, last).wait_recv()
        sib_copy(2 * s - 1, c, p2 - s, 0 if last else None).start()
        bwd_copy(s, p2 + s, last).wait_recv()
        sib_copy(2 * s, c, p2 + s, 1 if last else None).start()

    def sib_arrived(s, last):
        sib_copy(2 * s - 1, 1 - c, p1 - s, 0 if last else None).wait_recv()
        sib_copy(2 * s, 1 - c, p1 + s, 1 if last else None).wait_recv()

    for d in range(1, ring):
        one_copy(d, p1).start()
    moves[2].wait()
    moves[3].wait()

    lane = lax.broadcasted_iota(jnp.int32, (1, LANES), 1)
    line = lax.broadcasted_iota(jnp.int32, (LANES, 1), 0)
    ends = jnp.zeros((1, LANES), jnp.int32)
    begins = jnp.zeros((1, LANES), jnp.int32)
    ends_down = jnp.zeros((LANES, 1), jnp.int32)
    begins_down = jnp.zeros((LANES, 1), jnp.int32)
    for j in range(DOCS):
        length = lens[j]
        ends += jnp.where(lane >= j, length, 0)
        begins += jnp.where(lane > j, length, 0)
        ends_down += jnp.where(line >= j, length, 0)
        begins_down += jnp.where(line > j, length, 0)
    tok = lax.broadcasted_iota(jnp.int32, (LANES, rows), 1)
    col = lax.broadcasted_iota(jnp.int32, (LANES, rows), 0)
    pos = me * rows + tok
    hidden = jnp.where((col < DOCS) & ((pos < begins_down) | (pos >= ends_down)), -MASK, 0.0)
    hidden = jnp.where(col == DOCS, -MASK, hidden)
    first = col - 2 * DOCS
    later = (first >= 0) & (first < own) & (tok < x * own + first)
    hidden = jnp.where(later, -MASK, hidden).astype(jnp.bfloat16)
    for h in range(HEADS):
        qcat[:DIM, h * rows : (h + 1) * rows] = q_in[:, h * DIM : (h + 1) * DIM].T
        qcat[DIM:, h * rows : (h + 1) * rows] = hidden
    acc[...] = jnp.zeros_like(acc)
    tot[...] = jnp.zeros_like(tot)
    top[...] = jnp.full_like(top, EMPTY)

    def features(n, carry):
        cc, b = n // ring, lax.rem(n, ring)
        inner = lax.broadcasted_iota(jnp.int32, (own, LANES), 0)
        lanes_of = lax.broadcasted_iota(jnp.int32, (own, LANES), 1)
        for a in range(ring):
            zz, yy = place(cc, a, b)
            block = (zz * ring + yy) * 2 + cc
            at = block * rows + x * own + inner
            mark = ((at >= begins) & (at < ends)).astype(jnp.float32)
            mark = jnp.where((lanes_of == DOCS) & (block > me), 1.0, mark)
            mark = jnp.where((lanes_of == inner + 2 * DOCS) & (block == me), 1.0, mark)
            kfeat[cc, b, a * own : (a + 1) * own, :] = mark.astype(jnp.bfloat16)
        return carry

    lax.fori_loop(0, 2 * ring, features, 0)

    ones = jnp.ones((16, chunk), jnp.bfloat16)

    def scores(h, cc, b):
        keys = jnp.concatenate([kv[cc, b, 0], kfeat[cc, b]], axis=1)
        return jnp.dot(keys, qcat[:, h * rows : (h + 1) * rows], preferred_element_type=jnp.float32)

    def fold(h, cc, b, s):
        old = top[h : h + 1, :]
        new = jnp.maximum(old, jnp.max(s, axis=0, keepdims=True))
        p = jnp.exp2((s - new) * FACTOR).astype(jnp.bfloat16)
        vals = jnp.concatenate([kv[cc, b, 1, n : n + LANES] for n in range(0, chunk, LANES)], axis=1)
        both = jnp.dot(jnp.concatenate([vals, ones], axis=0), p, preferred_element_type=jnp.float32)
        alpha = jnp.exp2((old - new) * FACTOR)
        acc[h] = acc[h] * alpha + both[:DIM]
        tot[h : h + 1, :] = tot[h : h + 1, :] * alpha + both[DIM : DIM + 1]
        top[h : h + 1, :] = new

    def needed(cc, b):
        seen = (b <= z) & ((b + 1) * plane > me * rows - (MOST - 1))
        return (cc == 1) | seen

    def unit(cc, b):
        @pl.when(needed(cc, b))
        def _():
            s = scores(0, cc, b)
            for h in range(HEADS):
                after = scores(h + 1, cc, b) if h + 1 < HEADS else None
                fold(h, cc, b, s)
                s = after

    def pair(cc, base, s):
        def body(i, carry):
            unit(cc, wrap(base + (2 * i - 1) * s))
            return carry

        lax.fori_loop(0, 2, body, 0)

    for d in range(1, ring):
        one_copy(d, p1 - d).wait_recv()
    for n in range(ring):
        kv[c, p2, 0, n * own : (n + 1) * own] = stage[n, :, :DIM]
    side = LANES // own
    for n in range(ring // side):
        block = stage[n * side : (n + 1) * side, :, DIM:].reshape(LANES, DIM)
        kv[c, p2, 1, n * LANES : (n + 1) * LANES] = block.T
    ring_start(1, half == 1)
    sib_copy(0, c, p2, None).start()
    unit(c, p2)
    ring_arrived(1, half == 1)
    if half > 1:
        ring_start(2, half == 2)
    sib_copy(0, 1 - c, p1, None).wait_recv()
    unit(1 - c, p1)

    def step(s, carry):
        pair(c, p2, s)

        @pl.when(s + 1 < half)
        def _():
            ring_arrived(s + 1, False)

        @pl.when(s + 1 == half)
        def _():
            ring_arrived(s + 1, True)

        @pl.when(s + 2 < half)
        def _():
            ring_start(s + 2, False)

        @pl.when(s + 2 == half)
        def _():
            ring_start(s + 2, True)

        sib_arrived(s, False)
        pair(1 - c, p1, s)
        return carry

    lax.fori_loop(1, half, step, 0)
    sib_arrived(half, True)

    def out_copy(d, g):
        cols = pl.ds(g * 2 * DIM, 2 * DIM)
        return pltpu.make_async_remote_copy(
            src_ref=obuf.at[lax.rem(x + d, lanes), :, cols], dst_ref=rbuf.at[d, :, cols],
            send_sem=s_out.at[d, g], recv_sem=r_out.at[d, g],
            device_id={"ka": lax.rem(x + d, lanes)}, device_id_type=pl.DeviceIdType.MESH,
        )

    def lse_copy(d):
        return pltpu.make_async_remote_copy(
            src_ref=lbuf.at[lax.rem(x + d, lanes)], dst_ref=rlse.at[d],
            send_sem=s_lse.at[d], recv_sem=r_lse.at[d],
            device_id={"ka": lax.rem(x + d, lanes)}, device_id_type=pl.DeviceIdType.MESH,
        )

    last = ((c, wrap(p2 + half)), (1 - c, wrap(p1 + half)))
    logs = []
    work = [(h, cc, b) for h in range(HEADS) for cc, b in last]
    s = scores(*work[0])
    for n, (h, cc, b) in enumerate(work):
        after = scores(*work[n + 1]) if n + 1 < len(work) else None
        fold(h, cc, b, s)
        s = after
        if n % 2 == 1:
            total = tot[h : h + 1, :]
            some = total > 0.0
            safe = jnp.where(some, total, 1.0)
            part = (acc[h] / safe).T.astype(jnp.bfloat16)
            logs.append(jnp.where(some, top[h : h + 1, :] * FACTOR + jnp.log2(safe), NOTHING))
            for j in range(lanes):
                obuf[j, :, h * DIM : (h + 1) * DIM] = part[j * own : (j + 1) * own, :]
            if h % 2 == 1:
                for d in range(1, lanes):
                    out_copy(d, h // 2).start()
    logs.append(jnp.zeros((LANES - HEADS, rows), jnp.float32))
    logs = jnp.concatenate(logs, axis=0).T
    for j in range(lanes):
        lbuf[j] = logs[j * own : (j + 1) * own, :]
    for d in range(1, lanes):
        lse_copy(d).start()
    for d in range(1, lanes):
        lse_copy(d).wait_recv()
    sizes = [lbuf[x]] + [rlse[d] for d in range(1, lanes)]
    highest = functools.reduce(jnp.maximum, sizes)
    shares = [jnp.exp2(size - highest) for size in sizes]
    whole = functools.reduce(jnp.add, shares)
    shares = [share / whole for share in shares]
    for g in range(HEADS // 2):
        for d in range(1, lanes):
            out_copy(d, g).wait_recv()
        for h in (2 * g, 2 * g + 1):
            cols = slice(h * DIM, (h + 1) * DIM)
            mixed = shares[0][:, h : h + 1] * obuf[x, :, cols].astype(jnp.float32)
            for d in range(1, lanes):
                mixed += shares[d][:, h : h + 1] * rbuf[d, :, cols].astype(jnp.float32)
            out_ref[:, cols] = mixed.astype(out_ref.dtype)

    for d in range(1, ring):
        one_copy(d, p1).wait_send()
    for s in range(1, half + 1):
        fwd_copy(s, p2 - s + 1, s == half).wait_send()
        bwd_copy(s, p2 + s - 1, s == half).wait_send()
        sib_copy(2 * s - 1, c, p2 - s, 0 if s == half else None).wait_send()
        sib_copy(2 * s, c, p2 + s, 1 if s == half else None).wait_send()
    sib_copy(0, c, p2, None).wait_send()
    for d in range(1, lanes):
        lse_copy(d).wait_send()
        for g in range(HEADS // 2):
            out_copy(d, g).wait_send()


def per_device(ring, lanes, queries, keys, values, doc_lengths):
    rows, own = queries.shape[0], keys.shape[0]
    half = ring // 2
    chunk = ring * own
    vmem = pl.BlockSpec(memory_space=pltpu.VMEM)
    sems = pltpu.SemaphoreType.DMA
    return pl.pallas_call(
        functools.partial(kernel, ring, lanes),
        out_shape=jax.ShapeDtypeStruct((own, HEADS * DIM), jnp.bfloat16),
        in_specs=[pl.BlockSpec(memory_space=pl.ANY)] * 4,
        out_specs=vmem,
        scratch_shapes=[
            pltpu.VMEM(queries.shape, jnp.bfloat16),
            pltpu.VMEM(keys.shape, jnp.bfloat16),
            pltpu.VMEM(values.shape, jnp.bfloat16),
            pltpu.SMEM(doc_lengths.shape, jnp.int32),
            pltpu.VMEM((ring, own, 2 * DIM), jnp.bfloat16),
            pltpu.VMEM((2, ring, 2, chunk, DIM), jnp.bfloat16),
            pltpu.VMEM((2, ring, chunk, LANES), jnp.bfloat16),
            pltpu.VMEM((2 * DIM, HEADS * rows), jnp.bfloat16),
            pltpu.VMEM((HEADS, DIM, rows), jnp.float32),
            pltpu.VMEM((HEADS, rows), jnp.float32),
            pltpu.VMEM((HEADS, rows), jnp.float32),
            pltpu.VMEM((lanes, own, HEADS * DIM), jnp.bfloat16),
            pltpu.VMEM((lanes, own, LANES), jnp.float32),
            pltpu.VMEM((lanes, own, HEADS * DIM), jnp.bfloat16),
            pltpu.VMEM((lanes, own, LANES), jnp.float32),
            sems((4,)),
            sems((ring - 1,)), sems((ring - 1,)),
            sems((half,)), sems((half,)), sems((half,)), sems((half,)),
            sems((2 * half + 1,)), sems((2 * half + 1,)),
            sems((lanes, HEADS // 2)), sems((lanes, HEADS // 2)),
            sems((lanes,)), sems((lanes,)),
        ],
        compiler_params=pltpu.CompilerParams(
            collective_id=0, has_side_effects=True, vmem_limit_bytes=48 * 1024 * 1024
        ),
        cost_estimate=pl.CostEstimate(flops=10**10, bytes_accessed=10**7, transcendentals=10**7),
        name="attend",
    )(queries, keys, values, doc_lengths)


def solution(mesh):
    ring = math.isqrt(mesh.shape["pb"] // 2)
    return jax.shard_map(
        functools.partial(per_device, ring, mesh.shape["ka"]),
        mesh=mesh,
        in_specs=(P("pb", None), P(("pb", "ka"), None), P(("pb", "ka"), None), P()),
        out_specs=P(("pb", "ka"), None),
        check_vma=False,
    )
```

```python
import functools
import math

import jax
import jax.numpy as jnp
from jax import lax
from jax.experimental import pallas as pl
from jax.experimental.pallas import tpu as pltpu
from jax.sharding import PartitionSpec as P

HEADS = 8
DIM = 128
DOCS = 8
MOST = 24576
LANES = 128
FACTOR = math.log2(math.e) / math.sqrt(DIM)
MASK = 131072.0
EMPTY = -65536.0
NOTHING = -1e30
MESH = pl.DeviceIdType.MESH


def place(c, first, second):
    z = second * (1 - c) + first * c
    y = first * (1 - c) + second * c
    return z, y


def kernel(
    ring, lanes, q_hbm, k_hbm, v_hbm, len_hbm, out_ref,
    q_in, k_in, v_in, lens, stage, kv, kfeat, qcat, acc, tot, top, obuf, rbuf, logs, mixing,
    s_in, s_one, r_one, s_fwd, r_fwd, s_bwd, r_bwd, s_sib, r_sib, s_out, r_out, s_log, r_log,
):
    half = ring // 2
    rows = q_in.shape[0]
    own = k_in.shape[0]
    chunk = ring * own
    plane = ring * 2 * rows
    me = lax.axis_index("pb")
    x = lax.axis_index("ka")
    c = lax.rem(me, 2)
    z = me // (2 * ring)
    y = lax.rem(me // 2, ring)
    p1 = y * (1 - c) + z * c
    p2 = z * (1 - c) + y * c

    def wrap(value):
        return lax.rem(value + 2 * ring, ring)

    def device(first, second):
        zz, yy = place(c, wrap(first), wrap(second))
        return {"pb": (zz * ring + yy) * 2 + c}

    sibling = {"pb": me + 1 - 2 * c}

    barrier = pltpu.get_barrier_semaphore()
    partners = [device(p1 + d, p2) for d in range(1, ring)]
    partners += [device(p1, p2 + d) for d in ((1, ring - 1) if ring > 2 else (1,))]
    partners += [sibling]
    partners += [{"ka": lax.rem(x + d, lanes)} for d in range(1, lanes)]
    for partner in partners:
        pl.semaphore_signal(barrier, inc=1, device_id=partner, device_id_type=MESH)
    moves = [
        pltpu.make_async_copy(src, dst, s_in.at[n])
        for n, (src, dst) in enumerate(((k_hbm, k_in), (v_hbm, v_in), (len_hbm, lens), (q_hbm, q_in)))
    ]
    for move in moves:
        move.start()
    moves[0].wait()
    moves[1].wait()
    stage[p1, :, :DIM] = k_in[...]
    stage[p1, :, DIM:] = v_in[...]
    pl.semaphore_wait(barrier, len(partners))

    def copy(ref, send, recv, where):
        return pltpu.make_async_remote_copy(
            src_ref=ref, dst_ref=ref, send_sem=send, recv_sem=recv, device_id=where, device_id_type=MESH
        )

    def one_copy(d, b1):
        return copy(stage.at[wrap(b1)], s_one.at[d - 1], r_one.at[d - 1], device(p1 + d, p2))

    def piece(cc, b, p):
        return kv.at[cc, wrap(b), p // 2, pl.ds((p % 2) * (chunk // 2), chunk // 2)]

    def fwd_copy(s, b, p):
        return copy(piece(c, b, p), s_fwd.at[s - 1, p], r_fwd.at[s - 1, p], device(p1, p2 + 1))

    def bwd_copy(s, b, p):
        return copy(piece(c, b, p), s_bwd.at[s - 1, p], r_bwd.at[s - 1, p], device(p1, p2 - 1))

    def sib_copy(n, cc, b, p):
        return copy(piece(cc, b, p), s_sib.at[n, p], r_sib.at[n, p], sibling)

    def ring_arrived(s):
        for p in range(4):
            fwd_copy(s, p2 - s, p).wait_recv()
            onward = functools.partial(fwd_copy, s + 1, p2 - s, p)
            if p < 2:
                onward().start()
            else:
                pl.when(s + 1 < half)(lambda onward=onward: onward().start())
            sib_copy(2 * s - 1, c, p2 - s, p).start()
            bwd_copy(s, p2 + s, p).wait_recv()
            onward = functools.partial(bwd_copy, s + 1, p2 + s, p)
            if p >= 2:
                onward().start()
            else:
                pl.when(s + 1 < half)(lambda onward=onward: onward().start())
            sib_copy(2 * s, c, p2 + s, p).start()

    def ring_last():
        for p in range(2):
            fwd_copy(half, p2 - half, p).wait_recv()
            sib_copy(2 * half - 1, c, p2 - half, p).start()
            bwd_copy(half, p2 + half, p + 2).wait_recv()
            sib_copy(2 * half, c, p2 + half, p + 2).start()

    def sib_arrived(s):
        for p in range(4):
            sib_copy(2 * s - 1, 1 - c, p1 - s, p).wait_recv()
            sib_copy(2 * s, 1 - c, p1 + s, p).wait_recv()

    for d in range(1, ring):
        one_copy(d, p1).start()
    moves[2].wait()
    moves[3].wait()

    lane = lax.broadcasted_iota(jnp.int32, (1, LANES), 1)
    line = lax.broadcasted_iota(jnp.int32, (LANES, 1), 0)
    ends = jnp.zeros((1, LANES), jnp.int32)
    begins = jnp.zeros((1, LANES), jnp.int32)
    ends_down = jnp.zeros((LANES, 1), jnp.int32)
    begins_down = jnp.zeros((LANES, 1), jnp.int32)
    for j in range(DOCS):
        length = lens[j]
        ends += jnp.where(lane >= j, length, 0)
        begins += jnp.where(lane > j, length, 0)
        ends_down += jnp.where(line >= j, length, 0)
        begins_down += jnp.where(line > j, length, 0)
    tok = lax.broadcasted_iota(jnp.int32, (LANES, rows), 1)
    col = lax.broadcasted_iota(jnp.int32, (LANES, rows), 0)
    pos = me * rows + tok
    hidden = jnp.where((col < DOCS) & ((pos < begins_down) | (pos >= ends_down)), -MASK, 0.0)
    hidden = jnp.where(col == DOCS, -MASK, hidden)
    first = col - 2 * DOCS
    later = (first >= 0) & (first < own) & (tok < x * own + first)
    hidden = jnp.where(later, -MASK, hidden).astype(jnp.bfloat16)
    for h in range(HEADS):
        qcat[h, :DIM, :] = q_in[:, h * DIM : (h + 1) * DIM].T
        qcat[h, DIM:, :] = hidden
    acc[...] = jnp.zeros_like(acc)
    tot[...] = jnp.zeros_like(tot)
    top[...] = jnp.full_like(top, EMPTY)

    def features(n, carry):
        cc, b = n // ring, lax.rem(n, ring)
        inner = lax.broadcasted_iota(jnp.int32, (own, LANES), 0)
        lanes_of = lax.broadcasted_iota(jnp.int32, (own, LANES), 1)
        for a in range(ring):
            zz, yy = place(cc, a, b)
            block = (zz * ring + yy) * 2 + cc
            at = block * rows + x * own + inner
            mark = ((at >= begins) & (at < ends)).astype(jnp.float32)
            mark = jnp.where((lanes_of == DOCS) & (block > me), 1.0, mark)
            mark = jnp.where((lanes_of == inner + 2 * DOCS) & (block == me), 1.0, mark)
            kfeat[cc, b, a * own : (a + 1) * own, :] = mark.astype(jnp.bfloat16)
        return carry

    lax.fori_loop(0, 2 * ring, features, 0)

    ones = jnp.ones((16, chunk), jnp.bfloat16)

    def scores(h, cc, b):
        keys = jnp.concatenate([kv[cc, b, 0], kfeat[cc, b]], axis=1)
        return jnp.dot(keys, qcat[h], preferred_element_type=jnp.float32)

    def fold(h, cc, b, s):
        old = top[h]
        new = jnp.maximum(old, jnp.max(s, axis=0, keepdims=True))
        p = jnp.exp2((s - new) * FACTOR).astype(jnp.bfloat16)
        vals = jnp.concatenate([kv[cc, b, 1, n : n + LANES] for n in range(0, chunk, LANES)], axis=1)
        both = jnp.dot(jnp.concatenate([vals, ones], axis=0), p, preferred_element_type=jnp.float32)
        alpha = jnp.exp2((old - new) * FACTOR)
        acc[h] = acc[h] * alpha + both[:DIM]
        tot[h] = tot[h] * alpha + both[DIM : DIM + 1]
        top[h] = new

    def run(work):
        s = scores(*work[0])
        for n, item in enumerate(work):
            after = scores(*work[n + 1]) if n + 1 < len(work) else None
            fold(*item, s)
            s = after

    def needed(cc, b):
        seen = (b <= z) & ((b + 1) * plane > me * rows - (MOST - 1))
        return (cc == 1) | seen

    def unit(cc, b):
        @pl.when(needed(cc, b))
        def _():
            run([(h, cc, b) for h in range(HEADS)])

    for d in range(1, ring):
        one_copy(d, p1 - d).wait_recv()
    for n in range(ring):
        kv[c, p2, 0, n * own : (n + 1) * own] = stage[n, :, :DIM]
    for p in range(2):
        fwd_copy(1, p2, p).start()
        bwd_copy(1, p2, p).start()
        sib_copy(0, c, p2, p).start()
    side = LANES // own
    for n in range(ring // side):
        block = stage[n * side : (n + 1) * side, :, DIM:].reshape(LANES, DIM)
        kv[c, p2, 1, n * LANES : (n + 1) * LANES] = block.T
    for p in range(2, 4):
        fwd_copy(1, p2, p).start()
        bwd_copy(1, p2, p).start()
        sib_copy(0, c, p2, p).start()
    unit(c, p2)
    for p in range(4):
        sib_copy(0, 1 - c, p1, p).wait_recv()
    unit(1 - c, p1)
    ring_arrived(1)

    def step(s, carry):
        def mine(i, carry):
            unit(c, wrap(p2 + (2 * i - 1) * s))
            return carry

        def other(i, carry):
            unit(1 - c, wrap(p1 + (2 * i - 1) * s))

            @pl.when((s == half - 2) & (i == 0))
            def _():
                ring_last()

            return carry

        lax.fori_loop(0, 2, mine, 0)
        ring_arrived(s + 1)
        sib_arrived(s)
        lax.fori_loop(0, 2, other, 0)
        return carry

    lax.fori_loop(1, half - 1, step, 0)
    if half == 2:
        ring_last()
    sib_arrived(half - 1)
    for p in range(2):
        sib_copy(2 * half - 1, 1 - c, p1 - half, p).wait_recv()
        sib_copy(2 * half, 1 - c, p1 + half, p + 2).wait_recv()

    def peer(d):
        return lax.rem(x + d, lanes)

    def out_copy(d, h):
        cols = pl.ds(pl.multiple_of(h * DIM, DIM), DIM)
        return pltpu.make_async_remote_copy(
            src_ref=obuf.at[peer(d), :, cols], dst_ref=rbuf.at[d, :, cols],
            send_sem=s_out.at[d, h], recv_sem=r_out.at[d, h], device_id={"ka": peer(d)}, device_id_type=MESH,
        )

    def log_copy(d):
        return pltpu.make_async_remote_copy(
            src_ref=logs.at[0], dst_ref=logs.at[d],
            send_sem=s_log.at[d], recv_sem=r_log.at[d], device_id={"ka": peer(d)}, device_id_type=MESH,
        )

    late = [(c, p2 - half + 1), (c, p2 + half - 1), (1 - c, p1 - half + 1), (1 - c, p1 + half - 1)]
    late += [(c, p2 + half), (1 - c, p1 + half)]

    def finish(h, carry):
        run([(h, cc, wrap(b)) for cc, b in late])
        total = tot[h]
        some = total > 0.0
        safe = jnp.where(some, total, 1.0)
        part = (acc[h] / safe).T.astype(jnp.bfloat16)
        logs[0, h] = jnp.where(some, top[h] * FACTOR + jnp.log2(safe), NOTHING)
        cols = pl.ds(pl.multiple_of(h * DIM, DIM), DIM)
        for j in range(lanes):
            obuf[j, :, cols] = part[j * own : (j + 1) * own, :]
        for d in range(1, lanes):
            out_copy(d, h).start()
        return carry

    lax.fori_loop(0, HEADS, finish, 0)
    for d in range(1, lanes):
        log_copy(d).start()
    for d in range(1, lanes):
        log_copy(d).wait_recv()
    sizes = [jnp.concatenate([logs[d, h] for h in range(HEADS)], axis=0) for d in range(lanes)]
    highest = functools.reduce(jnp.maximum, sizes)
    shares = [jnp.exp2(size - highest) for size in sizes]
    whole = functools.reduce(jnp.add, shares)
    shares = [share / whole for share in shares]
    shares.append(jnp.zeros((LANES - HEADS * lanes, rows), jnp.float32))
    mixing[...] = jnp.concatenate(shares, axis=0).T
    mix = mixing[pl.ds(pl.multiple_of(x * own, own), own), :]
    for h in range(HEADS):
        cols = slice(h * DIM, (h + 1) * DIM)
        mixed = mix[:, h : h + 1] * obuf[x, :, cols].astype(jnp.float32)
        for d in range(1, lanes):
            out_copy(d, h).wait_recv()
            at = d * HEADS + h
            mixed += mix[:, at : at + 1] * rbuf[d, :, cols].astype(jnp.float32)
        out_ref[:, cols] = mixed.astype(out_ref.dtype)

    for d in range(1, ring):
        one_copy(d, p1).wait_send()
    for p in range(4):
        sib_copy(0, c, p2, p).wait_send()
    for s in range(1, half + 1):
        for p in range(4):
            if s < half or p < 2:
                fwd_copy(s, p2 - s + 1, p).wait_send()
                sib_copy(2 * s - 1, c, p2 - s, p).wait_send()
            if s < half or p >= 2:
                bwd_copy(s, p2 + s - 1, p).wait_send()
                sib_copy(2 * s, c, p2 + s, p).wait_send()
    for d in range(1, lanes):
        log_copy(d).wait_send()
        for h in range(HEADS):
            out_copy(d, h).wait_send()


def per_device(ring, lanes, queries, keys, values, doc_lengths):
    rows, own = queries.shape[0], keys.shape[0]
    half = ring // 2
    chunk = ring * own
    vmem = pl.BlockSpec(memory_space=pltpu.VMEM)
    sems = pltpu.SemaphoreType.DMA
    return pl.pallas_call(
        functools.partial(kernel, ring, lanes),
        out_shape=jax.ShapeDtypeStruct((own, HEADS * DIM), jnp.bfloat16),
        in_specs=[pl.BlockSpec(memory_space=pl.ANY)] * 4,
        out_specs=vmem,
        scratch_shapes=[
            pltpu.VMEM(queries.shape, jnp.bfloat16),
            pltpu.VMEM(keys.shape, jnp.bfloat16),
            pltpu.VMEM(values.shape, jnp.bfloat16),
            pltpu.SMEM(doc_lengths.shape, jnp.int32),
            pltpu.VMEM((ring, own, 2 * DIM), jnp.bfloat16),
            pltpu.VMEM((2, ring, 2, chunk, DIM), jnp.bfloat16),
            pltpu.VMEM((2, ring, chunk, LANES), jnp.bfloat16),
            pltpu.VMEM((HEADS, 2 * DIM, rows), jnp.bfloat16),
            pltpu.VMEM((HEADS, DIM, rows), jnp.float32),
            pltpu.VMEM((HEADS, 1, rows), jnp.float32),
            pltpu.VMEM((HEADS, 1, rows), jnp.float32),
            pltpu.VMEM((lanes, own, HEADS * DIM), jnp.bfloat16),
            pltpu.VMEM((lanes, own, HEADS * DIM), jnp.bfloat16),
            pltpu.VMEM((lanes, HEADS, 1, rows), jnp.float32),
            pltpu.VMEM((rows, LANES), jnp.float32),
            sems((4,)),
            sems((ring - 1,)), sems((ring - 1,)),
            sems((half, 4)), sems((half, 4)), sems((half, 4)), sems((half, 4)),
            sems((2 * half + 1, 4)), sems((2 * half + 1, 4)),
            sems((lanes, HEADS)), sems((lanes, HEADS)),
            sems((lanes,)), sems((lanes,)),
        ],
        compiler_params=pltpu.CompilerParams(
            collective_id=0, has_side_effects=True, vmem_limit_bytes=63 * 1024 * 1024
        ),
        cost_estimate=pl.CostEstimate(flops=10**10, bytes_accessed=10**7, transcendentals=10**7),
        name="attend",
    )(queries, keys, values, doc_lengths)


def solution(mesh):
    ring = math.isqrt(mesh.shape["pb"] // 2)
    return jax.shard_map(
        functools.partial(per_device, ring, mesh.shape["ka"]),
        mesh=mesh,
        in_specs=(P("pb", None), P(("pb", "ka"), None), P(("pb", "ka"), None), P()),
        out_specs=P(("pb", "ka"), None),
        check_vma=False,
    )
```

```python
import functools
import math

import jax
import jax.numpy as jnp
from jax import lax
from jax.experimental import pallas as pl
from jax.experimental.pallas import tpu as pltpu
from jax.sharding import PartitionSpec as P

HEADS = 8
DIM = 128
DOCS = 8
MOST = 24576
LANES = 128
FACTOR = math.log2(math.e) / math.sqrt(DIM)
MASK = 131072.0
EMPTY = -65536.0
NOTHING = -1e30
EXTRA = 16
SAFE = 100.0
MESH = pl.DeviceIdType.MESH


def place(c, first, second):
    z = second * (1 - c) + first * c
    y = first * (1 - c) + second * c
    return z, y


def swift_kernel(
    ring, lanes, q_hbm, k_hbm, v_hbm, len_hbm, out_ref, bound_ref,
    q_in, k_in, v_in, lens, stage, kv, kfeat, qcat, acc, tot, obuf, rbuf, sums, mixing,
    s_in, s_one, r_one, s_fwd, r_fwd, s_bwd, r_bwd, s_sib, r_sib, s_out, r_out, s_sum, r_sum,
):
    half = ring // 2
    rows = q_in.shape[0]
    own = k_in.shape[0]
    chunk = ring * own
    plane = ring * 2 * rows
    me = lax.axis_index("pb")
    x = lax.axis_index("ka")
    c = lax.rem(me, 2)
    z = me // (2 * ring)
    y = lax.rem(me // 2, ring)
    p1 = y * (1 - c) + z * c
    p2 = z * (1 - c) + y * c

    def wrap(value):
        return lax.rem(value + 2 * ring, ring)

    def device(first, second):
        zz, yy = place(c, wrap(first), wrap(second))
        return {"pb": (zz * ring + yy) * 2 + c}

    sibling = {"pb": me + 1 - 2 * c}

    barrier = pltpu.get_barrier_semaphore()
    partners = [device(p1 + d, p2) for d in range(1, ring)]
    partners += [device(p1, p2 + d) for d in ((1, ring - 1) if ring > 2 else (1,))]
    partners += [sibling]
    partners += [{"ka": lax.rem(x + d, lanes)} for d in range(1, lanes)]
    for partner in partners:
        pl.semaphore_signal(barrier, inc=1, device_id=partner, device_id_type=MESH)
    moves = [
        pltpu.make_async_copy(src, dst, s_in.at[n])
        for n, (src, dst) in enumerate(((k_hbm, k_in), (v_hbm, v_in), (len_hbm, lens), (q_hbm, q_in)))
    ]
    for move in moves:
        move.start()
    moves[0].wait()
    moves[1].wait()
    stage[p1, :own, :DIM] = k_in[...]
    stage[p1, :own, DIM:] = v_in[...]
    wide = k_in[...].astype(jnp.float32)
    longest = jnp.max(jnp.sum(wide * wide, axis=1, keepdims=True), axis=0, keepdims=True)
    stage[p1, own:, :DIM] = jnp.broadcast_to(longest * 1.01, (EXTRA, DIM)).astype(jnp.bfloat16)
    moves[3].wait()
    longest = jnp.zeros((rows, 1), jnp.float32)
    for h in range(HEADS):
        wide = q_in[:, h * DIM : (h + 1) * DIM].astype(jnp.float32)
        longest = jnp.maximum(longest, jnp.sum(wide * wide, axis=1, keepdims=True))
    longest = jnp.max(longest, axis=0, keepdims=True)
    stage[p1, own:, DIM:] = jnp.broadcast_to(longest * 1.01, (EXTRA, DIM)).astype(jnp.bfloat16)
    pl.semaphore_wait(barrier, len(partners))

    def copy(ref, send, recv, where):
        return pltpu.make_async_remote_copy(
            src_ref=ref, dst_ref=ref, send_sem=send, recv_sem=recv, device_id=where, device_id_type=MESH
        )

    def one_copy(d, b1):
        return copy(stage.at[wrap(b1)], s_one.at[d - 1], r_one.at[d - 1], device(p1 + d, p2))

    def piece(cc, b, i, q):
        return kv.at[cc, wrap(b), i, pl.ds(q * (chunk // 2), chunk // 2 + q * EXTRA)]

    def fwd_copy(s, b, i, q):
        n = 2 * i + q
        return copy(piece(c, b, i, q), s_fwd.at[s - 1, n], r_fwd.at[s - 1, n], device(p1, p2 + 1))

    def bwd_copy(s, b, i, q):
        n = 2 * i + q
        return copy(piece(c, b, i, q), s_bwd.at[s - 1, n], r_bwd.at[s - 1, n], device(p1, p2 - 1))

    def sib_copy(k, cc, b, i, q):
        n = 2 * i + q
        return copy(piece(cc, b, i, q), s_sib.at[k, n], r_sib.at[k, n], sibling)

    def pass_on(s, i):
        both = s + 1 < half
        for q in range(2):
            fwd_copy(s, p2 - s, i, q).wait_recv()
            pl.when(both | (i == 0))(lambda q=q: fwd_copy(s + 1, p2 - s, i, q).start())
            bwd_copy(s, p2 + s, i, q).wait_recv()
            pl.when(both | (i == 1))(lambda q=q: bwd_copy(s + 1, p2 + s, i, q).start())
        for q in range(2):
            sib_copy(2 * s - 1, c, p2 - s, i, q).start()
            sib_copy(2 * s, c, p2 + s, i, q).start()

    def pass_last():
        for q in range(2):
            fwd_copy(half, p2 - half, 0, q).wait_recv()
            sib_copy(2 * half - 1, c, p2 - half, 0, q).start()
            bwd_copy(half, p2 + half, 1, q).wait_recv()
            sib_copy(2 * half, c, p2 + half, 1, q).start()

    def sib_arrived(s):
        for i in range(2):
            for q in range(2):
                sib_copy(2 * s - 1, 1 - c, p1 - s, i, q).wait_recv()
                sib_copy(2 * s, 1 - c, p1 + s, i, q).wait_recv()

    for d in range(1, ring):
        one_copy(d, p1).start()
    moves[2].wait()

    lane = lax.broadcasted_iota(jnp.int32, (1, LANES), 1)
    line = lax.broadcasted_iota(jnp.int32, (LANES, 1), 0)
    ends = jnp.zeros((1, LANES), jnp.int32)
    begins = jnp.zeros((1, LANES), jnp.int32)
    ends_down = jnp.zeros((LANES, 1), jnp.int32)
    begins_down = jnp.zeros((LANES, 1), jnp.int32)
    for j in range(DOCS):
        length = lens[j]
        ends += jnp.where(lane >= j, length, 0)
        begins += jnp.where(lane > j, length, 0)
        ends_down += jnp.where(line >= j, length, 0)
        begins_down += jnp.where(line > j, length, 0)
    tok = lax.broadcasted_iota(jnp.int32, (LANES, rows), 1)
    col = lax.broadcasted_iota(jnp.int32, (LANES, rows), 0)
    pos = me * rows + tok
    hidden = jnp.where((col < DOCS) & ((pos < begins_down) | (pos >= ends_down)), -MASK, 0.0)
    hidden = jnp.where(col == DOCS, -MASK, hidden)
    first = col - 2 * DOCS
    later = (first >= 0) & (first < own) & (tok < x * own + first)
    hidden = jnp.where(later, -MASK, hidden).astype(jnp.bfloat16)
    for h in range(HEADS):
        qcat[h, :DIM, :] = q_in[:, h * DIM : (h + 1) * DIM].T
        qcat[h, DIM:, :] = hidden
    acc[...] = jnp.zeros_like(acc)
    tot[...] = jnp.zeros_like(tot)

    def features(n, carry):
        cc, b = n // ring, lax.rem(n, ring)
        inner = lax.broadcasted_iota(jnp.int32, (own, LANES), 0)
        lanes_of = lax.broadcasted_iota(jnp.int32, (own, LANES), 1)
        for a in range(ring):
            zz, yy = place(cc, a, b)
            block = (zz * ring + yy) * 2 + cc
            at = block * rows + x * own + inner
            mark = ((at >= begins) & (at < ends)).astype(jnp.float32)
            mark = jnp.where((lanes_of == DOCS) & (block > me), 1.0, mark)
            mark = jnp.where((lanes_of == inner + 2 * DOCS) & (block == me), 1.0, mark)
            kfeat[cc, b, a * own : (a + 1) * own, :] = mark.astype(jnp.bfloat16)
        return carry

    lax.fori_loop(0, 2 * ring, features, 0)

    ones = jnp.ones((16, chunk), jnp.bfloat16)

    def scores(h, cc, b):
        keys = jnp.concatenate([kv[cc, b, 0, :chunk], kfeat[cc, b]], axis=1)
        return jnp.dot(keys, qcat[h], preferred_element_type=jnp.float32)

    def fold(h, cc, b, s):
        p = jnp.exp2(s * FACTOR).astype(jnp.bfloat16)
        vals = jnp.concatenate([kv[cc, b, 1, n : n + LANES] for n in range(0, chunk, LANES)], axis=1)
        both = jnp.dot(jnp.concatenate([vals, ones], axis=0), p, preferred_element_type=jnp.float32)
        acc[h] += both[:DIM]
        tot[h] += both[DIM : DIM + 1]

    def run(work):
        s = scores(*work[0])
        for n, item in enumerate(work):
            after = scores(*work[n + 1]) if n + 1 < len(work) else None
            fold(*item, s)
            s = after

    for d in range(1, ring):
        one_copy(d, p1 - d).wait_recv()
    for n in range(ring):
        kv[c, p2, 0, n * own : (n + 1) * own] = stage[n, :own, :DIM]
    largest = functools.reduce(jnp.maximum, [stage[n, own:, :] for n in range(ring)])
    kv[c, p2, 0, chunk:] = largest[:, :DIM]
    kv[c, p2, 1, chunk:] = largest[:, DIM:]
    for q in range(2):
        fwd_copy(1, p2, 0, q).start()
        bwd_copy(1, p2, 0, q).start()
    side = LANES // own
    for n in range(ring // side):
        block = stage[n * side : (n + 1) * side, :own, DIM:].reshape(LANES, DIM)
        kv[c, p2, 1, n * LANES : (n + 1) * LANES] = block.T
    for q in range(2):
        fwd_copy(1, p2, 1, q).start()
        bwd_copy(1, p2, 1, q).start()
    for i in range(2):
        for q in range(2):
            sib_copy(0, c, p2, i, q).start()

    def unit(u, carry):
        v = jnp.maximum(u - 2, 0)
        s = v // 4 + 1
        r = lax.rem(v, 4)
        early = u < 2
        mine = jnp.where(early, u == 0, r < 2)
        cc = jnp.where(mine, c, 1 - c)
        shift = jnp.where(early, 0, (2 * lax.rem(r, 2) - 1) * s)
        b = wrap(jnp.where(mine, p2, p1) + shift)

        @pl.when(u == 1)
        def _():
            for i in range(2):
                for q in range(2):
                    sib_copy(0, 1 - c, p1, i, q).wait_recv()

        @pl.when((u >= 2) & (r == 2))
        def _():
            sib_arrived(s)

        seen = (b <= z) & ((b + 1) * plane > me * rows - (MOST - 1))

        @pl.when((cc == 1) | seen)
        def _():
            run([(h, cc, b) for h in range(HEADS)])

        @pl.when(u < 2 * (half - 1))
        def _():
            pass_on(u // 2 + 1, lax.rem(u, 2))

        @pl.when(u == 2 * (half - 1))
        def _():
            pass_last()

        return carry

    units = 2 + 4 * (half - 2)
    lax.fori_loop(0, units, unit, 0)
    if units <= 2 * (half - 1):
        pass_last()
    sib_arrived(half - 1)
    for q in range(2):
        sib_copy(2 * half - 1, 1 - c, p1 - half, 0, q).wait_recv()
        sib_copy(2 * half, 1 - c, p1 + half, 1, q).wait_recv()

    def peer(d):
        return lax.rem(x + d, lanes)

    def out_copy(d, h):
        cols = pl.ds(pl.multiple_of(h * DIM, DIM), DIM)
        return pltpu.make_async_remote_copy(
            src_ref=obuf.at[peer(d), :, cols], dst_ref=rbuf.at[d, :, cols],
            send_sem=s_out.at[d, h], recv_sem=r_out.at[d, h], device_id={"ka": peer(d)}, device_id_type=MESH,
        )

    def sum_copy(d):
        return pltpu.make_async_remote_copy(
            src_ref=sums.at[0], dst_ref=sums.at[d],
            send_sem=s_sum.at[d], recv_sem=r_sum.at[d], device_id={"ka": peer(d)}, device_id_type=MESH,
        )

    late = [(c, p2 - half + 1), (c, p2 + half - 1), (1 - c, p1 - half + 1), (1 - c, p1 + half - 1)]
    late += [(c, p2 + half), (1 - c, p1 + half)]

    def finish(h, carry):
        run([(h, cc, wrap(b)) for cc, b in late])
        part = acc[h].T.astype(jnp.bfloat16)
        sums[0, h] = tot[h]
        cols = pl.ds(pl.multiple_of(h * DIM, DIM), DIM)
        for j in range(lanes):
            obuf[j, :, cols] = part[j * own : (j + 1) * own, :]
        for d in range(1, lanes):
            out_copy(d, h).start()
        return carry

    lax.fori_loop(0, HEADS, finish, 0)
    for i in range(2):
        met = [kv[cc, b, i, chunk:] for cc in range(2) for b in range(ring)]
        met = functools.reduce(jnp.maximum, met)[:1, :].astype(jnp.float32)
        sums[0, HEADS + i] = jnp.concatenate([met] * (rows // LANES), axis=1)
    for d in range(1, lanes):
        sum_copy(d).start()
    for d in range(1, lanes):
        sum_copy(d).wait_recv()
    whole = functools.reduce(jnp.add, [sums[d] for d in range(lanes)])
    share = [1.0 / whole[h] for h in range(HEADS)] + [jnp.zeros((LANES - HEADS, rows), jnp.float32)]
    mixing[...] = jnp.concatenate(share, axis=0).T
    met = functools.reduce(jnp.maximum, [sums[d] for d in range(lanes)])
    bound_ref[...] = jnp.broadcast_to((met[HEADS] * met[HEADS + 1])[:, :LANES], bound_ref.shape)
    mix = mixing[pl.ds(pl.multiple_of(x * own, own), own), :]
    for h in range(HEADS):
        cols = slice(h * DIM, (h + 1) * DIM)
        mixed = obuf[x, :, cols].astype(jnp.float32)
        for d in range(1, lanes):
            out_copy(d, h).wait_recv()
            mixed += rbuf[d, :, cols].astype(jnp.float32)
        out_ref[:, cols] = (mixed * mix[:, h : h + 1]).astype(out_ref.dtype)

    for d in range(1, ring):
        one_copy(d, p1).wait_send()
    for i in range(2):
        for q in range(2):
            sib_copy(0, c, p2, i, q).wait_send()
    for s in range(1, half + 1):
        for i in range(2):
            for q in range(2):
                if s < half or i == 0:
                    fwd_copy(s, p2 - s + 1, i, q).wait_send()
                    sib_copy(2 * s - 1, c, p2 - s, i, q).wait_send()
                if s < half or i == 1:
                    bwd_copy(s, p2 + s - 1, i, q).wait_send()
                    sib_copy(2 * s, c, p2 + s, i, q).wait_send()
    for d in range(1, lanes):
        sum_copy(d).wait_send()
        for h in range(HEADS):
            out_copy(d, h).wait_send()


def swift(ring, lanes, queries, keys, values, doc_lengths):
    rows, own = queries.shape[0], keys.shape[0]
    half = ring // 2
    chunk = ring * own
    vmem = pl.BlockSpec(memory_space=pltpu.VMEM)
    sems = pltpu.SemaphoreType.DMA
    parts = (lanes, own, HEADS * DIM)
    return pl.pallas_call(
        functools.partial(swift_kernel, ring, lanes),
        out_shape=(
            jax.ShapeDtypeStruct((own, HEADS * DIM), jnp.bfloat16),
            jax.ShapeDtypeStruct((8, LANES), jnp.float32),
        ),
        in_specs=[pl.BlockSpec(memory_space=pltpu.HBM)] * 4,
        out_specs=(vmem, vmem),
        scratch_shapes=[
            pltpu.VMEM(queries.shape, jnp.bfloat16),
            pltpu.VMEM(keys.shape, jnp.bfloat16),
            pltpu.VMEM(values.shape, jnp.bfloat16),
            pltpu.SMEM(doc_lengths.shape, jnp.int32),
            pltpu.VMEM((ring, own + EXTRA, 2 * DIM), jnp.bfloat16),
            pltpu.VMEM((2, ring, 2, chunk + EXTRA, DIM), jnp.bfloat16),
            pltpu.VMEM((2, ring, chunk, LANES), jnp.bfloat16),
            pltpu.VMEM((HEADS, 2 * DIM, rows), jnp.bfloat16),
            pltpu.VMEM((HEADS, DIM, rows), jnp.float32),
            pltpu.VMEM((HEADS, 1, rows), jnp.float32),
            pltpu.VMEM(parts, jnp.bfloat16),
            pltpu.VMEM(parts, jnp.bfloat16),
            pltpu.VMEM((lanes, HEADS + 2, 1, rows), jnp.float32),
            pltpu.VMEM((rows, LANES), jnp.float32),
            sems((4,)),
            sems((ring - 1,)), sems((ring - 1,)),
            sems((half, 4)), sems((half, 4)), sems((half, 4)), sems((half, 4)),
            sems((2 * half + 1, 4)), sems((2 * half + 1, 4)),
            sems((lanes, HEADS)), sems((lanes, HEADS)),
            sems((lanes,)), sems((lanes,)),
        ],
        compiler_params=pltpu.CompilerParams(
            collective_id=0, has_side_effects=True, vmem_limit_bytes=63 * 1024 * 1024
        ),
        cost_estimate=pl.CostEstimate(flops=10**10, bytes_accessed=10**7, transcendentals=10**7),
        name="swift",
    )(queries, keys, values, doc_lengths)


def where(ring):
    me = lax.axis_index("pb")
    x = lax.axis_index("ka")
    c = lax.rem(me, 2)
    z = me // (2 * ring)
    y = lax.rem(me // 2, ring)
    return me, x, c, z, y


def greet(partners):
    barrier = pltpu.get_barrier_semaphore()
    for partner in partners:
        pl.semaphore_signal(barrier, inc=1, device_id=partner, device_id_type=MESH)
    return lambda: pl.semaphore_wait(barrier, len(partners))


def gather_kernel(
    ring, k_ref, v_ref, kv, stage,
    s_one, r_one, s_fwd, r_fwd, s_bwd, r_bwd, s_sib, r_sib,
):
    half = ring // 2
    own = k_ref.shape[0]
    me, x, c, z, y = where(ring)
    p1 = y * (1 - c) + z * c
    p2 = z * (1 - c) + y * c

    def wrap(value):
        return lax.rem(value + 2 * ring, ring)

    def device(first, second):
        zz, yy = place(c, wrap(first), wrap(second))
        return {"pb": (zz * ring + yy) * 2 + c}

    sibling = {"pb": me + 1 - 2 * c}
    partners = [device(p1 + d, p2) for d in range(1, ring)]
    partners += [device(p1, p2 + d) for d in ((1, ring - 1) if ring > 2 else (1,))]
    ready = greet(partners + [sibling])
    stage[p1, :, :DIM] = k_ref[...]
    stage[p1, :, DIM:] = v_ref[...]
    ready()

    def copy(ref, send, recv, to):
        return pltpu.make_async_remote_copy(
            src_ref=ref, dst_ref=ref, send_sem=send, recv_sem=recv, device_id=to, device_id_type=MESH
        )

    def one_copy(d, b1):
        return copy(stage.at[wrap(b1)], s_one.at[d - 1], r_one.at[d - 1], device(p1 + d, p2))

    def piece(cc, b, p):
        size = ring * own // 2
        return kv.at[cc, wrap(b), p // 2, pl.ds((p % 2) * size, size)]

    def fwd_copy(s, b, p):
        return copy(piece(c, b, p), s_fwd.at[s - 1, p], r_fwd.at[s - 1, p], device(p1, p2 + 1))

    def bwd_copy(s, b, p):
        return copy(piece(c, b, p), s_bwd.at[s - 1, p], r_bwd.at[s - 1, p], device(p1, p2 - 1))

    def sib_copy(n, cc, b, p):
        return copy(piece(cc, b, p), s_sib.at[n, p], r_sib.at[n, p], sibling)

    def travels(s, p):
        return s < half or (s == half and p < 2), s < half or (s == half and p >= 2)

    for d in range(1, ring):
        one_copy(d, p1).start()
    for d in range(1, ring):
        one_copy(d, p1 - d).wait_recv()
    for n in range(ring):
        kv[c, p2, 0, n * own : (n + 1) * own] = stage[n, :, :DIM]
    side = LANES // own
    for n in range(ring // side):
        block = stage[n * side : (n + 1) * side, :, DIM:].reshape(LANES, DIM)
        kv[c, p2, 1, n * LANES : (n + 1) * LANES] = block.T
    for p in range(4):
        if travels(1, p)[0]:
            fwd_copy(1, p2, p).start()
        if travels(1, p)[1]:
            bwd_copy(1, p2, p).start()
    for p in range(4):
        sib_copy(0, c, p2, p).start()
    for s in range(1, half + 1):
        for p in range(4):
            if travels(s, p)[0]:
                fwd_copy(s, p2 - s, p).wait_recv()
                if travels(s + 1, p)[0]:
                    fwd_copy(s + 1, p2 - s, p).start()
            if travels(s, p)[1]:
                bwd_copy(s, p2 + s, p).wait_recv()
                if travels(s + 1, p)[1]:
                    bwd_copy(s + 1, p2 + s, p).start()
        for p in range(4):
            if travels(s, p)[0]:
                sib_copy(2 * s - 1, c, p2 - s, p).start()
            if travels(s, p)[1]:
                sib_copy(2 * s, c, p2 + s, p).start()
    for p in range(4):
        sib_copy(0, 1 - c, p1, p).wait_recv()
    for s in range(1, half + 1):
        for p in range(4):
            if travels(s, p)[0]:
                sib_copy(2 * s - 1, 1 - c, p1 - s, p).wait_recv()
            if travels(s, p)[1]:
                sib_copy(2 * s, 1 - c, p1 + s, p).wait_recv()
    for d in range(1, ring):
        one_copy(d, p1).wait_send()
    for p in range(4):
        sib_copy(0, c, p2, p).wait_send()
    for s in range(1, half + 1):
        for p in range(4):
            if travels(s, p)[0]:
                fwd_copy(s, p2 - s + 1, p).wait_send()
                sib_copy(2 * s - 1, c, p2 - s, p).wait_send()
            if travels(s, p)[1]:
                bwd_copy(s, p2 + s - 1, p).wait_send()
                sib_copy(2 * s, c, p2 + s, p).wait_send()


def attend_kernel(ring, lanes, q_ref, kv, lens, obuf, lbuf, kfeat, qcat, acc, tot, top):
    rows = q_ref.shape[0]
    own = rows // lanes
    chunk = ring * own
    plane = ring * 2 * rows
    me, x, c, z, y = where(ring)

    lane = lax.broadcasted_iota(jnp.int32, (1, LANES), 1)
    line = lax.broadcasted_iota(jnp.int32, (LANES, 1), 0)
    ends = jnp.zeros((1, LANES), jnp.int32)
    begins = jnp.zeros((1, LANES), jnp.int32)
    ends_down = jnp.zeros((LANES, 1), jnp.int32)
    begins_down = jnp.zeros((LANES, 1), jnp.int32)
    for j in range(DOCS):
        length = lens[j]
        ends += jnp.where(lane >= j, length, 0)
        begins += jnp.where(lane > j, length, 0)
        ends_down += jnp.where(line >= j, length, 0)
        begins_down += jnp.where(line > j, length, 0)
    tok = lax.broadcasted_iota(jnp.int32, (LANES, rows), 1)
    col = lax.broadcasted_iota(jnp.int32, (LANES, rows), 0)
    pos = me * rows + tok
    hidden = jnp.where((col < DOCS) & ((pos < begins_down) | (pos >= ends_down)), -MASK, 0.0)
    hidden = jnp.where(col == DOCS, -MASK, hidden)
    first = col - 2 * DOCS
    later = (first >= 0) & (first < own) & (tok < x * own + first)
    hidden = jnp.where(later, -MASK, hidden).astype(jnp.bfloat16)
    for h in range(HEADS):
        turned = q_ref[:, h * DIM : (h + 1) * DIM].T
        qcat[:DIM, h * rows : (h + 1) * rows] = turned
        qcat[DIM:, h * rows : (h + 1) * rows] = hidden
    acc[...] = jnp.zeros_like(acc)
    tot[...] = jnp.zeros_like(tot)
    top[...] = jnp.full_like(top, EMPTY)

    def features(n, carry):
        cc, b = n // ring, lax.rem(n, ring)
        inner = lax.broadcasted_iota(jnp.int32, (own, LANES), 0)
        lanes_of = lax.broadcasted_iota(jnp.int32, (own, LANES), 1)
        for a in range(ring):
            zz, yy = place(cc, a, b)
            block = (zz * ring + yy) * 2 + cc
            at = block * rows + x * own + inner
            mark = ((at >= begins) & (at < ends)).astype(jnp.float32)
            mark = jnp.where((lanes_of == DOCS) & (block > me), 1.0, mark)
            mark = jnp.where((lanes_of == inner + 2 * DOCS) & (block == me), 1.0, mark)
            kfeat[cc, b, a * own : (a + 1) * own, :] = mark.astype(jnp.bfloat16)
        return carry

    lax.fori_loop(0, 2 * ring, features, 0)
    ones = jnp.ones((16, chunk), jnp.bfloat16)

    def scores(h, cc, b):
        keys = jnp.concatenate([kv[cc, b, 0], kfeat[cc, b]], axis=1)
        return jnp.dot(keys, qcat[:, h * rows : (h + 1) * rows], preferred_element_type=jnp.float32)

    def weighted(cc, b, p):
        vals = jnp.concatenate([kv[cc, b, 1, n : n + LANES] for n in range(0, chunk, LANES)], axis=1)
        return jnp.dot(jnp.concatenate([vals, ones], axis=0), p, preferred_element_type=jnp.float32)

    def fold(h, cc, b, s):
        old = top[h : h + 1, :]
        new = jnp.maximum(old, jnp.max(s, axis=0, keepdims=True))
        both = weighted(cc, b, jnp.exp2((s - new) * FACTOR).astype(jnp.bfloat16))
        alpha = jnp.exp2((old - new) * FACTOR)
        acc[h] = acc[h] * alpha + both[:DIM]
        tot[h : h + 1, :] = tot[h : h + 1, :] * alpha + both[DIM : DIM + 1]
        top[h : h + 1, :] = new

    def sweep(fold):
        def body(n, carry):
            cc, b = n // ring, lax.rem(n, ring)
            seen = (b <= z) & ((b + 1) * plane > me * rows - (MOST - 1))

            @pl.when((cc == 1) | seen)
            def _():
                s = scores(0, cc, b)
                for h in range(HEADS):
                    after = scores(h + 1, cc, b) if h + 1 < HEADS else None
                    fold(h, cc, b, s)
                    s = after

            return carry

        lax.fori_loop(0, 2 * ring, body, 0)

    sweep(fold)
    logs = []
    for h in range(HEADS):
        total = tot[h : h + 1, :]
        some = total > 0.0
        safe = jnp.where(some, total, 1.0)
        part = (acc[h] / safe).T.astype(jnp.bfloat16)
        logs.append(jnp.where(some, top[h : h + 1, :] * FACTOR + jnp.log2(safe), NOTHING))
        for j in range(lanes):
            obuf[j, :, h * DIM : (h + 1) * DIM] = part[j * own : (j + 1) * own, :]
    lbuf[...] = jnp.concatenate(logs, axis=0)


def merge_kernel(lanes, obuf, lbuf, out_ref, rbuf, logs, mixing, relay, s_out, r_out, s_log, r_log, s_rel, r_rel):
    x = lax.axis_index("ka")
    own = out_ref.shape[0]
    rows = lbuf.shape[1]
    near = [d for d in range(1, lanes) if lanes != 4 or d != 2]

    def peer(d):
        return lax.rem(x + d, lanes)

    def copy(src, dst, send, recv, d):
        return pltpu.make_async_remote_copy(
            src_ref=src, dst_ref=dst, send_sem=send, recv_sem=recv, device_id={"ka": peer(d)}, device_id_type=MESH
        )

    def cols_of(g):
        return pl.ds(g * 2 * DIM, 2 * DIM)

    def out_copy(d, g):
        cols = cols_of(g)
        return copy(obuf.at[peer(d), :, cols], rbuf.at[d, :, cols], s_out.at[d, g], r_out.at[d, g], d)

    def way(g):
        return 1 if g < HEADS // 4 else 3

    def relay_copy(g):
        cols = cols_of(g)
        return copy(obuf.at[peer(2), :, cols], relay.at[:, cols], s_rel.at[g], r_rel.at[g], way(g))

    def onward_copy(g):
        cols = cols_of(g)
        return copy(relay.at[:, cols], rbuf.at[2, :, cols], s_out.at[2, g], r_out.at[2, g], way(g))

    def log_copy(d):
        return copy(lbuf, logs.at[d], s_log.at[d], r_log.at[d], d)

    greet([{"ka": peer(d)} for d in range(1, lanes)])()
    groups = range(HEADS // 2)
    for d in range(1, lanes):
        log_copy(d).start()
    if lanes == 4:
        for g in (0, 2, 1, 3):
            relay_copy(g).start()
    for g in groups:
        for d in near:
            out_copy(d, g).start()
    if lanes == 4:
        for g in (0, 2, 1, 3):
            relay_copy(g).wait_recv()
            onward_copy(g).start()
    for d in range(1, lanes):
        log_copy(d).wait_recv()
    sizes = [lbuf[...]] + [logs[d] for d in range(1, lanes)]
    highest = functools.reduce(jnp.maximum, sizes)
    shares = [jnp.exp2(size - highest) for size in sizes]
    whole = functools.reduce(jnp.add, shares)
    shares = [share / whole for share in shares]
    shares.append(jnp.zeros((LANES - HEADS * lanes, rows), jnp.float32))
    mixing[...] = jnp.concatenate(shares, axis=0).T
    mix = mixing[pl.ds(pl.multiple_of(x * own, own), own), :]
    for g in groups:
        for d in range(1, lanes):
            out_copy(d, g).wait_recv()
        for h in (2 * g, 2 * g + 1):
            cols = slice(h * DIM, (h + 1) * DIM)
            mixed = mix[:, h : h + 1] * obuf[x, :, cols].astype(jnp.float32)
            for d in range(1, lanes):
                at = d * HEADS + h
                mixed += mix[:, at : at + 1] * rbuf[d, :, cols].astype(jnp.float32)
            out_ref[:, cols] = mixed.astype(out_ref.dtype)
    for d in range(1, lanes):
        log_copy(d).wait_send()
    for g in groups:
        for d in near:
            out_copy(d, g).wait_send()
        if lanes == 4:
            relay_copy(g).wait_send()
            onward_copy(g).wait_send()


def steady(ring, lanes, queries, keys, values, doc_lengths):
    rows, own = queries.shape[0], keys.shape[0]
    half = ring // 2
    chunk = ring * own
    vmem = pl.BlockSpec(memory_space=pltpu.VMEM)
    sems = pltpu.SemaphoreType.DMA
    limit = 48 * 1024 * 1024
    kv = pl.pallas_call(
        functools.partial(gather_kernel, ring),
        out_shape=jax.ShapeDtypeStruct((2, ring, 2, chunk, DIM), jnp.bfloat16),
        in_specs=[vmem, vmem],
        out_specs=vmem,
        scratch_shapes=[
            pltpu.VMEM((ring, own, 2 * DIM), jnp.bfloat16),
            sems((ring - 1,)), sems((ring - 1,)),
            sems((half, 4)), sems((half, 4)), sems((half, 4)), sems((half, 4)),
            sems((2 * half + 1, 4)), sems((2 * half + 1, 4)),
        ],
        compiler_params=pltpu.CompilerParams(collective_id=1, has_side_effects=True, vmem_limit_bytes=limit),
        name="gather",
    )(keys, values)
    parts, logs = pl.pallas_call(
        functools.partial(attend_kernel, ring, lanes),
        out_shape=(
            jax.ShapeDtypeStruct((lanes, own, HEADS * DIM), jnp.bfloat16),
            jax.ShapeDtypeStruct((HEADS, rows), jnp.float32),
        ),
        in_specs=[vmem, vmem, pl.BlockSpec(memory_space=pltpu.SMEM)],
        out_specs=(vmem, vmem),
        scratch_shapes=[
            pltpu.VMEM((2, ring, chunk, LANES), jnp.bfloat16),
            pltpu.VMEM((2 * DIM, HEADS * rows), jnp.bfloat16),
            pltpu.VMEM((HEADS, DIM, rows), jnp.float32),
            pltpu.VMEM((HEADS, rows), jnp.float32),
            pltpu.VMEM((HEADS, rows), jnp.float32),
        ],
        compiler_params=pltpu.CompilerParams(vmem_limit_bytes=limit),
        name="attend",
    )(queries, kv, doc_lengths)
    return pl.pallas_call(
        functools.partial(merge_kernel, lanes),
        out_shape=jax.ShapeDtypeStruct((own, HEADS * DIM), jnp.bfloat16),
        in_specs=[vmem, vmem],
        out_specs=vmem,
        scratch_shapes=[
            pltpu.VMEM((lanes, own, HEADS * DIM), jnp.bfloat16),
            pltpu.VMEM((lanes, HEADS, rows), jnp.float32),
            pltpu.VMEM((rows, LANES), jnp.float32),
            pltpu.VMEM((own, HEADS * DIM), jnp.bfloat16),
            sems((lanes, HEADS // 2)), sems((lanes, HEADS // 2)),
            sems((lanes,)), sems((lanes,)),
            sems((HEADS // 2,)), sems((HEADS // 2,)),
        ],
        compiler_params=pltpu.CompilerParams(collective_id=2, has_side_effects=True, vmem_limit_bytes=limit),
        name="merge",
    )(parts, logs)


def per_device(ring, lanes, queries, keys, values, doc_lengths):
    args = (queries, keys, values, doc_lengths)
    out, bound = swift(ring, lanes, *args)
    fits = bound[0, 0] <= (SAFE / FACTOR) ** 2
    return lax.cond(fits, lambda *_: out, functools.partial(steady, ring, lanes), *args)


def solution(mesh):
    ring = math.isqrt(mesh.shape["pb"] // 2)
    return jax.shard_map(
        functools.partial(per_device, ring, mesh.shape["ka"]),
        mesh=mesh,
        in_specs=(P("pb", None), P(("pb", "ka"), None), P(("pb", "ka"), None), P()),
        out_specs=P(("pb", "ka"), None),
        check_vma=False,
    )
```

```python
import functools
import math

import jax
import jax.numpy as jnp
from jax import lax
from jax.experimental import pallas as pl
from jax.experimental.pallas import tpu as pltpu
from jax.sharding import PartitionSpec as P

HEADS = 8
DIM = 128
DOCS = 8
MOST = 24576
LANES = 128
FACTOR = math.log2(math.e) / math.sqrt(DIM)
MASK = 131072.0
EMPTY = -65536.0
NOTHING = -1e30
EXTRA = 16
SAFE = 100.0
MESH = pl.DeviceIdType.MESH


def place(c, first, second):
    z = second * (1 - c) + first * c
    y = first * (1 - c) + second * c
    return z, y


def swift_kernel(
    ring, lanes, q_hbm, k_hbm, v_hbm, len_hbm, out_ref, bound_ref,
    q_in, k_in, v_in, lens, stage, kv, kfeat, qcat, acc, tot, obuf, rbuf, sums, mixing,
    s_in, s_one, r_one, s_fwd, r_fwd, s_bwd, r_bwd, s_sib, r_sib, s_out, r_out, s_sum, r_sum,
):
    half = ring // 2
    rows = q_in.shape[0]
    own = k_in.shape[0]
    part = own // 2
    side = ring * part
    chunk = 2 * side
    plane = ring * 2 * rows
    me = lax.axis_index("pb")
    x = lax.axis_index("ka")
    c = lax.rem(me, 2)
    z = me // (2 * ring)
    y = lax.rem(me // 2, ring)
    first, second = (y, z), (z, y)
    classes = (0, 1)

    def wrap(value):
        return lax.rem(value + 2 * ring, ring)

    def device(cls, along_first, along_second):
        zz, yy = place(cls, wrap(first[cls] + along_first), wrap(second[cls] + along_second))
        return {"pb": (zz * ring + yy) * 2 + c}

    sibling = {"pb": me + 1 - 2 * c}

    barrier = pltpu.get_barrier_semaphore()
    partners = [device(cls, d, 0) for cls in classes for d in range(1, ring)]
    partners += [sibling] + [{"ka": lax.rem(x + d, lanes)} for d in range(1, lanes)]
    for partner in partners:
        pl.semaphore_signal(barrier, inc=1, device_id=partner, device_id_type=MESH)
    moves = [
        pltpu.make_async_copy(src, dst, s_in.at[n])
        for n, (src, dst) in enumerate(((k_hbm, k_in), (v_hbm, v_in), (len_hbm, lens), (q_hbm, q_in)))
    ]
    for move in moves:
        move.start()
    moves[0].wait()
    moves[1].wait()
    wide = k_in[...].astype(jnp.float32)
    longest = jnp.max(jnp.sum(wide * wide, axis=1, keepdims=True), axis=0, keepdims=True)
    k_most = jnp.broadcast_to(longest * 1.01, (EXTRA, DIM)).astype(jnp.bfloat16)
    moves[3].wait()
    longest = jnp.zeros((rows, 1), jnp.float32)
    for h in range(HEADS):
        wide = q_in[:, h * DIM : (h + 1) * DIM].astype(jnp.float32)
        longest = jnp.maximum(longest, jnp.sum(wide * wide, axis=1, keepdims=True))
    longest = jnp.max(longest, axis=0, keepdims=True)
    q_most = jnp.broadcast_to(longest * 1.01, (EXTRA, DIM)).astype(jnp.bfloat16)
    for cls in classes:
        stage[cls, first[cls], :part, :DIM] = k_in[cls * part : (cls + 1) * part]
        stage[cls, first[cls], :part, DIM:] = v_in[cls * part : (cls + 1) * part]
        stage[cls, first[cls], part:, :DIM] = k_most
        stage[cls, first[cls], part:, DIM:] = q_most
    pl.semaphore_wait(barrier, len(partners))

    def copy(ref, send, recv, where):
        return pltpu.make_async_remote_copy(
            src_ref=ref, dst_ref=ref, send_sem=send, recv_sem=recv, device_id=where, device_id_type=MESH
        )

    def one_copy(cls, d, at):
        ref = stage.at[cls, wrap(at)]
        return copy(ref, s_one.at[cls, d - 1], r_one.at[cls, d - 1], device(cls, d, 0))

    def piece(cls, b, core, which):
        if which is None:
            return kv.at[cls, wrap(b), core]
        return kv.at[cls, wrap(b), core, pl.ds(which * side, side + which * EXTRA)]

    def fwd_copy(cls, s, b, last):
        ref = piece(cls, b, c, 0 if last else None)
        return copy(ref, s_fwd.at[cls, s - 1], r_fwd.at[cls, s - 1], device(cls, 0, 1))

    def bwd_copy(cls, s, b, last):
        ref = piece(cls, b, c, 1 if last else None)
        return copy(ref, s_bwd.at[cls, s - 1], r_bwd.at[cls, s - 1], device(cls, 0, -1))

    def sib_copy(cls, n, b, core, which):
        return copy(piece(cls, b, core, which), s_sib.at[cls, n], r_sib.at[cls, n], sibling)

    def pass_on(cls, s):
        at = second[cls]
        fwd_copy(cls, s, at - s, False).wait_recv()
        pl.when(s + 1 < half)(lambda: fwd_copy(cls, s + 1, at - s, False).start())
        pl.when(s + 1 == half)(lambda: fwd_copy(cls, s + 1, at - s, True).start())
        bwd_copy(cls, s, at + s, False).wait_recv()
        pl.when(s + 1 < half)(lambda: bwd_copy(cls, s + 1, at + s, False).start())
        pl.when(s + 1 == half)(lambda: bwd_copy(cls, s + 1, at + s, True).start())
        sib_copy(cls, 2 * s - 1, at - s, c, None).start()
        sib_copy(cls, 2 * s, at + s, c, None).start()

    def pass_last(cls):
        at = second[cls]
        fwd_copy(cls, half, at - half, True).wait_recv()
        sib_copy(cls, 2 * half - 1, at - half, c, 0).start()
        bwd_copy(cls, half, at + half, True).wait_recv()
        sib_copy(cls, 2 * half, at + half, c, 1).start()

    def sib_arrived(cls, s):
        at = second[cls]
        sib_copy(cls, 2 * s - 1, at - s, 1 - c, None).wait_recv()
        sib_copy(cls, 2 * s, at + s, 1 - c, None).wait_recv()

    for d in range(1, ring):
        for cls in classes:
            one_copy(cls, d, first[cls]).start()
    moves[2].wait()

    lane = lax.broadcasted_iota(jnp.int32, (1, LANES), 1)
    line = lax.broadcasted_iota(jnp.int32, (LANES, 1), 0)
    ends = jnp.zeros((1, LANES), jnp.int32)
    begins = jnp.zeros((1, LANES), jnp.int32)
    ends_down = jnp.zeros((LANES, 1), jnp.int32)
    begins_down = jnp.zeros((LANES, 1), jnp.int32)
    for j in range(DOCS):
        length = lens[j]
        ends += jnp.where(lane >= j, length, 0)
        begins += jnp.where(lane > j, length, 0)
        ends_down += jnp.where(line >= j, length, 0)
        begins_down += jnp.where(line > j, length, 0)
    tok = lax.broadcasted_iota(jnp.int32, (LANES, rows), 1)
    col = lax.broadcasted_iota(jnp.int32, (LANES, rows), 0)
    pos = me * rows + tok
    hidden = jnp.where((col < DOCS) & ((pos < begins_down) | (pos >= ends_down)), -MASK, 0.0)
    hidden = jnp.where(col == DOCS, -MASK, hidden)
    inside = col - 2 * DOCS
    later = (inside >= 0) & (inside < own) & (tok < x * own + inside)
    hidden = jnp.where(later, -MASK, hidden).astype(jnp.bfloat16)
    for h in range(HEADS):
        qcat[h, :DIM, :] = q_in[:, h * DIM : (h + 1) * DIM].T
        qcat[h, DIM:, :] = hidden
    acc[...] = jnp.zeros_like(acc)
    tot[...] = jnp.zeros_like(tot)

    def features(n, carry):
        cls, b = n // ring, lax.rem(n, ring)
        inner = lax.broadcasted_iota(jnp.int32, (part, LANES), 0) + cls * part
        lanes_of = lax.broadcasted_iota(jnp.int32, (part, LANES), 1)
        for core in range(2):
            for a in range(ring):
                zz, yy = place(cls, a, b)
                block = (zz * ring + yy) * 2 + core
                at = block * rows + x * own + inner
                mark = ((at >= begins) & (at < ends)).astype(jnp.float32)
                mark = jnp.where((lanes_of == DOCS) & (block > me), 1.0, mark)
                mark = jnp.where((lanes_of == inner + 2 * DOCS) & (block == me), 1.0, mark)
                row = core * side + a * part
                kfeat[cls, b, row : row + part, :] = mark.astype(jnp.bfloat16)
        return carry

    lax.fori_loop(0, 2 * ring, features, 0)

    ones = jnp.ones((16, chunk), jnp.bfloat16)

    def scores(h, cls, b):
        keys = jnp.concatenate([kv[cls, b, 0, :side], kv[cls, b, 1, :side]], axis=0)
        keys = jnp.concatenate([keys, kfeat[cls, b]], axis=1)
        return jnp.dot(keys, qcat[h], preferred_element_type=jnp.float32)

    def fold(h, cls, b, s):
        p = jnp.exp2(s * FACTOR).astype(jnp.bfloat16)
        vals = [kv[cls, b, core, n : n + LANES] for core in range(2) for n in range(side, chunk, LANES)]
        vals = jnp.concatenate([jnp.concatenate(vals, axis=1), ones], axis=0)
        both = jnp.dot(vals, p, preferred_element_type=jnp.float32)
        acc[h] += both[:DIM]
        tot[h] += both[DIM : DIM + 1]

    def run(work):
        s = scores(*work[0])
        for n, item in enumerate(work):
            after = scores(*work[n + 1]) if n + 1 < len(work) else None
            fold(*item, s)
            s = after

    per = LANES // part
    lower = lax.broadcasted_iota(jnp.int32, (EXTRA, DIM), 0) < EXTRA // 2
    for cls in classes:
        at = second[cls]
        for d in range(1, ring):
            one_copy(cls, d, first[cls] - d).wait_recv()
        for n in range(ring):
            kv[cls, at, c, n * part : (n + 1) * part] = stage[cls, n, :part, :DIM]
        for n in range(ring // per):
            block = stage[cls, n * per : (n + 1) * per, :part, DIM:].reshape(LANES, DIM)
            kv[cls, at, c, side + n * LANES : side + (n + 1) * LANES] = block.T
        largest = functools.reduce(jnp.maximum, [stage[cls, n, part:, :] for n in range(ring)])
        kv[cls, at, c, chunk:] = jnp.where(lower, largest[:, :DIM], largest[:, DIM:])
        fwd_copy(cls, 1, at, half == 1).start()
        bwd_copy(cls, 1, at, half == 1).start()
        sib_copy(cls, 0, at, c, None).start()

    def unit(u, carry):
        v = jnp.maximum(u - 2, 0)
        s = v // 4 + 1
        r = lax.rem(v, 4)
        early = u < 2
        cls = jnp.where(early, u, r // 2)
        shift = jnp.where(early, 0, (2 * lax.rem(r, 2) - 1) * s)
        b = wrap(jnp.where(cls == 0, z, y) + shift)
        for k in classes:

            @pl.when(u == k)
            def _(k=k):
                sib_copy(k, 0, second[k], 1 - c, None).wait_recv()

            @pl.when((u >= 2) & (r == 2 * k))
            def _(k=k):
                sib_arrived(k, s)

        seen = (b <= z) & ((b + 1) * plane > me * rows - (MOST - 1))

        @pl.when((cls == 1) | seen)
        def _():
            run([(h, cls, b) for h in range(HEADS)])

        for k in classes:

            @pl.when((u < 2 * (half - 1)) & (lax.rem(u, 2) == k))
            def _(k=k):
                pass_on(k, u // 2 + 1)

            @pl.when(u == 2 * (half - 1) + k)
            def _(k=k):
                pass_last(k)

        return carry

    units = 2 + 4 * (half - 2)
    lax.fori_loop(0, units, unit, 0)
    for cls in classes:
        if units <= 2 * (half - 1) + cls:
            pass_last(cls)
    for cls in classes:
        sib_arrived(cls, half - 1)
        sib_copy(cls, 2 * half - 1, second[cls] - half, 1 - c, 0).wait_recv()
        sib_copy(cls, 2 * half, second[cls] + half, 1 - c, 1).wait_recv()

    def peer(d):
        return lax.rem(x + d, lanes)

    def out_copy(d, h):
        cols = pl.ds(pl.multiple_of(h * DIM, DIM), DIM)
        return pltpu.make_async_remote_copy(
            src_ref=obuf.at[peer(d), :, cols], dst_ref=rbuf.at[d, :, cols],
            send_sem=s_out.at[d, h], recv_sem=r_out.at[d, h], device_id={"ka": peer(d)}, device_id_type=MESH,
        )

    def sum_copy(d):
        return pltpu.make_async_remote_copy(
            src_ref=sums.at[0], dst_ref=sums.at[d],
            send_sem=s_sum.at[d], recv_sem=r_sum.at[d], device_id={"ka": peer(d)}, device_id_type=MESH,
        )

    late = [(cls, second[cls] + sign * (half - 1)) for cls in classes for sign in (-1, 1)]
    late += [(cls, second[cls] + half) for cls in classes]

    def finish(h, carry):
        run([(h, cls, wrap(b)) for cls, b in late])
        turned = acc[h].T.astype(jnp.bfloat16)
        sums[0, h] = tot[h]
        cols = pl.ds(pl.multiple_of(h * DIM, DIM), DIM)
        for j in range(lanes):
            obuf[j, :, cols] = turned[j * own : (j + 1) * own, :]
        for d in range(1, lanes):
            out_copy(d, h).start()
        return carry

    lax.fori_loop(0, HEADS, finish, 0)
    met = [kv[cls, b, core, chunk:] for cls in classes for b in range(ring) for core in range(2)]
    met = functools.reduce(jnp.maximum, met).astype(jnp.float32)
    for i in range(2):
        row = met[i * EXTRA // 2 : i * EXTRA // 2 + 1, :]
        sums[0, HEADS + i] = jnp.concatenate([row] * (rows // LANES), axis=1)
    for d in range(1, lanes):
        sum_copy(d).start()
    for cls in classes:
        at = second[cls]
        for d in range(1, ring):
            one_copy(cls, d, first[cls]).wait_send()
        sib_copy(cls, 0, at, c, None).wait_send()
        for s in range(1, half + 1):
            last = s == half
            fwd_copy(cls, s, at - s + 1, last).wait_send()
            bwd_copy(cls, s, at + s - 1, last).wait_send()
            sib_copy(cls, 2 * s - 1, at - s, c, 0 if last else None).wait_send()
            sib_copy(cls, 2 * s, at + s, c, 1 if last else None).wait_send()
    for d in range(1, lanes):
        sum_copy(d).wait_recv()
    whole = functools.reduce(jnp.add, [sums[d] for d in range(lanes)])
    share = [1.0 / whole[h] for h in range(HEADS)] + [jnp.zeros((LANES - HEADS, rows), jnp.float32)]
    mixing[...] = jnp.concatenate(share, axis=0).T
    met = functools.reduce(jnp.maximum, [sums[d] for d in range(lanes)])
    bound_ref[...] = jnp.broadcast_to((met[HEADS] * met[HEADS + 1])[:, :LANES], bound_ref.shape)
    mix = mixing[pl.ds(pl.multiple_of(x * own, own), own), :]
    for h in range(HEADS):
        cols = slice(h * DIM, (h + 1) * DIM)
        mixed = obuf[x, :, cols].astype(jnp.float32)
        for d in range(1, lanes):
            out_copy(d, h).wait_recv()
            mixed += rbuf[d, :, cols].astype(jnp.float32)
        out_ref[:, cols] = (mixed * mix[:, h : h + 1]).astype(out_ref.dtype)

    for d in range(1, lanes):
        sum_copy(d).wait_send()
        for h in range(HEADS):
            out_copy(d, h).wait_send()


def swift(ring, lanes, queries, keys, values, doc_lengths):
    rows, own = queries.shape[0], keys.shape[0]
    half = ring // 2
    chunk = ring * own
    vmem = pl.BlockSpec(memory_space=pltpu.VMEM)
    sems = pltpu.SemaphoreType.DMA
    parts = (lanes, own, HEADS * DIM)
    return pl.pallas_call(
        functools.partial(swift_kernel, ring, lanes),
        out_shape=(
            jax.ShapeDtypeStruct((own, HEADS * DIM), jnp.bfloat16),
            jax.ShapeDtypeStruct((8, LANES), jnp.float32),
        ),
        in_specs=[pl.BlockSpec(memory_space=pltpu.HBM)] * 4,
        out_specs=(vmem, vmem),
        scratch_shapes=[
            pltpu.VMEM(queries.shape, jnp.bfloat16),
            pltpu.VMEM(keys.shape, jnp.bfloat16),
            pltpu.VMEM(values.shape, jnp.bfloat16),
            pltpu.SMEM(doc_lengths.shape, jnp.int32),
            pltpu.VMEM((2, ring, own // 2 + EXTRA, 2 * DIM), jnp.bfloat16),
            pltpu.VMEM((2, ring, 2, chunk + EXTRA, DIM), jnp.bfloat16),
            pltpu.VMEM((2, ring, chunk, LANES), jnp.bfloat16),
            pltpu.VMEM((HEADS, 2 * DIM, rows), jnp.bfloat16),
            pltpu.VMEM((HEADS, DIM, rows), jnp.float32),
            pltpu.VMEM((HEADS, 1, rows), jnp.float32),
            pltpu.VMEM(parts, jnp.bfloat16),
            pltpu.VMEM(parts, jnp.bfloat16),
            pltpu.VMEM((lanes, HEADS + 2, 1, rows), jnp.float32),
            pltpu.VMEM((rows, LANES), jnp.float32),
            sems((4,)),
            sems((2, ring - 1)), sems((2, ring - 1)),
            sems((2, half)), sems((2, half)), sems((2, half)), sems((2, half)),
            sems((2, 2 * half + 1)), sems((2, 2 * half + 1)),
            sems((lanes, HEADS)), sems((lanes, HEADS)),
            sems((lanes,)), sems((lanes,)),
        ],
        compiler_params=pltpu.CompilerParams(
            collective_id=0, has_side_effects=True, vmem_limit_bytes=63 * 1024 * 1024
        ),
        cost_estimate=pl.CostEstimate(flops=10**10, bytes_accessed=10**7, transcendentals=10**7),
        name="swift",
    )(queries, keys, values, doc_lengths)


def where(ring):
    me = lax.axis_index("pb")
    x = lax.axis_index("ka")
    c = lax.rem(me, 2)
    z = me // (2 * ring)
    y = lax.rem(me // 2, ring)
    return me, x, c, z, y


def greet(partners):
    barrier = pltpu.get_barrier_semaphore()
    for partner in partners:
        pl.semaphore_signal(barrier, inc=1, device_id=partner, device_id_type=MESH)
    return lambda: pl.semaphore_wait(barrier, len(partners))


def gather_kernel(
    ring, k_ref, v_ref, kv, stage,
    s_one, r_one, s_fwd, r_fwd, s_bwd, r_bwd, s_sib, r_sib,
):
    half = ring // 2
    own = k_ref.shape[0]
    me, x, c, z, y = where(ring)
    p1 = y * (1 - c) + z * c
    p2 = z * (1 - c) + y * c

    def wrap(value):
        return lax.rem(value + 2 * ring, ring)

    def device(first, second):
        zz, yy = place(c, wrap(first), wrap(second))
        return {"pb": (zz * ring + yy) * 2 + c}

    sibling = {"pb": me + 1 - 2 * c}
    partners = [device(p1 + d, p2) for d in range(1, ring)]
    partners += [device(p1, p2 + d) for d in ((1, ring - 1) if ring > 2 else (1,))]
    ready = greet(partners + [sibling])
    stage[p1, :, :DIM] = k_ref[...]
    stage[p1, :, DIM:] = v_ref[...]
    ready()

    def copy(ref, send, recv, to):
        return pltpu.make_async_remote_copy(
            src_ref=ref, dst_ref=ref, send_sem=send, recv_sem=recv, device_id=to, device_id_type=MESH
        )

    def one_copy(d, b1):
        return copy(stage.at[wrap(b1)], s_one.at[d - 1], r_one.at[d - 1], device(p1 + d, p2))

    def piece(cc, b, p):
        size = ring * own // 2
        return kv.at[cc, wrap(b), p // 2, pl.ds((p % 2) * size, size)]

    def fwd_copy(s, b, p):
        return copy(piece(c, b, p), s_fwd.at[s - 1, p], r_fwd.at[s - 1, p], device(p1, p2 + 1))

    def bwd_copy(s, b, p):
        return copy(piece(c, b, p), s_bwd.at[s - 1, p], r_bwd.at[s - 1, p], device(p1, p2 - 1))

    def sib_copy(n, cc, b, p):
        return copy(piece(cc, b, p), s_sib.at[n, p], r_sib.at[n, p], sibling)

    def travels(s, p):
        return s < half or (s == half and p < 2), s < half or (s == half and p >= 2)

    for d in range(1, ring):
        one_copy(d, p1).start()
    for d in range(1, ring):
        one_copy(d, p1 - d).wait_recv()
    for n in range(ring):
        kv[c, p2, 0, n * own : (n + 1) * own] = stage[n, :, :DIM]
    side = LANES // own
    for n in range(ring // side):
        block = stage[n * side : (n + 1) * side, :, DIM:].reshape(LANES, DIM)
        kv[c, p2, 1, n * LANES : (n + 1) * LANES] = block.T
    for p in range(4):
        if travels(1, p)[0]:
            fwd_copy(1, p2, p).start()
        if travels(1, p)[1]:
            bwd_copy(1, p2, p).start()
    for p in range(4):
        sib_copy(0, c, p2, p).start()
    for s in range(1, half + 1):
        for p in range(4):
            if travels(s, p)[0]:
                fwd_copy(s, p2 - s, p).wait_recv()
                if travels(s + 1, p)[0]:
                    fwd_copy(s + 1, p2 - s, p).start()
            if travels(s, p)[1]:
                bwd_copy(s, p2 + s, p).wait_recv()
                if travels(s + 1, p)[1]:
                    bwd_copy(s + 1, p2 + s, p).start()
        for p in range(4):
            if travels(s, p)[0]:
                sib_copy(2 * s - 1, c, p2 - s, p).start()
            if travels(s, p)[1]:
                sib_copy(2 * s, c, p2 + s, p).start()
    for p in range(4):
        sib_copy(0, 1 - c, p1, p).wait_recv()
    for s in range(1, half + 1):
        for p in range(4):
            if travels(s, p)[0]:
                sib_copy(2 * s - 1, 1 - c, p1 - s, p).wait_recv()
            if travels(s, p)[1]:
                sib_copy(2 * s, 1 - c, p1 + s, p).wait_recv()
    for d in range(1, ring):
        one_copy(d, p1).wait_send()
    for p in range(4):
        sib_copy(0, c, p2, p).wait_send()
    for s in range(1, half + 1):
        for p in range(4):
            if travels(s, p)[0]:
                fwd_copy(s, p2 - s + 1, p).wait_send()
                sib_copy(2 * s - 1, c, p2 - s, p).wait_send()
            if travels(s, p)[1]:
                bwd_copy(s, p2 + s - 1, p).wait_send()
                sib_copy(2 * s, c, p2 + s, p).wait_send()


def attend_kernel(ring, lanes, q_ref, kv, lens, obuf, lbuf, kfeat, qcat, acc, tot, top):
    rows = q_ref.shape[0]
    own = rows // lanes
    chunk = ring * own
    plane = ring * 2 * rows
    me, x, c, z, y = where(ring)

    lane = lax.broadcasted_iota(jnp.int32, (1, LANES), 1)
    line = lax.broadcasted_iota(jnp.int32, (LANES, 1), 0)
    ends = jnp.zeros((1, LANES), jnp.int32)
    begins = jnp.zeros((1, LANES), jnp.int32)
    ends_down = jnp.zeros((LANES, 1), jnp.int32)
    begins_down = jnp.zeros((LANES, 1), jnp.int32)
    for j in range(DOCS):
        length = lens[j]
        ends += jnp.where(lane >= j, length, 0)
        begins += jnp.where(lane > j, length, 0)
        ends_down += jnp.where(line >= j, length, 0)
        begins_down += jnp.where(line > j, length, 0)
    tok = lax.broadcasted_iota(jnp.int32, (LANES, rows), 1)
    col = lax.broadcasted_iota(jnp.int32, (LANES, rows), 0)
    pos = me * rows + tok
    hidden = jnp.where((col < DOCS) & ((pos < begins_down) | (pos >= ends_down)), -MASK, 0.0)
    hidden = jnp.where(col == DOCS, -MASK, hidden)
    first = col - 2 * DOCS
    later = (first >= 0) & (first < own) & (tok < x * own + first)
    hidden = jnp.where(later, -MASK, hidden).astype(jnp.bfloat16)
    for h in range(HEADS):
        turned = q_ref[:, h * DIM : (h + 1) * DIM].T
        qcat[:DIM, h * rows : (h + 1) * rows] = turned
        qcat[DIM:, h * rows : (h + 1) * rows] = hidden
    acc[...] = jnp.zeros_like(acc)
    tot[...] = jnp.zeros_like(tot)
    top[...] = jnp.full_like(top, EMPTY)

    def features(n, carry):
        cc, b = n // ring, lax.rem(n, ring)
        inner = lax.broadcasted_iota(jnp.int32, (own, LANES), 0)
        lanes_of = lax.broadcasted_iota(jnp.int32, (own, LANES), 1)
        for a in range(ring):
            zz, yy = place(cc, a, b)
            block = (zz * ring + yy) * 2 + cc
            at = block * rows + x * own + inner
            mark = ((at >= begins) & (at < ends)).astype(jnp.float32)
            mark = jnp.where((lanes_of == DOCS) & (block > me), 1.0, mark)
            mark = jnp.where((lanes_of == inner + 2 * DOCS) & (block == me), 1.0, mark)
            kfeat[cc, b, a * own : (a + 1) * own, :] = mark.astype(jnp.bfloat16)
        return carry

    lax.fori_loop(0, 2 * ring, features, 0)
    ones = jnp.ones((16, chunk), jnp.bfloat16)

    def scores(h, cc, b):
        keys = jnp.concatenate([kv[cc, b, 0], kfeat[cc, b]], axis=1)
        return jnp.dot(keys, qcat[:, h * rows : (h + 1) * rows], preferred_element_type=jnp.float32)

    def weighted(cc, b, p):
        vals = jnp.concatenate([kv[cc, b, 1, n : n + LANES] for n in range(0, chunk, LANES)], axis=1)
        return jnp.dot(jnp.concatenate([vals, ones], axis=0), p, preferred_element_type=jnp.float32)

    def fold(h, cc, b, s):
        old = top[h : h + 1, :]
        new = jnp.maximum(old, jnp.max(s, axis=0, keepdims=True))
        both = weighted(cc, b, jnp.exp2((s - new) * FACTOR).astype(jnp.bfloat16))
        alpha = jnp.exp2((old - new) * FACTOR)
        acc[h] = acc[h] * alpha + both[:DIM]
        tot[h : h + 1, :] = tot[h : h + 1, :] * alpha + both[DIM : DIM + 1]
        top[h : h + 1, :] = new

    def sweep(fold):
        def body(n, carry):
            cc, b = n // ring, lax.rem(n, ring)
            seen = (b <= z) & ((b + 1) * plane > me * rows - (MOST - 1))

            @pl.when((cc == 1) | seen)
            def _():
                s = scores(0, cc, b)
                for h in range(HEADS):
                    after = scores(h + 1, cc, b) if h + 1 < HEADS else None
                    fold(h, cc, b, s)
                    s = after

            return carry

        lax.fori_loop(0, 2 * ring, body, 0)

    sweep(fold)
    logs = []
    for h in range(HEADS):
        total = tot[h : h + 1, :]
        some = total > 0.0
        safe = jnp.where(some, total, 1.0)
        part = (acc[h] / safe).T.astype(jnp.bfloat16)
        logs.append(jnp.where(some, top[h : h + 1, :] * FACTOR + jnp.log2(safe), NOTHING))
        for j in range(lanes):
            obuf[j, :, h * DIM : (h + 1) * DIM] = part[j * own : (j + 1) * own, :]
    lbuf[...] = jnp.concatenate(logs, axis=0)


def merge_kernel(lanes, obuf, lbuf, out_ref, rbuf, logs, mixing, relay, s_out, r_out, s_log, r_log, s_rel, r_rel):
    x = lax.axis_index("ka")
    own = out_ref.shape[0]
    rows = lbuf.shape[1]
    near = [d for d in range(1, lanes) if lanes != 4 or d != 2]

    def peer(d):
        return lax.rem(x + d, lanes)

    def copy(src, dst, send, recv, d):
        return pltpu.make_async_remote_copy(
            src_ref=src, dst_ref=dst, send_sem=send, recv_sem=recv, device_id={"ka": peer(d)}, device_id_type=MESH
        )

    def cols_of(g):
        return pl.ds(g * 2 * DIM, 2 * DIM)

    def out_copy(d, g):
        cols = cols_of(g)
        return copy(obuf.at[peer(d), :, cols], rbuf.at[d, :, cols], s_out.at[d, g], r_out.at[d, g], d)

    def way(g):
        return 1 if g < HEADS // 4 else 3

    def relay_copy(g):
        cols = cols_of(g)
        return copy(obuf.at[peer(2), :, cols], relay.at[:, cols], s_rel.at[g], r_rel.at[g], way(g))

    def onward_copy(g):
        cols = cols_of(g)
        return copy(relay.at[:, cols], rbuf.at[2, :, cols], s_out.at[2, g], r_out.at[2, g], way(g))

    def log_copy(d):
        return copy(lbuf, logs.at[d], s_log.at[d], r_log.at[d], d)

    greet([{"ka": peer(d)} for d in range(1, lanes)])()
    groups = range(HEADS // 2)
    for d in range(1, lanes):
        log_copy(d).start()
    if lanes == 4:
        for g in (0, 2, 1, 3):
            relay_copy(g).start()
    for g in groups:
        for d in near:
            out_copy(d, g).start()
    if lanes == 4:
        for g in (0, 2, 1, 3):
            relay_copy(g).wait_recv()
            onward_copy(g).start()
    for d in range(1, lanes):
        log_copy(d).wait_recv()
    sizes = [lbuf[...]] + [logs[d] for d in range(1, lanes)]
    highest = functools.reduce(jnp.maximum, sizes)
    shares = [jnp.exp2(size - highest) for size in sizes]
    whole = functools.reduce(jnp.add, shares)
    shares = [share / whole for share in shares]
    shares.append(jnp.zeros((LANES - HEADS * lanes, rows), jnp.float32))
    mixing[...] = jnp.concatenate(shares, axis=0).T
    mix = mixing[pl.ds(pl.multiple_of(x * own, own), own), :]
    for g in groups:
        for d in range(1, lanes):
            out_copy(d, g).wait_recv()
        for h in (2 * g, 2 * g + 1):
            cols = slice(h * DIM, (h + 1) * DIM)
            mixed = mix[:, h : h + 1] * obuf[x, :, cols].astype(jnp.float32)
            for d in range(1, lanes):
                at = d * HEADS + h
                mixed += mix[:, at : at + 1] * rbuf[d, :, cols].astype(jnp.float32)
            out_ref[:, cols] = mixed.astype(out_ref.dtype)
    for d in range(1, lanes):
        log_copy(d).wait_send()
    for g in groups:
        for d in near:
            out_copy(d, g).wait_send()
        if lanes == 4:
            relay_copy(g).wait_send()
            onward_copy(g).wait_send()


def steady(ring, lanes, queries, keys, values, doc_lengths):
    rows, own = queries.shape[0], keys.shape[0]
    half = ring // 2
    chunk = ring * own
    vmem = pl.BlockSpec(memory_space=pltpu.VMEM)
    sems = pltpu.SemaphoreType.DMA
    limit = 48 * 1024 * 1024
    kv = pl.pallas_call(
        functools.partial(gather_kernel, ring),
        out_shape=jax.ShapeDtypeStruct((2, ring, 2, chunk, DIM), jnp.bfloat16),
        in_specs=[vmem, vmem],
        out_specs=vmem,
        scratch_shapes=[
            pltpu.VMEM((ring, own, 2 * DIM), jnp.bfloat16),
            sems((ring - 1,)), sems((ring - 1,)),
            sems((half, 4)), sems((half, 4)), sems((half, 4)), sems((half, 4)),
            sems((2 * half + 1, 4)), sems((2 * half + 1, 4)),
        ],
        compiler_params=pltpu.CompilerParams(collective_id=1, has_side_effects=True, vmem_limit_bytes=limit),
        name="gather",
    )(keys, values)
    parts, logs = pl.pallas_call(
        functools.partial(attend_kernel, ring, lanes),
        out_shape=(
            jax.ShapeDtypeStruct((lanes, own, HEADS * DIM), jnp.bfloat16),
            jax.ShapeDtypeStruct((HEADS, rows), jnp.float32),
        ),
        in_specs=[vmem, vmem, pl.BlockSpec(memory_space=pltpu.SMEM)],
        out_specs=(vmem, vmem),
        scratch_shapes=[
            pltpu.VMEM((2, ring, chunk, LANES), jnp.bfloat16),
            pltpu.VMEM((2 * DIM, HEADS * rows), jnp.bfloat16),
            pltpu.VMEM((HEADS, DIM, rows), jnp.float32),
            pltpu.VMEM((HEADS, rows), jnp.float32),
            pltpu.VMEM((HEADS, rows), jnp.float32),
        ],
        compiler_params=pltpu.CompilerParams(vmem_limit_bytes=limit),
        name="attend",
    )(queries, kv, doc_lengths)
    return pl.pallas_call(
        functools.partial(merge_kernel, lanes),
        out_shape=jax.ShapeDtypeStruct((own, HEADS * DIM), jnp.bfloat16),
        in_specs=[vmem, vmem],
        out_specs=vmem,
        scratch_shapes=[
            pltpu.VMEM((lanes, own, HEADS * DIM), jnp.bfloat16),
            pltpu.VMEM((lanes, HEADS, rows), jnp.float32),
            pltpu.VMEM((rows, LANES), jnp.float32),
            pltpu.VMEM((own, HEADS * DIM), jnp.bfloat16),
            sems((lanes, HEADS // 2)), sems((lanes, HEADS // 2)),
            sems((lanes,)), sems((lanes,)),
            sems((HEADS // 2,)), sems((HEADS // 2,)),
        ],
        compiler_params=pltpu.CompilerParams(collective_id=2, has_side_effects=True, vmem_limit_bytes=limit),
        name="merge",
    )(parts, logs)


def per_device(ring, lanes, queries, keys, values, doc_lengths):
    args = (queries, keys, values, doc_lengths)
    out, bound = swift(ring, lanes, *args)
    fits = bound[0, 0] <= (SAFE / FACTOR) ** 2
    return lax.cond(fits, lambda *_: out, functools.partial(steady, ring, lanes), *args)


def solution(mesh):
    ring = math.isqrt(mesh.shape["pb"] // 2)
    return jax.shard_map(
        functools.partial(per_device, ring, mesh.shape["ka"]),
        mesh=mesh,
        in_specs=(P("pb", None), P(("pb", "ka"), None), P(("pb", "ka"), None), P()),
        out_specs=P(("pb", "ka"), None),
        check_vma=False,
    )
```

```python
import functools
import math

import jax
import jax.numpy as jnp
from jax import lax
from jax.experimental import pallas as pl
from jax.experimental.pallas import tpu as pltpu
from jax.sharding import PartitionSpec as P

HEADS = 8
DIM = 128
DOCS = 8
MOST = 24576
LANES = 128
FACTOR = math.log2(math.e) / math.sqrt(DIM)
MASK = 131072.0
EMPTY = -65536.0
NOTHING = -1e30
EXTRA = 16
SAFE = 100.0
MESH = pl.DeviceIdType.MESH


def place(c, first, second):
    z = second * (1 - c) + first * c
    y = first * (1 - c) + second * c
    return z, y


def swift_kernel(
    ring, lanes, q_hbm, k_hbm, v_hbm, len_hbm, out_ref, bound_ref,
    q_in, k_in, v_in, lens, stage, kv, kfeat, qcat, acc, tot, obuf, rbuf, sums, mixing,
    s_in, s_one, r_one, s_fwd, r_fwd, s_bwd, r_bwd, s_sib, r_sib, s_cross, r_cross, s_out, r_out, s_sum, r_sum,
):
    half = ring // 2
    rows = q_in.shape[0]
    own = k_in.shape[0]
    chunk = ring * own
    plane = ring * 2 * rows
    me = lax.axis_index("pb")
    x = lax.axis_index("ka")
    c = lax.rem(me, 2)
    z = me // (2 * ring)
    y = lax.rem(me // 2, ring)
    p1 = y * (1 - c) + z * c
    p2 = z * (1 - c) + y * c

    def wrap(value):
        return lax.rem(value + 2 * ring, ring)

    def device(first, second, core=c):
        zz, yy = place(c, wrap(first), wrap(second))
        return {"pb": (zz * ring + yy) * 2 + core}

    sibling = {"pb": me + 1 - 2 * c}

    barrier = pltpu.get_barrier_semaphore()
    partners = [device(p1 + d, p2) for d in range(1, ring)]
    partners += [device(p1, p2 + d, core) for d in (1, -1) for core in (c, 1 - c)]
    partners += [device(p1 + d, p2, 1 - c) for d in (1, -1)]
    partners += [sibling] + [{"ka": lax.rem(x + d, lanes)} for d in range(1, lanes)]
    for partner in partners:
        pl.semaphore_signal(barrier, inc=1, device_id=partner, device_id_type=MESH)
    moves = [
        pltpu.make_async_copy(src, dst, s_in.at[n])
        for n, (src, dst) in enumerate(((k_hbm, k_in), (v_hbm, v_in), (len_hbm, lens), (q_hbm, q_in)))
    ]
    for move in moves:
        move.start()
    moves[0].wait()
    moves[1].wait()
    stage[p1, :own, :DIM] = k_in[...]
    stage[p1, :own, DIM:] = v_in[...]
    wide = k_in[...].astype(jnp.float32)
    longest = jnp.max(jnp.sum(wide * wide, axis=1, keepdims=True), axis=0, keepdims=True)
    stage[p1, own:, :DIM] = jnp.broadcast_to(longest * 1.01, (EXTRA, DIM)).astype(jnp.bfloat16)
    moves[3].wait()
    longest = jnp.zeros((rows, 1), jnp.float32)
    for h in range(HEADS):
        wide = q_in[:, h * DIM : (h + 1) * DIM].astype(jnp.float32)
        longest = jnp.maximum(longest, jnp.sum(wide * wide, axis=1, keepdims=True))
    longest = jnp.max(longest, axis=0, keepdims=True)
    stage[p1, own:, DIM:] = jnp.broadcast_to(longest * 1.01, (EXTRA, DIM)).astype(jnp.bfloat16)
    pl.semaphore_wait(barrier, len(partners))

    def copy(ref, send, recv, where):
        return pltpu.make_async_remote_copy(
            src_ref=ref, dst_ref=ref, send_sem=send, recv_sem=recv, device_id=where, device_id_type=MESH
        )

    def one_copy(d, b1):
        return copy(stage.at[wrap(b1)], s_one.at[d - 1], r_one.at[d - 1], device(p1 + d, p2))

    def piece(cc, b, i):
        return kv.at[cc, wrap(b), i]

    def fwd_copy(s, b, i):
        return copy(piece(c, b, i), s_fwd.at[s - 1, i], r_fwd.at[s - 1, i], device(p1, p2 + 1))

    def bwd_copy(s, b, i):
        return copy(piece(c, b, i), s_bwd.at[s - 1, i], r_bwd.at[s - 1, i], device(p1, p2 - 1))

    def sib_copy(k, cc, b, i):
        return copy(piece(cc, b, i), s_sib.at[k, i], r_sib.at[k, i], sibling)

    def cross_copy(cc, b, i):
        return copy(piece(cc, b, i), s_cross.at[i], r_cross.at[i], device(p1, p2 + 1 - 2 * i, 1 - c))

    def pass_on(s):
        for i in range(2):
            fwd_copy(s, p2 - s, i).wait_recv()
            if s + 1 < half or i == 0:
                fwd_copy(s + 1, p2 - s, i).start()
            bwd_copy(s, p2 + s, i).wait_recv()
            if s + 1 < half or i == 1:
                bwd_copy(s + 1, p2 + s, i).start()
            if s + 1 == half:
                cross_copy(c, p2 - s + 2 * i * s, i).start()
        for i in range(2):
            sib_copy(2 * s - 1, c, p2 - s, i).start()
            sib_copy(2 * s, c, p2 + s, i).start()

    def sib_arrived(s):
        for i in range(2):
            sib_copy(2 * s - 1, 1 - c, p1 - s, i).wait_recv()
            sib_copy(2 * s, 1 - c, p1 + s, i).wait_recv()

    for d in range(1, ring):
        one_copy(d, p1).start()
    moves[2].wait()

    lane = lax.broadcasted_iota(jnp.int32, (1, LANES), 1)
    line = lax.broadcasted_iota(jnp.int32, (LANES, 1), 0)
    ends = jnp.zeros((1, LANES), jnp.int32)
    begins = jnp.zeros((1, LANES), jnp.int32)
    ends_down = jnp.zeros((LANES, 1), jnp.int32)
    begins_down = jnp.zeros((LANES, 1), jnp.int32)
    for j in range(DOCS):
        length = lens[j]
        ends += jnp.where(lane >= j, length, 0)
        begins += jnp.where(lane > j, length, 0)
        ends_down += jnp.where(line >= j, length, 0)
        begins_down += jnp.where(line > j, length, 0)
    tok = lax.broadcasted_iota(jnp.int32, (LANES, rows), 1)
    col = lax.broadcasted_iota(jnp.int32, (LANES, rows), 0)
    pos = me * rows + tok
    hidden = jnp.where((col < DOCS) & ((pos < begins_down) | (pos >= ends_down)), -MASK, 0.0)
    hidden = jnp.where(col == DOCS, -MASK, hidden)
    first = col - 2 * DOCS
    later = (first >= 0) & (first < own) & (tok < x * own + first)
    hidden = jnp.where(later, -MASK, hidden).astype(jnp.bfloat16)
    for h in range(HEADS):
        qcat[h, :DIM, :] = q_in[:, h * DIM : (h + 1) * DIM].T
        qcat[h, DIM:, :] = hidden
    acc[...] = jnp.zeros_like(acc)
    tot[...] = jnp.zeros_like(tot)

    def features(n, carry):
        cc, b = n // ring, lax.rem(n, ring)
        inner = lax.broadcasted_iota(jnp.int32, (own, LANES), 0)
        lanes_of = lax.broadcasted_iota(jnp.int32, (own, LANES), 1)
        for a in range(ring):
            zz, yy = place(cc, a, b)
            block = (zz * ring + yy) * 2 + cc
            at = block * rows + x * own + inner
            mark = ((at >= begins) & (at < ends)).astype(jnp.float32)
            mark = jnp.where((lanes_of == DOCS) & (block > me), 1.0, mark)
            mark = jnp.where((lanes_of == inner + 2 * DOCS) & (block == me), 1.0, mark)
            kfeat[cc, b, a * own : (a + 1) * own, :] = mark.astype(jnp.bfloat16)
        return carry

    lax.fori_loop(0, 2 * ring, features, 0)

    ones = jnp.ones((16, chunk), jnp.bfloat16)

    def scores(h, cc, b, size):
        keys = jnp.concatenate([kv[cc, b, 0, :size], kfeat[cc, b, :size]], axis=1)
        return jnp.dot(keys, qcat[h], preferred_element_type=jnp.float32)

    def fold(h, cc, b, size, s):
        p = jnp.exp2(s * FACTOR).astype(jnp.bfloat16)
        vals = jnp.concatenate([kv[cc, b, 1, n : n + LANES] for n in range(0, size, LANES)], axis=1)
        both = jnp.dot(jnp.concatenate([vals, ones[:, :size]], axis=0), p, preferred_element_type=jnp.float32)
        acc[h] += both[:DIM]
        tot[h] += both[DIM : DIM + 1]

    def run(work):
        s = scores(*work[0])
        for n, item in enumerate(work):
            after = scores(*work[n + 1]) if n + 1 < len(work) else None
            fold(*item, s)
            s = after

    for d in range(1, ring):
        one_copy(d, p1 - d).wait_recv()
    for n in range(ring):
        kv[c, p2, 0, n * own : (n + 1) * own] = stage[n, :own, :DIM]
    largest = functools.reduce(jnp.maximum, [stage[n, own:, :] for n in range(ring)])
    kv[c, p2, 0, chunk:] = largest[:, :DIM]
    kv[c, p2, 1, chunk:] = largest[:, DIM:]
    fwd_copy(1, p2, 0).start()
    bwd_copy(1, p2, 0).start()
    side = LANES // own
    for n in range(ring // side):
        block = stage[n * side : (n + 1) * side, :own, DIM:].reshape(LANES, DIM)
        kv[c, p2, 1, n * LANES : (n + 1) * LANES] = block.T
    fwd_copy(1, p2, 1).start()
    bwd_copy(1, p2, 1).start()
    for i in range(2):
        sib_copy(0, c, p2, i).start()

    def seen(b):
        return (b <= z) & ((b + 1) * plane > me * rows - (MOST - 1))

    def unit(u, carry):
        v = jnp.maximum(u - 2, 0)
        s = v // 4 + 1
        r = lax.rem(v, 4)
        early = u < 2
        mine = jnp.where(early, u == 0, r < 2)
        cc = jnp.where(mine, c, 1 - c)
        shift = jnp.where(early, 0, (2 * lax.rem(r, 2) - 1) * s)
        b = wrap(jnp.where(mine, p2, p1) + shift)

        @pl.when(u == 1)
        def _():
            for i in range(2):
                sib_copy(0, 1 - c, p1, i).wait_recv()

        @pl.when((u >= 2) & (r == 2))
        def _():
            sib_arrived(s)

        @pl.when((cc == 1) | seen(b))
        def _():
            run([(h, cc, b, chunk) for h in range(HEADS)])

        for step, after in ((1, 1), (2, 3), (3, 6)):
            if step < half:
                pl.when(u == after)(functools.partial(pass_on, step))
        return carry

    lax.fori_loop(0, 2 + 4 * (half - 2), unit, 0)
    sib_arrived(half - 1)
    fwd_copy(half, p2 - half, 0).wait_recv()
    bwd_copy(half, p2 + half, 1).wait_recv()
    cross_copy(1 - c, p1 - half, 0).wait_recv()
    cross_copy(1 - c, p1 + half, 1).wait_recv()

    def peer(d):
        return lax.rem(x + d, lanes)

    def out_copy(d, h):
        cols = pl.ds(pl.multiple_of(h * DIM, DIM), DIM)
        return pltpu.make_async_remote_copy(
            src_ref=obuf.at[peer(d), :, cols], dst_ref=rbuf.at[d, :, cols],
            send_sem=s_out.at[d, h], recv_sem=r_out.at[d, h], device_id={"ka": peer(d)}, device_id_type=MESH,
        )

    def sum_copy(d):
        return pltpu.make_async_remote_copy(
            src_ref=sums.at[0], dst_ref=sums.at[d],
            send_sem=s_sum.at[d], recv_sem=r_sum.at[d], device_id={"ka": peer(d)}, device_id_type=MESH,
        )

    shifts = (1 - half, half - 1, half)
    early_cc = [(c, p2 + d) for d in shifts[:2]] + [(1 - c, p1 + d) for d in shifts[:2]]
    late = early_cc + [(c, p2 + half), (1 - c, p1 + half)]
    some = functools.reduce(jnp.logical_or, [seen(wrap(z + d)) for d in shifts])

    def finish(work, h, carry):
        run([(h, cc, wrap(b), size) for cc, b, size in work])
        part = acc[h].T.astype(jnp.bfloat16)
        sums[0, h] = tot[h]
        cols = pl.ds(pl.multiple_of(h * DIM, DIM), DIM)
        for j in range(lanes):
            obuf[j, :, cols] = part[j * own : (j + 1) * own, :]
        for d in range(1, lanes):
            out_copy(d, h).start()
        return carry

    @pl.when(some)
    def _():
        lax.fori_loop(0, HEADS, functools.partial(finish, [(cc, b, chunk) for cc, b in late]), 0)

    @pl.when(jnp.logical_not(some))
    def _():
        lax.fori_loop(0, HEADS, functools.partial(finish, [(1, y + d, chunk // 2) for d in shifts]), 0)

    for i in range(2):
        met = [kv[cc, b, i, chunk:] for cc in range(2) for b in range(ring)]
        met = functools.reduce(jnp.maximum, met)[:1, :].astype(jnp.float32)
        sums[0, HEADS + i] = jnp.concatenate([met] * (rows // LANES), axis=1)
    for d in range(1, lanes):
        sum_copy(d).start()
    for d in range(1, ring):
        one_copy(d, p1).wait_send()
    for i in range(2):
        sib_copy(0, c, p2, i).wait_send()
        for s in range(1, half):
            fwd_copy(s, p2 - s + 1, i).wait_send()
            bwd_copy(s, p2 + s - 1, i).wait_send()
            sib_copy(2 * s - 1, c, p2 - s, i).wait_send()
            sib_copy(2 * s, c, p2 + s, i).wait_send()
        cross_copy(c, p2 + (2 * i - 1) * (half - 1), i).wait_send()
    fwd_copy(half, p2 - half + 1, 0).wait_send()
    bwd_copy(half, p2 + half - 1, 1).wait_send()
    for d in range(1, lanes):
        sum_copy(d).wait_recv()
    whole = functools.reduce(jnp.add, [sums[d] for d in range(lanes)])
    share = [1.0 / whole[h] for h in range(HEADS)] + [jnp.zeros((LANES - HEADS, rows), jnp.float32)]
    mixing[...] = jnp.concatenate(share, axis=0).T
    met = functools.reduce(jnp.maximum, [sums[d] for d in range(lanes)])
    bound_ref[0] = jnp.max(met[HEADS] * met[HEADS + 1])
    mix = mixing[pl.ds(pl.multiple_of(x * own, own), own), :]
    for h in range(HEADS):
        cols = slice(h * DIM, (h + 1) * DIM)
        mixed = obuf[x, :, cols].astype(jnp.float32)
        for d in range(1, lanes):
            out_copy(d, h).wait_recv()
            mixed += rbuf[d, :, cols].astype(jnp.float32)
        out_ref[:, cols] = (mixed * mix[:, h : h + 1]).astype(out_ref.dtype)

    for d in range(1, lanes):
        sum_copy(d).wait_send()
        for h in range(HEADS):
            out_copy(d, h).wait_send()


def swift(ring, lanes, queries, keys, values, doc_lengths):
    rows, own = queries.shape[0], keys.shape[0]
    half = ring // 2
    chunk = ring * own
    vmem = pl.BlockSpec(memory_space=pltpu.VMEM)
    sems = pltpu.SemaphoreType.DMA
    parts = (lanes, own, HEADS * DIM)
    return pl.pallas_call(
        functools.partial(swift_kernel, ring, lanes),
        out_shape=(
            jax.ShapeDtypeStruct((own, HEADS * DIM), jnp.bfloat16),
            jax.ShapeDtypeStruct((1,), jnp.float32),
        ),
        in_specs=[pl.BlockSpec(memory_space=pltpu.HBM)] * 4,
        out_specs=(vmem, pl.BlockSpec(memory_space=pltpu.SMEM)),
        scratch_shapes=[
            pltpu.VMEM(queries.shape, jnp.bfloat16),
            pltpu.VMEM(keys.shape, jnp.bfloat16),
            pltpu.VMEM(values.shape, jnp.bfloat16),
            pltpu.SMEM(doc_lengths.shape, jnp.int32),
            pltpu.VMEM((ring, own + EXTRA, 2 * DIM), jnp.bfloat16),
            pltpu.VMEM((2, ring, 2, chunk + EXTRA, DIM), jnp.bfloat16),
            pltpu.VMEM((2, ring, chunk, LANES), jnp.bfloat16),
            pltpu.VMEM((HEADS, 2 * DIM, rows), jnp.bfloat16),
            pltpu.VMEM((HEADS, DIM, rows), jnp.float32),
            pltpu.VMEM((HEADS, 1, rows), jnp.float32),
            pltpu.VMEM(parts, jnp.bfloat16),
            pltpu.VMEM(parts, jnp.bfloat16),
            pltpu.VMEM((lanes, HEADS + 2, 1, rows), jnp.float32),
            pltpu.VMEM((rows, LANES), jnp.float32),
            sems((4,)),
            sems((ring - 1,)), sems((ring - 1,)),
            sems((half, 2)), sems((half, 2)), sems((half, 2)), sems((half, 2)),
            sems((2 * half - 1, 2)), sems((2 * half - 1, 2)), sems((2,)), sems((2,)),
            sems((lanes, HEADS)), sems((lanes, HEADS)),
            sems((lanes,)), sems((lanes,)),
        ],
        compiler_params=pltpu.CompilerParams(
            collective_id=0, has_side_effects=True, vmem_limit_bytes=63 * 1024 * 1024
        ),
        cost_estimate=pl.CostEstimate(flops=10**10, bytes_accessed=10**7, transcendentals=10**7),
        name="swift",
    )(queries, keys, values, doc_lengths)


def where(ring):
    me = lax.axis_index("pb")
    x = lax.axis_index("ka")
    c = lax.rem(me, 2)
    z = me // (2 * ring)
    y = lax.rem(me // 2, ring)
    return me, x, c, z, y


def greet(partners):
    barrier = pltpu.get_barrier_semaphore()
    for partner in partners:
        pl.semaphore_signal(barrier, inc=1, device_id=partner, device_id_type=MESH)
    return lambda: pl.semaphore_wait(barrier, len(partners))


def gather_kernel(
    ring, k_ref, v_ref, kv, stage,
    s_one, r_one, s_fwd, r_fwd, s_bwd, r_bwd, s_sib, r_sib,
):
    half = ring // 2
    own = k_ref.shape[0]
    me, x, c, z, y = where(ring)
    p1 = y * (1 - c) + z * c
    p2 = z * (1 - c) + y * c

    def wrap(value):
        return lax.rem(value + 2 * ring, ring)

    def device(first, second):
        zz, yy = place(c, wrap(first), wrap(second))
        return {"pb": (zz * ring + yy) * 2 + c}

    sibling = {"pb": me + 1 - 2 * c}
    partners = [device(p1 + d, p2) for d in range(1, ring)]
    partners += [device(p1, p2 + d) for d in ((1, ring - 1) if ring > 2 else (1,))]
    ready = greet(partners + [sibling])
    stage[p1, :, :DIM] = k_ref[...]
    stage[p1, :, DIM:] = v_ref[...]
    ready()

    def copy(ref, send, recv, to):
        return pltpu.make_async_remote_copy(
            src_ref=ref, dst_ref=ref, send_sem=send, recv_sem=recv, device_id=to, device_id_type=MESH
        )

    def one_copy(d, b1):
        return copy(stage.at[wrap(b1)], s_one.at[d - 1], r_one.at[d - 1], device(p1 + d, p2))

    def piece(cc, b, p):
        size = ring * own // 2
        return kv.at[cc, wrap(b), p // 2, pl.ds((p % 2) * size, size)]

    def fwd_copy(s, b, p):
        return copy(piece(c, b, p), s_fwd.at[s - 1, p], r_fwd.at[s - 1, p], device(p1, p2 + 1))

    def bwd_copy(s, b, p):
        return copy(piece(c, b, p), s_bwd.at[s - 1, p], r_bwd.at[s - 1, p], device(p1, p2 - 1))

    def sib_copy(n, cc, b, p):
        return copy(piece(cc, b, p), s_sib.at[n, p], r_sib.at[n, p], sibling)

    def travels(s, p):
        return s < half or (s == half and p < 2), s < half or (s == half and p >= 2)

    for d in range(1, ring):
        one_copy(d, p1).start()
    for d in range(1, ring):
        one_copy(d, p1 - d).wait_recv()
    for n in range(ring):
        kv[c, p2, 0, n * own : (n + 1) * own] = stage[n, :, :DIM]
    side = LANES // own
    for n in range(ring // side):
        block = stage[n * side : (n + 1) * side, :, DIM:].reshape(LANES, DIM)
        kv[c, p2, 1, n * LANES : (n + 1) * LANES] = block.T
    for p in range(4):
        if travels(1, p)[0]:
            fwd_copy(1, p2, p).start()
        if travels(1, p)[1]:
            bwd_copy(1, p2, p).start()
    for p in range(4):
        sib_copy(0, c, p2, p).start()
    for s in range(1, half + 1):
        for p in range(4):
            if travels(s, p)[0]:
                fwd_copy(s, p2 - s, p).wait_recv()
                if travels(s + 1, p)[0]:
                    fwd_copy(s + 1, p2 - s, p).start()
            if travels(s, p)[1]:
                bwd_copy(s, p2 + s, p).wait_recv()
                if travels(s + 1, p)[1]:
                    bwd_copy(s + 1, p2 + s, p).start()
        for p in range(4):
            if travels(s, p)[0]:
                sib_copy(2 * s - 1, c, p2 - s, p).start()
            if travels(s, p)[1]:
                sib_copy(2 * s, c, p2 + s, p).start()
    for p in range(4):
        sib_copy(0, 1 - c, p1, p).wait_recv()
    for s in range(1, half + 1):
        for p in range(4):
            if travels(s, p)[0]:
                sib_copy(2 * s - 1, 1 - c, p1 - s, p).wait_recv()
            if travels(s, p)[1]:
                sib_copy(2 * s, 1 - c, p1 + s, p).wait_recv()
    for d in range(1, ring):
        one_copy(d, p1).wait_send()
    for p in range(4):
        sib_copy(0, c, p2, p).wait_send()
    for s in range(1, half + 1):
        for p in range(4):
            if travels(s, p)[0]:
                fwd_copy(s, p2 - s + 1, p).wait_send()
                sib_copy(2 * s - 1, c, p2 - s, p).wait_send()
            if travels(s, p)[1]:
                bwd_copy(s, p2 + s - 1, p).wait_send()
                sib_copy(2 * s, c, p2 + s, p).wait_send()


def attend_kernel(ring, lanes, q_ref, kv, lens, obuf, lbuf, kfeat, qcat, acc, tot, top):
    rows = q_ref.shape[0]
    own = rows // lanes
    chunk = ring * own
    plane = ring * 2 * rows
    me, x, c, z, y = where(ring)

    lane = lax.broadcasted_iota(jnp.int32, (1, LANES), 1)
    line = lax.broadcasted_iota(jnp.int32, (LANES, 1), 0)
    ends = jnp.zeros((1, LANES), jnp.int32)
    begins = jnp.zeros((1, LANES), jnp.int32)
    ends_down = jnp.zeros((LANES, 1), jnp.int32)
    begins_down = jnp.zeros((LANES, 1), jnp.int32)
    for j in range(DOCS):
        length = lens[j]
        ends += jnp.where(lane >= j, length, 0)
        begins += jnp.where(lane > j, length, 0)
        ends_down += jnp.where(line >= j, length, 0)
        begins_down += jnp.where(line > j, length, 0)
    tok = lax.broadcasted_iota(jnp.int32, (LANES, rows), 1)
    col = lax.broadcasted_iota(jnp.int32, (LANES, rows), 0)
    pos = me * rows + tok
    hidden = jnp.where((col < DOCS) & ((pos < begins_down) | (pos >= ends_down)), -MASK, 0.0)
    hidden = jnp.where(col == DOCS, -MASK, hidden)
    first = col - 2 * DOCS
    later = (first >= 0) & (first < own) & (tok < x * own + first)
    hidden = jnp.where(later, -MASK, hidden).astype(jnp.bfloat16)
    for h in range(HEADS):
        turned = q_ref[:, h * DIM : (h + 1) * DIM].T
        qcat[:DIM, h * rows : (h + 1) * rows] = turned
        qcat[DIM:, h * rows : (h + 1) * rows] = hidden
    acc[...] = jnp.zeros_like(acc)
    tot[...] = jnp.zeros_like(tot)
    top[...] = jnp.full_like(top, EMPTY)

    def features(n, carry):
        cc, b = n // ring, lax.rem(n, ring)
        inner = lax.broadcasted_iota(jnp.int32, (own, LANES), 0)
        lanes_of = lax.broadcasted_iota(jnp.int32, (own, LANES), 1)
        for a in range(ring):
            zz, yy = place(cc, a, b)
            block = (zz * ring + yy) * 2 + cc
            at = block * rows + x * own + inner
            mark = ((at >= begins) & (at < ends)).astype(jnp.float32)
            mark = jnp.where((lanes_of == DOCS) & (block > me), 1.0, mark)
            mark = jnp.where((lanes_of == inner + 2 * DOCS) & (block == me), 1.0, mark)
            kfeat[cc, b, a * own : (a + 1) * own, :] = mark.astype(jnp.bfloat16)
        return carry

    lax.fori_loop(0, 2 * ring, features, 0)
    ones = jnp.ones((16, chunk), jnp.bfloat16)

    def scores(h, cc, b):
        keys = jnp.concatenate([kv[cc, b, 0], kfeat[cc, b]], axis=1)
        return jnp.dot(keys, qcat[:, h * rows : (h + 1) * rows], preferred_element_type=jnp.float32)

    def weighted(cc, b, p):
        vals = jnp.concatenate([kv[cc, b, 1, n : n + LANES] for n in range(0, chunk, LANES)], axis=1)
        return jnp.dot(jnp.concatenate([vals, ones], axis=0), p, preferred_element_type=jnp.float32)

    def fold(h, cc, b, s):
        old = top[h : h + 1, :]
        new = jnp.maximum(old, jnp.max(s, axis=0, keepdims=True))
        both = weighted(cc, b, jnp.exp2((s - new) * FACTOR).astype(jnp.bfloat16))
        alpha = jnp.exp2((old - new) * FACTOR)
        acc[h] = acc[h] * alpha + both[:DIM]
        tot[h : h + 1, :] = tot[h : h + 1, :] * alpha + both[DIM : DIM + 1]
        top[h : h + 1, :] = new

    def sweep(fold):
        def body(n, carry):
            cc, b = n // ring, lax.rem(n, ring)
            seen = (b <= z) & ((b + 1) * plane > me * rows - (MOST - 1))

            @pl.when((cc == 1) | seen)
            def _():
                s = scores(0, cc, b)
                for h in range(HEADS):
                    after = scores(h + 1, cc, b) if h + 1 < HEADS else None
                    fold(h, cc, b, s)
                    s = after

            return carry

        lax.fori_loop(0, 2 * ring, body, 0)

    sweep(fold)
    logs = []
    for h in range(HEADS):
        total = tot[h : h + 1, :]
        some = total > 0.0
        safe = jnp.where(some, total, 1.0)
        part = (acc[h] / safe).T.astype(jnp.bfloat16)
        logs.append(jnp.where(some, top[h : h + 1, :] * FACTOR + jnp.log2(safe), NOTHING))
        for j in range(lanes):
            obuf[j, :, h * DIM : (h + 1) * DIM] = part[j * own : (j + 1) * own, :]
    lbuf[...] = jnp.concatenate(logs, axis=0)


def merge_kernel(lanes, obuf, lbuf, out_ref, rbuf, logs, mixing, relay, s_out, r_out, s_log, r_log, s_rel, r_rel):
    x = lax.axis_index("ka")
    own = out_ref.shape[0]
    rows = lbuf.shape[1]
    near = [d for d in range(1, lanes) if lanes != 4 or d != 2]

    def peer(d):
        return lax.rem(x + d, lanes)

    def copy(src, dst, send, recv, d):
        return pltpu.make_async_remote_copy(
            src_ref=src, dst_ref=dst, send_sem=send, recv_sem=recv, device_id={"ka": peer(d)}, device_id_type=MESH
        )

    def cols_of(g):
        return pl.ds(g * 2 * DIM, 2 * DIM)

    def out_copy(d, g):
        cols = cols_of(g)
        return copy(obuf.at[peer(d), :, cols], rbuf.at[d, :, cols], s_out.at[d, g], r_out.at[d, g], d)

    def way(g):
        return 1 if g < HEADS // 4 else 3

    def relay_copy(g):
        cols = cols_of(g)
        return copy(obuf.at[peer(2), :, cols], relay.at[:, cols], s_rel.at[g], r_rel.at[g], way(g))

    def onward_copy(g):
        cols = cols_of(g)
        return copy(relay.at[:, cols], rbuf.at[2, :, cols], s_out.at[2, g], r_out.at[2, g], way(g))

    def log_copy(d):
        return copy(lbuf, logs.at[d], s_log.at[d], r_log.at[d], d)

    greet([{"ka": peer(d)} for d in range(1, lanes)])()
    groups = range(HEADS // 2)
    for d in range(1, lanes):
        log_copy(d).start()
    if lanes == 4:
        for g in (0, 2, 1, 3):
            relay_copy(g).start()
    for g in groups:
        for d in near:
            out_copy(d, g).start()
    if lanes == 4:
        for g in (0, 2, 1, 3):
            relay_copy(g).wait_recv()
            onward_copy(g).start()
    for d in range(1, lanes):
        log_copy(d).wait_recv()
    sizes = [lbuf[...]] + [logs[d] for d in range(1, lanes)]
    highest = functools.reduce(jnp.maximum, sizes)
    shares = [jnp.exp2(size - highest) for size in sizes]
    whole = functools.reduce(jnp.add, shares)
    shares = [share / whole for share in shares]
    shares.append(jnp.zeros((LANES - HEADS * lanes, rows), jnp.float32))
    mixing[...] = jnp.concatenate(shares, axis=0).T
    mix = mixing[pl.ds(pl.multiple_of(x * own, own), own), :]
    for g in groups:
        for d in range(1, lanes):
            out_copy(d, g).wait_recv()
        for h in (2 * g, 2 * g + 1):
            cols = slice(h * DIM, (h + 1) * DIM)
            mixed = mix[:, h : h + 1] * obuf[x, :, cols].astype(jnp.float32)
            for d in range(1, lanes):
                at = d * HEADS + h
                mixed += mix[:, at : at + 1] * rbuf[d, :, cols].astype(jnp.float32)
            out_ref[:, cols] = mixed.astype(out_ref.dtype)
    for d in range(1, lanes):
        log_copy(d).wait_send()
    for g in groups:
        for d in near:
            out_copy(d, g).wait_send()
        if lanes == 4:
            relay_copy(g).wait_send()
            onward_copy(g).wait_send()


def steady(ring, lanes, queries, keys, values, doc_lengths):
    rows, own = queries.shape[0], keys.shape[0]
    half = ring // 2
    chunk = ring * own
    vmem = pl.BlockSpec(memory_space=pltpu.VMEM)
    sems = pltpu.SemaphoreType.DMA
    limit = 48 * 1024 * 1024
    kv = pl.pallas_call(
        functools.partial(gather_kernel, ring),
        out_shape=jax.ShapeDtypeStruct((2, ring, 2, chunk, DIM), jnp.bfloat16),
        in_specs=[vmem, vmem],
        out_specs=vmem,
        scratch_shapes=[
            pltpu.VMEM((ring, own, 2 * DIM), jnp.bfloat16),
            sems((ring - 1,)), sems((ring - 1,)),
            sems((half, 4)), sems((half, 4)), sems((half, 4)), sems((half, 4)),
            sems((2 * half + 1, 4)), sems((2 * half + 1, 4)),
        ],
        compiler_params=pltpu.CompilerParams(collective_id=1, has_side_effects=True, vmem_limit_bytes=limit),
        name="gather",
    )(keys, values)
    parts, logs = pl.pallas_call(
        functools.partial(attend_kernel, ring, lanes),
        out_shape=(
            jax.ShapeDtypeStruct((lanes, own, HEADS * DIM), jnp.bfloat16),
            jax.ShapeDtypeStruct((HEADS, rows), jnp.float32),
        ),
        in_specs=[vmem, vmem, pl.BlockSpec(memory_space=pltpu.SMEM)],
        out_specs=(vmem, vmem),
        scratch_shapes=[
            pltpu.VMEM((2, ring, chunk, LANES), jnp.bfloat16),
            pltpu.VMEM((2 * DIM, HEADS * rows), jnp.bfloat16),
            pltpu.VMEM((HEADS, DIM, rows), jnp.float32),
            pltpu.VMEM((HEADS, rows), jnp.float32),
            pltpu.VMEM((HEADS, rows), jnp.float32),
        ],
        compiler_params=pltpu.CompilerParams(vmem_limit_bytes=limit),
        name="attend",
    )(queries, kv, doc_lengths)
    return pl.pallas_call(
        functools.partial(merge_kernel, lanes),
        out_shape=jax.ShapeDtypeStruct((own, HEADS * DIM), jnp.bfloat16),
        in_specs=[vmem, vmem],
        out_specs=vmem,
        scratch_shapes=[
            pltpu.VMEM((lanes, own, HEADS * DIM), jnp.bfloat16),
            pltpu.VMEM((lanes, HEADS, rows), jnp.float32),
            pltpu.VMEM((rows, LANES), jnp.float32),
            pltpu.VMEM((own, HEADS * DIM), jnp.bfloat16),
            sems((lanes, HEADS // 2)), sems((lanes, HEADS // 2)),
            sems((lanes,)), sems((lanes,)),
            sems((HEADS // 2,)), sems((HEADS // 2,)),
        ],
        compiler_params=pltpu.CompilerParams(collective_id=2, has_side_effects=True, vmem_limit_bytes=limit),
        name="merge",
    )(parts, logs)


def per_device(ring, lanes, queries, keys, values, doc_lengths):
    args = (queries, keys, values, doc_lengths)
    out, bound = swift(ring, lanes, *args)
    fits = bound[0] <= (SAFE / FACTOR) ** 2
    return lax.cond(fits, lambda *_: out, functools.partial(steady, ring, lanes), *args)


def solution(mesh):
    ring = math.isqrt(mesh.shape["pb"] // 2)
    return jax.shard_map(
        functools.partial(per_device, ring, mesh.shape["ka"]),
        mesh=mesh,
        in_specs=(P("pb", None), P(("pb", "ka"), None), P(("pb", "ka"), None), P()),
        out_specs=P(("pb", "ka"), None),
        check_vma=False,
    )
```

```python
import functools
import math

import jax
import jax.numpy as jnp
from jax import lax
from jax.experimental import pallas as pl
from jax.experimental.pallas import tpu as pltpu
from jax.sharding import PartitionSpec as P

HEADS = 8
DIM = 128
DOCS = 8
MOST = 24576
LANES = 128
FACTOR = math.log2(math.e) / math.sqrt(DIM)
MASK = 131072.0
EMPTY = -65536.0
NOTHING = -1e30
EXTRA = 16
SAFE = 100.0
MESH = pl.DeviceIdType.MESH


def place(c, first, second):
    z = second * (1 - c) + first * c
    y = first * (1 - c) + second * c
    return z, y


def swift_kernel(
    ring, lanes, q_hbm, k_hbm, v_hbm, len_hbm, out_ref, bound_ref,
    q_in, k_in, v_in, lens, stage, kv, kfeat, qcat, acc, tot, obuf, rbuf, sums, mixing,
    s_in, s_one, r_one, s_fwd, r_fwd, s_bwd, r_bwd, s_sib, r_sib, s_cross, r_cross, s_out, r_out, s_sum, r_sum,
):
    half = ring // 2
    rows = q_in.shape[0]
    own = k_in.shape[0]
    chunk = ring * own
    plane = ring * 2 * rows
    me = lax.axis_index("pb")
    x = lax.axis_index("ka")
    c = lax.rem(me, 2)
    z = me // (2 * ring)
    y = lax.rem(me // 2, ring)
    p1 = y * (1 - c) + z * c
    p2 = z * (1 - c) + y * c

    def wrap(value):
        return lax.rem(value + 2 * ring, ring)

    def device(first, second, core=c):
        zz, yy = place(c, wrap(first), wrap(second))
        return {"pb": (zz * ring + yy) * 2 + core}

    sibling = {"pb": me + 1 - 2 * c}

    barrier = pltpu.get_barrier_semaphore()
    partners = [device(p1 + d, p2) for d in range(1, ring)]
    partners += [device(p1, p2 + d, core) for d in (1, -1) for core in (c, 1 - c)]
    partners += [device(p1 + d, p2, 1 - c) for d in (1, -1)]
    partners += [sibling] + [{"ka": lax.rem(x + d, lanes)} for d in range(1, lanes)]
    for partner in partners:
        pl.semaphore_signal(barrier, inc=1, device_id=partner, device_id_type=MESH)
    moves = [
        pltpu.make_async_copy(src, dst, s_in.at[n])
        for n, (src, dst) in enumerate(((k_hbm, k_in), (v_hbm, v_in), (len_hbm, lens), (q_hbm, q_in)))
    ]
    for move in moves:
        move.start()
    moves[0].wait()
    moves[1].wait()
    stage[p1, :own] = k_in[...]
    stage[p1, own : 2 * own] = v_in[...]
    wide = k_in[...].astype(jnp.float32)
    longest = jnp.max(jnp.sum(wide * wide, axis=1, keepdims=True), axis=0, keepdims=True)
    k_most = longest
    moves[3].wait()
    longest = jnp.zeros((rows, 1), jnp.float32)
    for h in range(HEADS):
        wide = q_in[:, h * DIM : (h + 1) * DIM].astype(jnp.float32)
        longest = jnp.maximum(longest, jnp.sum(wide * wide, axis=1, keepdims=True))
    longest = jnp.max(longest, axis=0, keepdims=True)
    upper = lax.broadcasted_iota(jnp.int32, (EXTRA, DIM), 0) < EXTRA // 2
    stage[p1, 2 * own :] = (jnp.where(upper, k_most, longest) * 1.01).astype(jnp.bfloat16)
    pl.semaphore_wait(barrier, len(partners))

    def copy(ref, send, recv, where):
        return pltpu.make_async_remote_copy(
            src_ref=ref, dst_ref=ref, send_sem=send, recv_sem=recv, device_id=where, device_id_type=MESH
        )

    def one_copy(d, b1):
        return copy(stage.at[wrap(b1)], s_one.at[d - 1], r_one.at[d - 1], device(p1 + d, p2))

    def piece(cc, b, i):
        return kv.at[cc, wrap(b), i]

    def fwd_copy(s, b, i):
        return copy(piece(c, b, i), s_fwd.at[s - 1, i], r_fwd.at[s - 1, i], device(p1, p2 + 1))

    def bwd_copy(s, b, i):
        return copy(piece(c, b, i), s_bwd.at[s - 1, i], r_bwd.at[s - 1, i], device(p1, p2 - 1))

    def sib_copy(k, cc, b, i):
        return copy(piece(cc, b, i), s_sib.at[k, i], r_sib.at[k, i], sibling)

    def cross_copy(cc, b, i):
        return copy(piece(cc, b, i), s_cross.at[i], r_cross.at[i], device(p1, p2 + 1 - 2 * i, 1 - c))

    def pass_on(s):
        for i in range(2):
            fwd_copy(s, p2 - s, i).wait_recv()
            if s + 1 < half or i == 0:
                fwd_copy(s + 1, p2 - s, i).start()
            bwd_copy(s, p2 + s, i).wait_recv()
            if s + 1 < half or i == 1:
                bwd_copy(s + 1, p2 + s, i).start()
            if s + 1 == half:
                cross_copy(c, p2 - s + 2 * i * s, i).start()
        for i in range(2):
            sib_copy(2 * s - 1, c, p2 - s, i).start()
            sib_copy(2 * s, c, p2 + s, i).start()

    def sib_arrived(s):
        for i in range(2):
            sib_copy(2 * s - 1, 1 - c, p1 - s, i).wait_recv()
            sib_copy(2 * s, 1 - c, p1 + s, i).wait_recv()

    for d in sorted(range(1, ring), key=lambda d: abs(d - half)):
        one_copy(d, p1).start()
    moves[2].wait()

    lane = lax.broadcasted_iota(jnp.int32, (1, LANES), 1)
    line = lax.broadcasted_iota(jnp.int32, (LANES, 1), 0)
    ends = jnp.zeros((1, LANES), jnp.int32)
    begins = jnp.zeros((1, LANES), jnp.int32)
    ends_down = jnp.zeros((LANES, 1), jnp.int32)
    begins_down = jnp.zeros((LANES, 1), jnp.int32)
    for j in range(DOCS):
        length = lens[j]
        ends += jnp.where(lane >= j, length, 0)
        begins += jnp.where(lane > j, length, 0)
        ends_down += jnp.where(line >= j, length, 0)
        begins_down += jnp.where(line > j, length, 0)
    tok = lax.broadcasted_iota(jnp.int32, (LANES, rows), 1)
    col = lax.broadcasted_iota(jnp.int32, (LANES, rows), 0)
    pos = me * rows + tok
    hidden = jnp.where((col < DOCS) & ((pos < begins_down) | (pos >= ends_down)), -MASK, 0.0)
    hidden = jnp.where(col == DOCS, -MASK, hidden)
    first = col - 2 * DOCS
    later = (first >= 0) & (first < own) & (tok < x * own + first)
    hidden = jnp.where(later, -MASK, hidden).astype(jnp.bfloat16)
    for h in range(HEADS):
        qcat[h, :DIM, :] = q_in[:, h * DIM : (h + 1) * DIM].T
        qcat[h, DIM:, :] = hidden
    acc[...] = jnp.zeros_like(acc)
    tot[...] = jnp.zeros_like(tot)

    def features(n, carry):
        cc, b = n // ring, lax.rem(n, ring)
        inner = lax.broadcasted_iota(jnp.int32, (own, LANES), 0)
        lanes_of = lax.broadcasted_iota(jnp.int32, (own, LANES), 1)
        for a in range(ring):
            zz, yy = place(cc, a, b)
            block = (zz * ring + yy) * 2 + cc
            at = block * rows + x * own + inner
            mark = ((at >= begins) & (at < ends)).astype(jnp.float32)
            mark = jnp.where((lanes_of == DOCS) & (block > me), 1.0, mark)
            mark = jnp.where((lanes_of == inner + 2 * DOCS) & (block == me), 1.0, mark)
            kfeat[cc, b, a * own : (a + 1) * own, :] = mark.astype(jnp.bfloat16)
        return carry

    lax.fori_loop(0, 2 * ring, features, 0)

    ones = jnp.ones((16, chunk), jnp.bfloat16)

    def scores(h, cc, b, size):
        keys = jnp.concatenate([kv[cc, b, 0, :size], kfeat[cc, b, :size]], axis=1)
        return jnp.dot(keys, qcat[h], preferred_element_type=jnp.float32)

    def fold(h, cc, b, size, s):
        p = jnp.exp2(s * FACTOR).astype(jnp.bfloat16)
        vals = jnp.concatenate([kv[cc, b, 1, n : n + LANES] for n in range(0, size, LANES)], axis=1)
        both = jnp.dot(jnp.concatenate([vals, ones[:, :size]], axis=0), p, preferred_element_type=jnp.float32)
        acc[h] += both[:DIM]
        tot[h] += both[DIM : DIM + 1]

    def run(work):
        s = scores(*work[0])
        for n, item in enumerate(work):
            after = scores(*work[n + 1]) if n + 1 < len(work) else None
            fold(*item, s)
            s = after

    for d in range(1, ring):
        one_copy(d, p1 - d).wait_recv()
    for n in range(ring):
        kv[c, p2, 0, n * own : (n + 1) * own] = stage[n, :own]
    largest = functools.reduce(jnp.maximum, [stage[n, 2 * own :] for n in range(ring)])
    for i in range(2):
        kv[c, p2, i, chunk:] = largest
    fwd_copy(1, p2, 0).start()
    bwd_copy(1, p2, 0).start()
    side = LANES // own
    for n in range(ring // side):
        block = stage[n * side : (n + 1) * side, own : 2 * own].reshape(LANES, DIM)
        kv[c, p2, 1, n * LANES : (n + 1) * LANES] = block.T
    fwd_copy(1, p2, 1).start()
    bwd_copy(1, p2, 1).start()
    for i in range(2):
        sib_copy(0, c, p2, i).start()

    def seen(b):
        return (b <= z) & ((b + 1) * plane > me * rows - (MOST - 1))

    def unit(u, carry):
        v = jnp.maximum(u - 2, 0)
        s = v // 4 + 1
        r = lax.rem(v, 4)
        early = u < 2
        mine = jnp.where(early, u == 0, r < 2)
        cc = jnp.where(mine, c, 1 - c)
        shift = jnp.where(early, 0, (2 * lax.rem(r, 2) - 1) * s)
        b = wrap(jnp.where(mine, p2, p1) + shift)

        @pl.when(u == 1)
        def _():
            for i in range(2):
                sib_copy(0, 1 - c, p1, i).wait_recv()

        @pl.when((u >= 2) & (r == 2))
        def _():
            sib_arrived(s)

        @pl.when((cc == 1) | seen(b))
        def _():
            run([(h, cc, b, chunk) for h in range(HEADS)])

        for step, after in ((1, 0), (2, 3), (3, 6)):
            if step < half:
                pl.when(u == after)(functools.partial(pass_on, step))
        return carry

    lax.fori_loop(0, 2 + 4 * (half - 2), unit, 0)

    def last_mine():
        fwd_copy(half, p2 - half, 0).wait_recv()
        bwd_copy(half, p2 + half, 1).wait_recv()

    def last_other():
        sib_arrived(half - 1)
        cross_copy(1 - c, p1 - half, 0).wait_recv()
        cross_copy(1 - c, p1 + half, 1).wait_recv()

    def peer(d):
        return lax.rem(x + d, lanes)

    def out_copy(d, g):
        cols = pl.ds(pl.multiple_of(g * 2 * DIM, 2 * DIM), 2 * DIM)
        return pltpu.make_async_remote_copy(
            src_ref=obuf.at[peer(d), :, cols], dst_ref=rbuf.at[d, :, cols],
            send_sem=s_out.at[d, g], recv_sem=r_out.at[d, g], device_id={"ka": peer(d)}, device_id_type=MESH,
        )

    def sum_copy(d):
        return pltpu.make_async_remote_copy(
            src_ref=sums.at[0], dst_ref=sums.at[d],
            send_sem=s_sum.at[d], recv_sem=r_sum.at[d], device_id={"ka": peer(d)}, device_id_type=MESH,
        )

    shifts = (1 - half, half - 1, half)
    early_cc = [(c, p2 + d) for d in shifts[:2]] + [(1 - c, p1 + d) for d in shifts[:2]]
    late = early_cc + [(c, p2 + half), (1 - c, p1 + half)]
    some = functools.reduce(jnp.logical_or, [seen(wrap(z + d)) for d in shifts])

    def finish(work, g, carry):
        pair = [2 * g, 2 * g + 1]
        run([(h, cc, wrap(b), size) for h in pair for cc, b, size in work])
        for h in pair:
            part = acc[h].T.astype(jnp.bfloat16)
            sums[0, h] = tot[h]
            cols = pl.ds(pl.multiple_of(h * DIM, DIM), DIM)
            for j in range(lanes):
                obuf[j, :, cols] = part[j * own : (j + 1) * own, :]
        for d in range(1, lanes):
            out_copy(d, g).start()
        return carry

    @pl.when(some)
    def _():
        last_other()
        last_mine()
        work = [(cc, b, chunk) for cc, b in late]
        lax.fori_loop(0, HEADS // 2, functools.partial(finish, work), 0)

    @pl.when(jnp.logical_not(some))
    def _():
        pl.when(c == 0)(last_other)
        pl.when(c == 1)(last_mine)
        work = [(1, y + d, chunk // 2) for d in shifts]
        lax.fori_loop(0, HEADS // 2, functools.partial(finish, work), 0)
        pl.when(c == 0)(last_mine)
        pl.when(c == 1)(last_other)

    met = [kv[cc, b, i, chunk:] for cc in range(2) for b in range(ring) for i in range(2)]
    met = functools.reduce(jnp.maximum, met).astype(jnp.float32)
    for i in range(2):
        row = met[i * EXTRA // 2 : i * EXTRA // 2 + 1, :]
        sums[0, HEADS + i] = jnp.concatenate([row] * (rows // LANES), axis=1)
    for d in range(1, lanes):
        sum_copy(d).start()
    for d in range(1, ring):
        one_copy(d, p1).wait_send()
    for i in range(2):
        sib_copy(0, c, p2, i).wait_send()
        for s in range(1, half):
            fwd_copy(s, p2 - s + 1, i).wait_send()
            bwd_copy(s, p2 + s - 1, i).wait_send()
            sib_copy(2 * s - 1, c, p2 - s, i).wait_send()
            sib_copy(2 * s, c, p2 + s, i).wait_send()
        cross_copy(c, p2 + (2 * i - 1) * (half - 1), i).wait_send()
    fwd_copy(half, p2 - half + 1, 0).wait_send()
    bwd_copy(half, p2 + half - 1, 1).wait_send()
    for d in range(1, lanes):
        sum_copy(d).wait_recv()
    whole = functools.reduce(jnp.add, [sums[d] for d in range(lanes)])
    share = [1.0 / whole[h] for h in range(HEADS)] + [jnp.zeros((LANES - HEADS, rows), jnp.float32)]
    mixing[...] = jnp.concatenate(share, axis=0).T
    met = functools.reduce(jnp.maximum, [sums[d] for d in range(lanes)])
    bound_ref[0] = jnp.max(met[HEADS] * met[HEADS + 1])
    mix = mixing[pl.ds(pl.multiple_of(x * own, own), own), :]
    for h in range(HEADS):
        cols = slice(h * DIM, (h + 1) * DIM)
        mixed = obuf[x, :, cols].astype(jnp.float32)
        for d in range(1, lanes):
            if h % 2 == 0:
                out_copy(d, h // 2).wait_recv()
            mixed += rbuf[d, :, cols].astype(jnp.float32)
        out_ref[:, cols] = (mixed * mix[:, h : h + 1]).astype(out_ref.dtype)

    for d in range(1, lanes):
        sum_copy(d).wait_send()
        for g in range(HEADS // 2):
            out_copy(d, g).wait_send()


def swift(ring, lanes, queries, keys, values, doc_lengths):
    rows, own = queries.shape[0], keys.shape[0]
    half = ring // 2
    chunk = ring * own
    vmem = pl.BlockSpec(memory_space=pltpu.VMEM)
    sems = pltpu.SemaphoreType.DMA
    parts = (lanes, own, HEADS * DIM)
    return pl.pallas_call(
        functools.partial(swift_kernel, ring, lanes),
        out_shape=(
            jax.ShapeDtypeStruct((own, HEADS * DIM), jnp.bfloat16),
            jax.ShapeDtypeStruct((1,), jnp.float32),
        ),
        in_specs=[pl.BlockSpec(memory_space=pltpu.HBM)] * 4,
        out_specs=(vmem, pl.BlockSpec(memory_space=pltpu.SMEM)),
        scratch_shapes=[
            pltpu.VMEM(queries.shape, jnp.bfloat16),
            pltpu.VMEM(keys.shape, jnp.bfloat16),
            pltpu.VMEM(values.shape, jnp.bfloat16),
            pltpu.SMEM(doc_lengths.shape, jnp.int32),
            pltpu.VMEM((ring, 2 * own + EXTRA, DIM), jnp.bfloat16),
            pltpu.VMEM((2, ring, 2, chunk + EXTRA, DIM), jnp.bfloat16),
            pltpu.VMEM((2, ring, chunk, LANES), jnp.bfloat16),
            pltpu.VMEM((HEADS, 2 * DIM, rows), jnp.bfloat16),
            pltpu.VMEM((HEADS, DIM, rows), jnp.float32),
            pltpu.VMEM((HEADS, 1, rows), jnp.float32),
            pltpu.VMEM(parts, jnp.bfloat16),
            pltpu.VMEM(parts, jnp.bfloat16),
            pltpu.VMEM((lanes, HEADS + 2, 1, rows), jnp.float32),
            pltpu.VMEM((rows, LANES), jnp.float32),
            sems((4,)),
            sems((ring - 1,)), sems((ring - 1,)),
            sems((half, 2)), sems((half, 2)), sems((half, 2)), sems((half, 2)),
            sems((2 * half - 1, 2)), sems((2 * half - 1, 2)), sems((2,)), sems((2,)),
            sems((lanes, HEADS // 2)), sems((lanes, HEADS // 2)),
            sems((lanes,)), sems((lanes,)),
        ],
        compiler_params=pltpu.CompilerParams(
            collective_id=0, has_side_effects=True, vmem_limit_bytes=63 * 1024 * 1024
        ),
        cost_estimate=pl.CostEstimate(flops=10**10, bytes_accessed=10**7, transcendentals=10**7),
        name="swift",
    )(queries, keys, values, doc_lengths)


def where(ring):
    me = lax.axis_index("pb")
    x = lax.axis_index("ka")
    c = lax.rem(me, 2)
    z = me // (2 * ring)
    y = lax.rem(me // 2, ring)
    return me, x, c, z, y


def greet(partners):
    barrier = pltpu.get_barrier_semaphore()
    for partner in partners:
        pl.semaphore_signal(barrier, inc=1, device_id=partner, device_id_type=MESH)
    return lambda: pl.semaphore_wait(barrier, len(partners))


def gather_kernel(
    ring, k_ref, v_ref, kv, stage,
    s_one, r_one, s_fwd, r_fwd, s_bwd, r_bwd, s_sib, r_sib,
):
    half = ring // 2
    own = k_ref.shape[0]
    me, x, c, z, y = where(ring)
    p1 = y * (1 - c) + z * c
    p2 = z * (1 - c) + y * c

    def wrap(value):
        return lax.rem(value + 2 * ring, ring)

    def device(first, second):
        zz, yy = place(c, wrap(first), wrap(second))
        return {"pb": (zz * ring + yy) * 2 + c}

    sibling = {"pb": me + 1 - 2 * c}
    partners = [device(p1 + d, p2) for d in range(1, ring)]
    partners += [device(p1, p2 + d) for d in ((1, ring - 1) if ring > 2 else (1,))]
    ready = greet(partners + [sibling])
    stage[p1, :, :DIM] = k_ref[...]
    stage[p1, :, DIM:] = v_ref[...]
    ready()

    def copy(ref, send, recv, to):
        return pltpu.make_async_remote_copy(
            src_ref=ref, dst_ref=ref, send_sem=send, recv_sem=recv, device_id=to, device_id_type=MESH
        )

    def one_copy(d, b1):
        return copy(stage.at[wrap(b1)], s_one.at[d - 1], r_one.at[d - 1], device(p1 + d, p2))

    def piece(cc, b, p):
        size = ring * own // 2
        return kv.at[cc, wrap(b), p // 2, pl.ds((p % 2) * size, size)]

    def fwd_copy(s, b, p):
        return copy(piece(c, b, p), s_fwd.at[s - 1, p], r_fwd.at[s - 1, p], device(p1, p2 + 1))

    def bwd_copy(s, b, p):
        return copy(piece(c, b, p), s_bwd.at[s - 1, p], r_bwd.at[s - 1, p], device(p1, p2 - 1))

    def sib_copy(n, cc, b, p):
        return copy(piece(cc, b, p), s_sib.at[n, p], r_sib.at[n, p], sibling)

    def travels(s, p):
        return s < half or (s == half and p < 2), s < half or (s == half and p >= 2)

    for d in sorted(range(1, ring), key=lambda d: abs(d - half)):
        one_copy(d, p1).start()
    for d in range(1, ring):
        one_copy(d, p1 - d).wait_recv()
    for n in range(ring):
        kv[c, p2, 0, n * own : (n + 1) * own] = stage[n, :, :DIM]
    side = LANES // own
    for n in range(ring // side):
        block = stage[n * side : (n + 1) * side, :, DIM:].reshape(LANES, DIM)
        kv[c, p2, 1, n * LANES : (n + 1) * LANES] = block.T
    for p in range(4):
        if travels(1, p)[0]:
            fwd_copy(1, p2, p).start()
        if travels(1, p)[1]:
            bwd_copy(1, p2, p).start()
    for p in range(4):
        sib_copy(0, c, p2, p).start()
    for s in range(1, half + 1):
        for p in range(4):
            if travels(s, p)[0]:
                fwd_copy(s, p2 - s, p).wait_recv()
                if travels(s + 1, p)[0]:
                    fwd_copy(s + 1, p2 - s, p).start()
            if travels(s, p)[1]:
                bwd_copy(s, p2 + s, p).wait_recv()
                if travels(s + 1, p)[1]:
                    bwd_copy(s + 1, p2 + s, p).start()
        for p in range(4):
            if travels(s, p)[0]:
                sib_copy(2 * s - 1, c, p2 - s, p).start()
            if travels(s, p)[1]:
                sib_copy(2 * s, c, p2 + s, p).start()
    for p in range(4):
        sib_copy(0, 1 - c, p1, p).wait_recv()
    for s in range(1, half + 1):
        for p in range(4):
            if travels(s, p)[0]:
                sib_copy(2 * s - 1, 1 - c, p1 - s, p).wait_recv()
            if travels(s, p)[1]:
                sib_copy(2 * s, 1 - c, p1 + s, p).wait_recv()
    for d in range(1, ring):
        one_copy(d, p1).wait_send()
    for p in range(4):
        sib_copy(0, c, p2, p).wait_send()
    for s in range(1, half + 1):
        for p in range(4):
            if travels(s, p)[0]:
                fwd_copy(s, p2 - s + 1, p).wait_send()
                sib_copy(2 * s - 1, c, p2 - s, p).wait_send()
            if travels(s, p)[1]:
                bwd_copy(s, p2 + s - 1, p).wait_send()
                sib_copy(2 * s, c, p2 + s, p).wait_send()


def attend_kernel(ring, lanes, q_ref, kv, lens, obuf, lbuf, kfeat, qcat, acc, tot, top):
    rows = q_ref.shape[0]
    own = rows // lanes
    chunk = ring * own
    plane = ring * 2 * rows
    me, x, c, z, y = where(ring)

    lane = lax.broadcasted_iota(jnp.int32, (1, LANES), 1)
    line = lax.broadcasted_iota(jnp.int32, (LANES, 1), 0)
    ends = jnp.zeros((1, LANES), jnp.int32)
    begins = jnp.zeros((1, LANES), jnp.int32)
    ends_down = jnp.zeros((LANES, 1), jnp.int32)
    begins_down = jnp.zeros((LANES, 1), jnp.int32)
    for j in range(DOCS):
        length = lens[j]
        ends += jnp.where(lane >= j, length, 0)
        begins += jnp.where(lane > j, length, 0)
        ends_down += jnp.where(line >= j, length, 0)
        begins_down += jnp.where(line > j, length, 0)
    tok = lax.broadcasted_iota(jnp.int32, (LANES, rows), 1)
    col = lax.broadcasted_iota(jnp.int32, (LANES, rows), 0)
    pos = me * rows + tok
    hidden = jnp.where((col < DOCS) & ((pos < begins_down) | (pos >= ends_down)), -MASK, 0.0)
    hidden = jnp.where(col == DOCS, -MASK, hidden)
    first = col - 2 * DOCS
    later = (first >= 0) & (first < own) & (tok < x * own + first)
    hidden = jnp.where(later, -MASK, hidden).astype(jnp.bfloat16)
    for h in range(HEADS):
        turned = q_ref[:, h * DIM : (h + 1) * DIM].T
        qcat[:DIM, h * rows : (h + 1) * rows] = turned
        qcat[DIM:, h * rows : (h + 1) * rows] = hidden
    acc[...] = jnp.zeros_like(acc)
    tot[...] = jnp.zeros_like(tot)
    top[...] = jnp.full_like(top, EMPTY)

    def features(n, carry):
        cc, b = n // ring, lax.rem(n, ring)
        inner = lax.broadcasted_iota(jnp.int32, (own, LANES), 0)
        lanes_of = lax.broadcasted_iota(jnp.int32, (own, LANES), 1)
        for a in range(ring):
            zz, yy = place(cc, a, b)
            block = (zz * ring + yy) * 2 + cc
            at = block * rows + x * own + inner
            mark = ((at >= begins) & (at < ends)).astype(jnp.float32)
            mark = jnp.where((lanes_of == DOCS) & (block > me), 1.0, mark)
            mark = jnp.where((lanes_of == inner + 2 * DOCS) & (block == me), 1.0, mark)
            kfeat[cc, b, a * own : (a + 1) * own, :] = mark.astype(jnp.bfloat16)
        return carry

    lax.fori_loop(0, 2 * ring, features, 0)
    ones = jnp.ones((16, chunk), jnp.bfloat16)

    def scores(h, cc, b):
        keys = jnp.concatenate([kv[cc, b, 0], kfeat[cc, b]], axis=1)
        return jnp.dot(keys, qcat[:, h * rows : (h + 1) * rows], preferred_element_type=jnp.float32)

    def weighted(cc, b, p):
        vals = jnp.concatenate([kv[cc, b, 1, n : n + LANES] for n in range(0, chunk, LANES)], axis=1)
        return jnp.dot(jnp.concatenate([vals, ones], axis=0), p, preferred_element_type=jnp.float32)

    def fold(h, cc, b, s):
        old = top[h : h + 1, :]
        new = jnp.maximum(old, jnp.max(s, axis=0, keepdims=True))
        both = weighted(cc, b, jnp.exp2((s - new) * FACTOR).astype(jnp.bfloat16))
        alpha = jnp.exp2((old - new) * FACTOR)
        acc[h] = acc[h] * alpha + both[:DIM]
        tot[h : h + 1, :] = tot[h : h + 1, :] * alpha + both[DIM : DIM + 1]
        top[h : h + 1, :] = new

    def sweep(fold):
        def body(n, carry):
            cc, b = n // ring, lax.rem(n, ring)
            seen = (b <= z) & ((b + 1) * plane > me * rows - (MOST - 1))

            @pl.when((cc == 1) | seen)
            def _():
                s = scores(0, cc, b)
                for h in range(HEADS):
                    after = scores(h + 1, cc, b) if h + 1 < HEADS else None
                    fold(h, cc, b, s)
                    s = after

            return carry

        lax.fori_loop(0, 2 * ring, body, 0)

    sweep(fold)
    logs = []
    for h in range(HEADS):
        total = tot[h : h + 1, :]
        some = total > 0.0
        safe = jnp.where(some, total, 1.0)
        part = (acc[h] / safe).T.astype(jnp.bfloat16)
        logs.append(jnp.where(some, top[h : h + 1, :] * FACTOR + jnp.log2(safe), NOTHING))
        for j in range(lanes):
            obuf[j, :, h * DIM : (h + 1) * DIM] = part[j * own : (j + 1) * own, :]
    lbuf[...] = jnp.concatenate(logs, axis=0)


def merge_kernel(lanes, obuf, lbuf, out_ref, rbuf, logs, mixing, relay, s_out, r_out, s_log, r_log, s_rel, r_rel):
    x = lax.axis_index("ka")
    own = out_ref.shape[0]
    rows = lbuf.shape[1]
    near = [d for d in range(1, lanes) if lanes != 4 or d != 2]

    def peer(d):
        return lax.rem(x + d, lanes)

    def copy(src, dst, send, recv, d):
        return pltpu.make_async_remote_copy(
            src_ref=src, dst_ref=dst, send_sem=send, recv_sem=recv, device_id={"ka": peer(d)}, device_id_type=MESH
        )

    def cols_of(g):
        return pl.ds(g * 2 * DIM, 2 * DIM)

    def out_copy(d, g):
        cols = cols_of(g)
        return copy(obuf.at[peer(d), :, cols], rbuf.at[d, :, cols], s_out.at[d, g], r_out.at[d, g], d)

    def way(g):
        return 1 if g < HEADS // 4 else 3

    def relay_copy(g):
        cols = cols_of(g)
        return copy(obuf.at[peer(2), :, cols], relay.at[:, cols], s_rel.at[g], r_rel.at[g], way(g))

    def onward_copy(g):
        cols = cols_of(g)
        return copy(relay.at[:, cols], rbuf.at[2, :, cols], s_out.at[2, g], r_out.at[2, g], way(g))

    def log_copy(d):
        return copy(lbuf, logs.at[d], s_log.at[d], r_log.at[d], d)

    greet([{"ka": peer(d)} for d in range(1, lanes)])()
    groups = range(HEADS // 2)
    for d in range(1, lanes):
        log_copy(d).start()
    if lanes == 4:
        for g in (0, 2, 1, 3):
            relay_copy(g).start()
    for g in groups:
        for d in near:
            out_copy(d, g).start()
    if lanes == 4:
        for g in (0, 2, 1, 3):
            relay_copy(g).wait_recv()
            onward_copy(g).start()
    for d in range(1, lanes):
        log_copy(d).wait_recv()
    sizes = [lbuf[...]] + [logs[d] for d in range(1, lanes)]
    highest = functools.reduce(jnp.maximum, sizes)
    shares = [jnp.exp2(size - highest) for size in sizes]
    whole = functools.reduce(jnp.add, shares)
    shares = [share / whole for share in shares]
    shares.append(jnp.zeros((LANES - HEADS * lanes, rows), jnp.float32))
    mixing[...] = jnp.concatenate(shares, axis=0).T
    mix = mixing[pl.ds(pl.multiple_of(x * own, own), own), :]
    for g in groups:
        for d in range(1, lanes):
            out_copy(d, g).wait_recv()
        for h in (2 * g, 2 * g + 1):
            cols = slice(h * DIM, (h + 1) * DIM)
            mixed = mix[:, h : h + 1] * obuf[x, :, cols].astype(jnp.float32)
            for d in range(1, lanes):
                at = d * HEADS + h
                mixed += mix[:, at : at + 1] * rbuf[d, :, cols].astype(jnp.float32)
            out_ref[:, cols] = mixed.astype(out_ref.dtype)
    for d in range(1, lanes):
        log_copy(d).wait_send()
    for g in groups:
        for d in near:
            out_copy(d, g).wait_send()
        if lanes == 4:
            relay_copy(g).wait_send()
            onward_copy(g).wait_send()


def steady(ring, lanes, queries, keys, values, doc_lengths):
    rows, own = queries.shape[0], keys.shape[0]
    half = ring // 2
    chunk = ring * own
    vmem = pl.BlockSpec(memory_space=pltpu.VMEM)
    sems = pltpu.SemaphoreType.DMA
    limit = 48 * 1024 * 1024
    kv = pl.pallas_call(
        functools.partial(gather_kernel, ring),
        out_shape=jax.ShapeDtypeStruct((2, ring, 2, chunk, DIM), jnp.bfloat16),
        in_specs=[vmem, vmem],
        out_specs=vmem,
        scratch_shapes=[
            pltpu.VMEM((ring, own, 2 * DIM), jnp.bfloat16),
            sems((ring - 1,)), sems((ring - 1,)),
            sems((half, 4)), sems((half, 4)), sems((half, 4)), sems((half, 4)),
            sems((2 * half + 1, 4)), sems((2 * half + 1, 4)),
        ],
        compiler_params=pltpu.CompilerParams(collective_id=1, has_side_effects=True, vmem_limit_bytes=limit),
        name="gather",
    )(keys, values)
    parts, logs = pl.pallas_call(
        functools.partial(attend_kernel, ring, lanes),
        out_shape=(
            jax.ShapeDtypeStruct((lanes, own, HEADS * DIM), jnp.bfloat16),
            jax.ShapeDtypeStruct((HEADS, rows), jnp.float32),
        ),
        in_specs=[vmem, vmem, pl.BlockSpec(memory_space=pltpu.SMEM)],
        out_specs=(vmem, vmem),
        scratch_shapes=[
            pltpu.VMEM((2, ring, chunk, LANES), jnp.bfloat16),
            pltpu.VMEM((2 * DIM, HEADS * rows), jnp.bfloat16),
            pltpu.VMEM((HEADS, DIM, rows), jnp.float32),
            pltpu.VMEM((HEADS, rows), jnp.float32),
            pltpu.VMEM((HEADS, rows), jnp.float32),
        ],
        compiler_params=pltpu.CompilerParams(vmem_limit_bytes=limit),
        name="attend",
    )(queries, kv, doc_lengths)
    return pl.pallas_call(
        functools.partial(merge_kernel, lanes),
        out_shape=jax.ShapeDtypeStruct((own, HEADS * DIM), jnp.bfloat16),
        in_specs=[vmem, vmem],
        out_specs=vmem,
        scratch_shapes=[
            pltpu.VMEM((lanes, own, HEADS * DIM), jnp.bfloat16),
            pltpu.VMEM((lanes, HEADS, rows), jnp.float32),
            pltpu.VMEM((rows, LANES), jnp.float32),
            pltpu.VMEM((own, HEADS * DIM), jnp.bfloat16),
            sems((lanes, HEADS // 2)), sems((lanes, HEADS // 2)),
            sems((lanes,)), sems((lanes,)),
            sems((HEADS // 2,)), sems((HEADS // 2,)),
        ],
        compiler_params=pltpu.CompilerParams(collective_id=2, has_side_effects=True, vmem_limit_bytes=limit),
        name="merge",
    )(parts, logs)


def per_device(ring, lanes, queries, keys, values, doc_lengths):
    args = (queries, keys, values, doc_lengths)
    out, bound = swift(ring, lanes, *args)
    fits = bound[0] <= (SAFE / FACTOR) ** 2
    return lax.cond(fits, lambda *_: out, functools.partial(steady, ring, lanes), *args)


def solution(mesh):
    ring = math.isqrt(mesh.shape["pb"] // 2)
    return jax.shard_map(
        functools.partial(per_device, ring, mesh.shape["ka"]),
        mesh=mesh,
        in_specs=(P("pb", None), P(("pb", "ka"), None), P(("pb", "ka"), None), P()),
        out_specs=P(("pb", "ka"), None),
        check_vma=False,
    )
```

```python
import functools
import math

import jax
import jax.numpy as jnp
from jax import lax
from jax.experimental import pallas as pl
from jax.experimental.pallas import tpu as pltpu
from jax.sharding import PartitionSpec as P

HEADS = 8
DIM = 128
DOCS = 8
MOST = 24576
LANES = 128
FACTOR = math.log2(math.e) / math.sqrt(DIM)
MASK = 131072.0
EMPTY = -65536.0
NOTHING = -1e30
EXTRA = 16
SAFE = 100.0
MESH = pl.DeviceIdType.MESH


def place(c, first, second):
    z = second * (1 - c) + first * c
    y = first * (1 - c) + second * c
    return z, y


def swift_kernel(
    ring, lanes, q_hbm, k_hbm, v_hbm, len_hbm, out_ref, bound_ref,
    q_in, k_in, v_in, lens, stage, kv, kfeat, qcat, acc, tot, obuf, rbuf, sums, mixing,
    s_in, s_one, r_one, s_fwd, r_fwd, s_bwd, r_bwd, s_sib, r_sib, s_cross, r_cross, s_out, r_out, s_sum, r_sum,
):
    half = ring // 2
    rows = q_in.shape[0]
    own = k_in.shape[0]
    chunk = ring * own
    plane = ring * 2 * rows
    me = lax.axis_index("pb")
    x = lax.axis_index("ka")
    c = lax.rem(me, 2)
    z = me // (2 * ring)
    y = lax.rem(me // 2, ring)
    p1 = y * (1 - c) + z * c
    p2 = z * (1 - c) + y * c

    def wrap(value):
        return lax.rem(value + 2 * ring, ring)

    def device(first, second, core=c):
        zz, yy = place(c, wrap(first), wrap(second))
        return {"pb": (zz * ring + yy) * 2 + core}

    sibling = {"pb": me + 1 - 2 * c}

    barrier = pltpu.get_barrier_semaphore()
    partners = [device(p1 + d, p2) for d in range(1, ring)]
    partners += [device(p1, p2 + d, core) for d in (1, -1) for core in (c, 1 - c)]
    partners += [device(p1 + d, p2, 1 - c) for d in (1, -1)]
    partners += [sibling] + [{"ka": lax.rem(x + d, lanes)} for d in range(1, lanes)]
    for partner in partners:
        pl.semaphore_signal(barrier, inc=1, device_id=partner, device_id_type=MESH)
    moves = [
        pltpu.make_async_copy(src, dst, s_in.at[n])
        for n, (src, dst) in enumerate(((k_hbm, k_in), (v_hbm, v_in), (len_hbm, lens), (q_hbm, q_in)))
    ]
    for move in moves:
        move.start()
    moves[0].wait()
    moves[1].wait()
    stage[p1, :own] = k_in[...]
    stage[p1, own : 2 * own] = v_in[...]
    wide = k_in[...].astype(jnp.float32)
    longest = jnp.max(jnp.sum(wide * wide, axis=1, keepdims=True), axis=0, keepdims=True)
    k_most = longest
    moves[3].wait()
    longest = jnp.zeros((rows, 1), jnp.float32)
    for h in range(HEADS):
        wide = q_in[:, h * DIM : (h + 1) * DIM].astype(jnp.float32)
        longest = jnp.maximum(longest, jnp.sum(wide * wide, axis=1, keepdims=True))
    longest = jnp.max(longest, axis=0, keepdims=True)
    upper = lax.broadcasted_iota(jnp.int32, (EXTRA, DIM), 0) < EXTRA // 2
    stage[p1, 2 * own :] = (jnp.where(upper, k_most, longest) * 1.01).astype(jnp.bfloat16)
    pl.semaphore_wait(barrier, len(partners))

    def copy(ref, send, recv, where):
        return pltpu.make_async_remote_copy(
            src_ref=ref, dst_ref=ref, send_sem=send, recv_sem=recv, device_id=where, device_id_type=MESH
        )

    def one_copy(d, b1):
        return copy(stage.at[wrap(b1)], s_one.at[d - 1], r_one.at[d - 1], device(p1 + d, p2))

    def piece(cc, b, i):
        return kv.at[cc, wrap(b), i]

    def fwd_copy(s, b, i):
        return copy(piece(c, b, i), s_fwd.at[s - 1, i], r_fwd.at[s - 1, i], device(p1, p2 + 1))

    def bwd_copy(s, b, i):
        return copy(piece(c, b, i), s_bwd.at[s - 1, i], r_bwd.at[s - 1, i], device(p1, p2 - 1))

    def sib_copy(k, cc, b, i):
        return copy(piece(cc, b, i), s_sib.at[k, i], r_sib.at[k, i], sibling)

    def cross_copy(cc, b, i):
        return copy(piece(cc, b, i), s_cross.at[i], r_cross.at[i], device(p1, p2 + 1 - 2 * i, 1 - c))

    def pass_on(s):
        for i in range(2):
            fwd_copy(s, p2 - s, i).wait_recv()
            if s + 1 < half or i == 0:
                fwd_copy(s + 1, p2 - s, i).start()
            bwd_copy(s, p2 + s, i).wait_recv()
            if s + 1 < half or i == 1:
                bwd_copy(s + 1, p2 + s, i).start()
            if s + 1 == half:
                cross_copy(c, p2 - s + 2 * i * s, i).start()
        for i in range(2):
            sib_copy(2 * s - 1, c, p2 - s, i).start()
            sib_copy(2 * s, c, p2 + s, i).start()

    def sib_arrived(s):
        for i in range(2):
            sib_copy(2 * s - 1, 1 - c, p1 - s, i).wait_recv()
            sib_copy(2 * s, 1 - c, p1 + s, i).wait_recv()

    for d in sorted(range(1, ring), key=lambda d: abs(d - half)):
        one_copy(d, p1).start()
    moves[2].wait()

    lane = lax.broadcasted_iota(jnp.int32, (1, LANES), 1)
    line = lax.broadcasted_iota(jnp.int32, (LANES, 1), 0)
    ends = jnp.zeros((1, LANES), jnp.int32)
    begins = jnp.zeros((1, LANES), jnp.int32)
    ends_down = jnp.zeros((LANES, 1), jnp.int32)
    begins_down = jnp.zeros((LANES, 1), jnp.int32)
    for j in range(DOCS):
        length = lens[j]
        ends += jnp.where(lane >= j, length, 0)
        begins += jnp.where(lane > j, length, 0)
        ends_down += jnp.where(line >= j, length, 0)
        begins_down += jnp.where(line > j, length, 0)
    tok = lax.broadcasted_iota(jnp.int32, (LANES, rows), 1)
    col = lax.broadcasted_iota(jnp.int32, (LANES, rows), 0)
    pos = me * rows + tok
    hidden = jnp.where((col < DOCS) & ((pos < begins_down) | (pos >= ends_down)), -MASK, 0.0)
    hidden = jnp.where(col == DOCS, -MASK, hidden)
    first = col - 2 * DOCS
    later = (first >= 0) & (first < own) & (tok < x * own + first)
    hidden = jnp.where(later, -MASK, hidden).astype(jnp.bfloat16)
    for h in range(HEADS):
        at = slice(h % 2 * rows, (h % 2 + 1) * rows)
        qcat[h // 2, :DIM, at] = q_in[:, h * DIM : (h + 1) * DIM].T
        qcat[h // 2, DIM:, at] = hidden
    acc[...] = jnp.zeros_like(acc)
    tot[...] = jnp.zeros_like(tot)

    def features(n, carry):
        cc, b = n // ring, lax.rem(n, ring)
        inner = lax.broadcasted_iota(jnp.int32, (own, LANES), 0)
        lanes_of = lax.broadcasted_iota(jnp.int32, (own, LANES), 1)
        for a in range(ring):
            zz, yy = place(cc, a, b)
            block = (zz * ring + yy) * 2 + cc
            at = block * rows + x * own + inner
            mark = ((at >= begins) & (at < ends)).astype(jnp.float32)
            mark = jnp.where((lanes_of == DOCS) & (block > me), 1.0, mark)
            mark = jnp.where((lanes_of == inner + 2 * DOCS) & (block == me), 1.0, mark)
            kfeat[cc, b, a * own : (a + 1) * own, :] = mark.astype(jnp.bfloat16)
        return carry

    lax.fori_loop(0, 2 * ring, features, 0)

    ones = jnp.ones((16, chunk), jnp.bfloat16)

    def scores(g, cc, b, size):
        keys = jnp.concatenate([kv[cc, b, 0, :size], kfeat[cc, b, :size]], axis=1)
        return jnp.dot(keys, qcat[g], preferred_element_type=jnp.float32)

    def fold(g, cc, b, size, s):
        p = jnp.exp2(s * FACTOR).astype(jnp.bfloat16)
        vals = jnp.concatenate([kv[cc, b, 1, n : n + LANES] for n in range(0, size, LANES)], axis=1)
        both = jnp.dot(jnp.concatenate([vals, ones[:, :size]], axis=0), p, preferred_element_type=jnp.float32)
        acc[g] += both[:DIM]
        tot[g] += both[DIM : DIM + 1]

    def run(work):
        s = scores(*work[0])
        for n, item in enumerate(work):
            after = scores(*work[n + 1]) if n + 1 < len(work) else None
            fold(*item, s)
            s = after

    for d in range(1, ring):
        one_copy(d, p1 - d).wait_recv()
    for n in range(ring):
        kv[c, p2, 0, n * own : (n + 1) * own] = stage[n, :own]
    largest = functools.reduce(jnp.maximum, [stage[n, 2 * own :] for n in range(ring)])
    for i in range(2):
        kv[c, p2, i, chunk:] = largest
    fwd_copy(1, p2, 0).start()
    bwd_copy(1, p2, 0).start()
    side = LANES // own
    for n in range(ring // side):
        block = stage[n * side : (n + 1) * side, own : 2 * own].reshape(LANES, DIM)
        kv[c, p2, 1, n * LANES : (n + 1) * LANES] = block.T
    fwd_copy(1, p2, 1).start()
    bwd_copy(1, p2, 1).start()
    for i in range(2):
        sib_copy(0, c, p2, i).start()

    def seen(b):
        return (b <= z) & ((b + 1) * plane > me * rows - (MOST - 1))

    def unit(u, carry):
        v = jnp.maximum(u - 2, 0)
        s = v // 4 + 1
        r = lax.rem(v, 4)
        early = u < 2
        mine = jnp.where(early, u == 0, r < 2)
        cc = jnp.where(mine, c, 1 - c)
        shift = jnp.where(early, 0, (2 * lax.rem(r, 2) - 1) * s)
        b = wrap(jnp.where(mine, p2, p1) + shift)

        @pl.when(u == 1)
        def _():
            for i in range(2):
                sib_copy(0, 1 - c, p1, i).wait_recv()

        @pl.when((u >= 2) & (r == 2))
        def _():
            sib_arrived(s)

        @pl.when((cc == 1) | seen(b))
        def _():
            run([(g, cc, b, chunk) for g in range(HEADS // 2)])

        for step, after in ((1, 0), (2, 3), (3, 6)):
            if step < half:
                pl.when(u == after)(functools.partial(pass_on, step))
        return carry

    lax.fori_loop(0, 2 + 4 * (half - 2), unit, 0)

    def last_mine():
        fwd_copy(half, p2 - half, 0).wait_recv()
        bwd_copy(half, p2 + half, 1).wait_recv()

    def last_sib():
        sib_arrived(half - 1)

    def last_cross():
        cross_copy(1 - c, p1 - half, 0).wait_recv()
        cross_copy(1 - c, p1 + half, 1).wait_recv()

    def peer(d):
        return lax.rem(x + d, lanes)

    def out_copy(d, g):
        cols = pl.ds(pl.multiple_of(g * 2 * DIM, 2 * DIM), 2 * DIM)
        return pltpu.make_async_remote_copy(
            src_ref=obuf.at[peer(d), :, cols], dst_ref=rbuf.at[d, :, cols],
            send_sem=s_out.at[d, g], recv_sem=r_out.at[d, g], device_id={"ka": peer(d)}, device_id_type=MESH,
        )

    def sum_copy(d):
        return pltpu.make_async_remote_copy(
            src_ref=sums.at[0], dst_ref=sums.at[d],
            send_sem=s_sum.at[d], recv_sem=r_sum.at[d], device_id={"ka": peer(d)}, device_id_type=MESH,
        )

    shifts = (1 - half, half - 1, half)
    early_cc = [(c, p2 + d) for d in shifts[:2]] + [(1 - c, p1 + d) for d in shifts[:2]]
    late = early_cc + [(c, p2 + half), (1 - c, p1 + half)]

    def finish(work, g, carry):
        run([(g, cc, wrap(b), size) for cc, b, size in work])
        for n in range(2):
            h = 2 * g + n
            at = slice(n * rows, (n + 1) * rows)
            part = acc[g, :, at].T.astype(jnp.bfloat16)
            sums[0, h] = tot[g, :, at]
            cols = pl.ds(pl.multiple_of(h * DIM, DIM), DIM)
            for j in range(lanes):
                obuf[j, :, cols] = part[j * own : (j + 1) * own, :]
        for d in range(1, lanes):
            out_copy(d, g).start()
        return carry

    def finish_all(work):
        lax.fori_loop(0, HEADS // 2, functools.partial(finish, work), 0)

    @pl.when(z >= half)
    def _():
        last_sib()
        last_cross()
        last_mine()
        finish_all([(cc, b, chunk) for cc, b in late])

    halves = [(1, y + d, chunk // 2) for d in shifts]

    @pl.when(z == half - 1)
    def _():
        last_sib()
        pl.when(c == 0)(last_cross)
        pl.when(c == 1)(last_mine)
        finish_all([(0, 0, chunk)] + halves)
        pl.when(c == 0)(last_mine)
        pl.when(c == 1)(last_cross)

    @pl.when(z < half - 1)
    def _():
        @pl.when(c == 0)
        def _():
            last_sib()
            last_cross()

        pl.when(c == 1)(last_mine)
        finish_all(halves)
        pl.when(c == 0)(last_mine)

        @pl.when(c == 1)
        def _():
            last_sib()
            last_cross()

    met = [kv[cc, b, i, chunk:] for cc in range(2) for b in range(ring) for i in range(2)]
    met = functools.reduce(jnp.maximum, met).astype(jnp.float32)
    for i in range(2):
        row = met[i * EXTRA // 2 : i * EXTRA // 2 + 1, :]
        sums[0, HEADS + i] = jnp.concatenate([row] * (rows // LANES), axis=1)
    for d in range(1, lanes):
        sum_copy(d).start()
    for d in range(1, ring):
        one_copy(d, p1).wait_send()
    for i in range(2):
        sib_copy(0, c, p2, i).wait_send()
        for s in range(1, half):
            fwd_copy(s, p2 - s + 1, i).wait_send()
            bwd_copy(s, p2 + s - 1, i).wait_send()
            sib_copy(2 * s - 1, c, p2 - s, i).wait_send()
            sib_copy(2 * s, c, p2 + s, i).wait_send()
        cross_copy(c, p2 + (2 * i - 1) * (half - 1), i).wait_send()
    fwd_copy(half, p2 - half + 1, 0).wait_send()
    bwd_copy(half, p2 + half - 1, 1).wait_send()
    for d in range(1, lanes):
        sum_copy(d).wait_recv()
    whole = functools.reduce(jnp.add, [sums[d] for d in range(lanes)])
    share = [1.0 / whole[h] for h in range(HEADS)] + [jnp.zeros((LANES - HEADS, rows), jnp.float32)]
    mixing[...] = jnp.concatenate(share, axis=0).T
    met = functools.reduce(jnp.maximum, [sums[d] for d in range(lanes)])
    bound_ref[0] = jnp.max(met[HEADS] * met[HEADS + 1])
    mix = mixing[pl.ds(pl.multiple_of(x * own, own), own), :]
    for h in range(HEADS):
        cols = slice(h * DIM, (h + 1) * DIM)
        mixed = obuf[x, :, cols].astype(jnp.float32)
        for d in range(1, lanes):
            if h % 2 == 0:
                out_copy(d, h // 2).wait_recv()
            mixed += rbuf[d, :, cols].astype(jnp.float32)
        out_ref[:, cols] = (mixed * mix[:, h : h + 1]).astype(out_ref.dtype)

    for d in range(1, lanes):
        sum_copy(d).wait_send()
        for g in range(HEADS // 2):
            out_copy(d, g).wait_send()


def swift(ring, lanes, queries, keys, values, doc_lengths):
    rows, own = queries.shape[0], keys.shape[0]
    half = ring // 2
    chunk = ring * own
    vmem = pl.BlockSpec(memory_space=pltpu.VMEM)
    sems = pltpu.SemaphoreType.DMA
    parts = (lanes, own, HEADS * DIM)
    return pl.pallas_call(
        functools.partial(swift_kernel, ring, lanes),
        out_shape=(
            jax.ShapeDtypeStruct((own, HEADS * DIM), jnp.bfloat16),
            jax.ShapeDtypeStruct((1,), jnp.float32),
        ),
        in_specs=[pl.BlockSpec(memory_space=pltpu.HBM)] * 4,
        out_specs=(vmem, pl.BlockSpec(memory_space=pltpu.SMEM)),
        scratch_shapes=[
            pltpu.VMEM(queries.shape, jnp.bfloat16),
            pltpu.VMEM(keys.shape, jnp.bfloat16),
            pltpu.VMEM(values.shape, jnp.bfloat16),
            pltpu.SMEM(doc_lengths.shape, jnp.int32),
            pltpu.VMEM((ring, 2 * own + EXTRA, DIM), jnp.bfloat16),
            pltpu.VMEM((2, ring, 2, chunk + EXTRA, DIM), jnp.bfloat16),
            pltpu.VMEM((2, ring, chunk, LANES), jnp.bfloat16),
            pltpu.VMEM((HEADS // 2, 2 * DIM, 2 * rows), jnp.bfloat16),
            pltpu.VMEM((HEADS // 2, DIM, 2 * rows), jnp.float32),
            pltpu.VMEM((HEADS // 2, 1, 2 * rows), jnp.float32),
            pltpu.VMEM(parts, jnp.bfloat16),
            pltpu.VMEM(parts, jnp.bfloat16),
            pltpu.VMEM((lanes, HEADS + 2, 1, rows), jnp.float32),
            pltpu.VMEM((rows, LANES), jnp.float32),
            sems((4,)),
            sems((ring - 1,)), sems((ring - 1,)),
            sems((half, 2)), sems((half, 2)), sems((half, 2)), sems((half, 2)),
            sems((2 * half - 1, 2)), sems((2 * half - 1, 2)), sems((2,)), sems((2,)),
            sems((lanes, HEADS // 2)), sems((lanes, HEADS // 2)),
            sems((lanes,)), sems((lanes,)),
        ],
        compiler_params=pltpu.CompilerParams(
            collective_id=0, has_side_effects=True, vmem_limit_bytes=63 * 1024 * 1024
        ),
        cost_estimate=pl.CostEstimate(flops=10**10, bytes_accessed=10**7, transcendentals=10**7),
        name="swift",
    )(queries, keys, values, doc_lengths)


def where(ring):
    me = lax.axis_index("pb")
    x = lax.axis_index("ka")
    c = lax.rem(me, 2)
    z = me // (2 * ring)
    y = lax.rem(me // 2, ring)
    return me, x, c, z, y


def greet(partners):
    barrier = pltpu.get_barrier_semaphore()
    for partner in partners:
        pl.semaphore_signal(barrier, inc=1, device_id=partner, device_id_type=MESH)
    return lambda: pl.semaphore_wait(barrier, len(partners))


def gather_kernel(
    ring, k_ref, v_ref, kv, stage,
    s_one, r_one, s_fwd, r_fwd, s_bwd, r_bwd, s_sib, r_sib,
):
    half = ring // 2
    own = k_ref.shape[0]
    me, x, c, z, y = where(ring)
    p1 = y * (1 - c) + z * c
    p2 = z * (1 - c) + y * c

    def wrap(value):
        return lax.rem(value + 2 * ring, ring)

    def device(first, second):
        zz, yy = place(c, wrap(first), wrap(second))
        return {"pb": (zz * ring + yy) * 2 + c}

    sibling = {"pb": me + 1 - 2 * c}
    partners = [device(p1 + d, p2) for d in range(1, ring)]
    partners += [device(p1, p2 + d) for d in ((1, ring - 1) if ring > 2 else (1,))]
    ready = greet(partners + [sibling])
    stage[p1, :, :DIM] = k_ref[...]
    stage[p1, :, DIM:] = v_ref[...]
    ready()

    def copy(ref, send, recv, to):
        return pltpu.make_async_remote_copy(
            src_ref=ref, dst_ref=ref, send_sem=send, recv_sem=recv, device_id=to, device_id_type=MESH
        )

    def one_copy(d, b1):
        return copy(stage.at[wrap(b1)], s_one.at[d - 1], r_one.at[d - 1], device(p1 + d, p2))

    def piece(cc, b, p):
        size = ring * own // 2
        return kv.at[cc, wrap(b), p // 2, pl.ds((p % 2) * size, size)]

    def fwd_copy(s, b, p):
        return copy(piece(c, b, p), s_fwd.at[s - 1, p], r_fwd.at[s - 1, p], device(p1, p2 + 1))

    def bwd_copy(s, b, p):
        return copy(piece(c, b, p), s_bwd.at[s - 1, p], r_bwd.at[s - 1, p], device(p1, p2 - 1))

    def sib_copy(n, cc, b, p):
        return copy(piece(cc, b, p), s_sib.at[n, p], r_sib.at[n, p], sibling)

    def travels(s, p):
        return s < half or (s == half and p < 2), s < half or (s == half and p >= 2)

    for d in sorted(range(1, ring), key=lambda d: abs(d - half)):
        one_copy(d, p1).start()
    for d in range(1, ring):
        one_copy(d, p1 - d).wait_recv()
    for n in range(ring):
        kv[c, p2, 0, n * own : (n + 1) * own] = stage[n, :, :DIM]
    side = LANES // own
    for n in range(ring // side):
        block = stage[n * side : (n + 1) * side, :, DIM:].reshape(LANES, DIM)
        kv[c, p2, 1, n * LANES : (n + 1) * LANES] = block.T
    for p in range(4):
        if travels(1, p)[0]:
            fwd_copy(1, p2, p).start()
        if travels(1, p)[1]:
            bwd_copy(1, p2, p).start()
    for p in range(4):
        sib_copy(0, c, p2, p).start()
    for s in range(1, half + 1):
        for p in range(4):
            if travels(s, p)[0]:
                fwd_copy(s, p2 - s, p).wait_recv()
                if travels(s + 1, p)[0]:
                    fwd_copy(s + 1, p2 - s, p).start()
            if travels(s, p)[1]:
                bwd_copy(s, p2 + s, p).wait_recv()
                if travels(s + 1, p)[1]:
                    bwd_copy(s + 1, p2 + s, p).start()
        for p in range(4):
            if travels(s, p)[0]:
                sib_copy(2 * s - 1, c, p2 - s, p).start()
            if travels(s, p)[1]:
                sib_copy(2 * s, c, p2 + s, p).start()
    for p in range(4):
        sib_copy(0, 1 - c, p1, p).wait_recv()
    for s in range(1, half + 1):
        for p in range(4):
            if travels(s, p)[0]:
                sib_copy(2 * s - 1, 1 - c, p1 - s, p).wait_recv()
            if travels(s, p)[1]:
                sib_copy(2 * s, 1 - c, p1 + s, p).wait_recv()
    for d in range(1, ring):
        one_copy(d, p1).wait_send()
    for p in range(4):
        sib_copy(0, c, p2, p).wait_send()
    for s in range(1, half + 1):
        for p in range(4):
            if travels(s, p)[0]:
                fwd_copy(s, p2 - s + 1, p).wait_send()
                sib_copy(2 * s - 1, c, p2 - s, p).wait_send()
            if travels(s, p)[1]:
                bwd_copy(s, p2 + s - 1, p).wait_send()
                sib_copy(2 * s, c, p2 + s, p).wait_send()


def attend_kernel(ring, lanes, q_ref, kv, lens, obuf, lbuf, kfeat, qcat, acc, tot, top):
    rows = q_ref.shape[0]
    own = rows // lanes
    chunk = ring * own
    plane = ring * 2 * rows
    me, x, c, z, y = where(ring)

    lane = lax.broadcasted_iota(jnp.int32, (1, LANES), 1)
    line = lax.broadcasted_iota(jnp.int32, (LANES, 1), 0)
    ends = jnp.zeros((1, LANES), jnp.int32)
    begins = jnp.zeros((1, LANES), jnp.int32)
    ends_down = jnp.zeros((LANES, 1), jnp.int32)
    begins_down = jnp.zeros((LANES, 1), jnp.int32)
    for j in range(DOCS):
        length = lens[j]
        ends += jnp.where(lane >= j, length, 0)
        begins += jnp.where(lane > j, length, 0)
        ends_down += jnp.where(line >= j, length, 0)
        begins_down += jnp.where(line > j, length, 0)
    tok = lax.broadcasted_iota(jnp.int32, (LANES, rows), 1)
    col = lax.broadcasted_iota(jnp.int32, (LANES, rows), 0)
    pos = me * rows + tok
    hidden = jnp.where((col < DOCS) & ((pos < begins_down) | (pos >= ends_down)), -MASK, 0.0)
    hidden = jnp.where(col == DOCS, -MASK, hidden)
    first = col - 2 * DOCS
    later = (first >= 0) & (first < own) & (tok < x * own + first)
    hidden = jnp.where(later, -MASK, hidden).astype(jnp.bfloat16)
    for h in range(HEADS):
        turned = q_ref[:, h * DIM : (h + 1) * DIM].T
        qcat[:DIM, h * rows : (h + 1) * rows] = turned
        qcat[DIM:, h * rows : (h + 1) * rows] = hidden
    acc[...] = jnp.zeros_like(acc)
    tot[...] = jnp.zeros_like(tot)
    top[...] = jnp.full_like(top, EMPTY)

    def features(n, carry):
        cc, b = n // ring, lax.rem(n, ring)
        inner = lax.broadcasted_iota(jnp.int32, (own, LANES), 0)
        lanes_of = lax.broadcasted_iota(jnp.int32, (own, LANES), 1)
        for a in range(ring):
            zz, yy = place(cc, a, b)
            block = (zz * ring + yy) * 2 + cc
            at = block * rows + x * own + inner
            mark = ((at >= begins) & (at < ends)).astype(jnp.float32)
            mark = jnp.where((lanes_of == DOCS) & (block > me), 1.0, mark)
            mark = jnp.where((lanes_of == inner + 2 * DOCS) & (block == me), 1.0, mark)
            kfeat[cc, b, a * own : (a + 1) * own, :] = mark.astype(jnp.bfloat16)
        return carry

    lax.fori_loop(0, 2 * ring, features, 0)
    ones = jnp.ones((16, chunk), jnp.bfloat16)

    def scores(h, cc, b):
        keys = jnp.concatenate([kv[cc, b, 0], kfeat[cc, b]], axis=1)
        return jnp.dot(keys, qcat[:, h * rows : (h + 1) * rows], preferred_element_type=jnp.float32)

    def weighted(cc, b, p):
        vals = jnp.concatenate([kv[cc, b, 1, n : n + LANES] for n in range(0, chunk, LANES)], axis=1)
        return jnp.dot(jnp.concatenate([vals, ones], axis=0), p, preferred_element_type=jnp.float32)

    def fold(h, cc, b, s):
        old = top[h : h + 1, :]
        new = jnp.maximum(old, jnp.max(s, axis=0, keepdims=True))
        both = weighted(cc, b, jnp.exp2((s - new) * FACTOR).astype(jnp.bfloat16))
        alpha = jnp.exp2((old - new) * FACTOR)
        acc[h] = acc[h] * alpha + both[:DIM]
        tot[h : h + 1, :] = tot[h : h + 1, :] * alpha + both[DIM : DIM + 1]
        top[h : h + 1, :] = new

    def sweep(fold):
        def body(n, carry):
            cc, b = n // ring, lax.rem(n, ring)
            seen = (b <= z) & ((b + 1) * plane > me * rows - (MOST - 1))

            @pl.when((cc == 1) | seen)
            def _():
                s = scores(0, cc, b)
                for h in range(HEADS):
                    after = scores(h + 1, cc, b) if h + 1 < HEADS else None
                    fold(h, cc, b, s)
                    s = after

            return carry

        lax.fori_loop(0, 2 * ring, body, 0)

    sweep(fold)
    logs = []
    for h in range(HEADS):
        total = tot[h : h + 1, :]
        some = total > 0.0
        safe = jnp.where(some, total, 1.0)
        part = (acc[h] / safe).T.astype(jnp.bfloat16)
        logs.append(jnp.where(some, top[h : h + 1, :] * FACTOR + jnp.log2(safe), NOTHING))
        for j in range(lanes):
            obuf[j, :, h * DIM : (h + 1) * DIM] = part[j * own : (j + 1) * own, :]
    lbuf[...] = jnp.concatenate(logs, axis=0)


def merge_kernel(lanes, obuf, lbuf, out_ref, rbuf, logs, mixing, relay, s_out, r_out, s_log, r_log, s_rel, r_rel):
    x = lax.axis_index("ka")
    own = out_ref.shape[0]
    rows = lbuf.shape[1]
    near = [d for d in range(1, lanes) if lanes != 4 or d != 2]

    def peer(d):
        return lax.rem(x + d, lanes)

    def copy(src, dst, send, recv, d):
        return pltpu.make_async_remote_copy(
            src_ref=src, dst_ref=dst, send_sem=send, recv_sem=recv, device_id={"ka": peer(d)}, device_id_type=MESH
        )

    def cols_of(g):
        return pl.ds(g * 2 * DIM, 2 * DIM)

    def out_copy(d, g):
        cols = cols_of(g)
        return copy(obuf.at[peer(d), :, cols], rbuf.at[d, :, cols], s_out.at[d, g], r_out.at[d, g], d)

    def way(g):
        return 1 if g < HEADS // 4 else 3

    def relay_copy(g):
        cols = cols_of(g)
        return copy(obuf.at[peer(2), :, cols], relay.at[:, cols], s_rel.at[g], r_rel.at[g], way(g))

    def onward_copy(g):
        cols = cols_of(g)
        return copy(relay.at[:, cols], rbuf.at[2, :, cols], s_out.at[2, g], r_out.at[2, g], way(g))

    def log_copy(d):
        return copy(lbuf, logs.at[d], s_log.at[d], r_log.at[d], d)

    greet([{"ka": peer(d)} for d in range(1, lanes)])()
    groups = range(HEADS // 2)
    for d in range(1, lanes):
        log_copy(d).start()
    if lanes == 4:
        for g in (0, 2, 1, 3):
            relay_copy(g).start()
    for g in groups:
        for d in near:
            out_copy(d, g).start()
    if lanes == 4:
        for g in (0, 2, 1, 3):
            relay_copy(g).wait_recv()
            onward_copy(g).start()
    for d in range(1, lanes):
        log_copy(d).wait_recv()
    sizes = [lbuf[...]] + [logs[d] for d in range(1, lanes)]
    highest = functools.reduce(jnp.maximum, sizes)
    shares = [jnp.exp2(size - highest) for size in sizes]
    whole = functools.reduce(jnp.add, shares)
    shares = [share / whole for share in shares]
    shares.append(jnp.zeros((LANES - HEADS * lanes, rows), jnp.float32))
    mixing[...] = jnp.concatenate(shares, axis=0).T
    mix = mixing[pl.ds(pl.multiple_of(x * own, own), own), :]
    for g in groups:
        for d in range(1, lanes):
            out_copy(d, g).wait_recv()
        for h in (2 * g, 2 * g + 1):
            cols = slice(h * DIM, (h + 1) * DIM)
            mixed = mix[:, h : h + 1] * obuf[x, :, cols].astype(jnp.float32)
            for d in range(1, lanes):
                at = d * HEADS + h
                mixed += mix[:, at : at + 1] * rbuf[d, :, cols].astype(jnp.float32)
            out_ref[:, cols] = mixed.astype(out_ref.dtype)
    for d in range(1, lanes):
        log_copy(d).wait_send()
    for g in groups:
        for d in near:
            out_copy(d, g).wait_send()
        if lanes == 4:
            relay_copy(g).wait_send()
            onward_copy(g).wait_send()


def steady(ring, lanes, queries, keys, values, doc_lengths):
    rows, own = queries.shape[0], keys.shape[0]
    half = ring // 2
    chunk = ring * own
    vmem = pl.BlockSpec(memory_space=pltpu.VMEM)
    sems = pltpu.SemaphoreType.DMA
    limit = 48 * 1024 * 1024
    kv = pl.pallas_call(
        functools.partial(gather_kernel, ring),
        out_shape=jax.ShapeDtypeStruct((2, ring, 2, chunk, DIM), jnp.bfloat16),
        in_specs=[vmem, vmem],
        out_specs=vmem,
        scratch_shapes=[
            pltpu.VMEM((ring, own, 2 * DIM), jnp.bfloat16),
            sems((ring - 1,)), sems((ring - 1,)),
            sems((half, 4)), sems((half, 4)), sems((half, 4)), sems((half, 4)),
            sems((2 * half + 1, 4)), sems((2 * half + 1, 4)),
        ],
        compiler_params=pltpu.CompilerParams(collective_id=1, has_side_effects=True, vmem_limit_bytes=limit),
        name="gather",
    )(keys, values)
    parts, logs = pl.pallas_call(
        functools.partial(attend_kernel, ring, lanes),
        out_shape=(
            jax.ShapeDtypeStruct((lanes, own, HEADS * DIM), jnp.bfloat16),
            jax.ShapeDtypeStruct((HEADS, rows), jnp.float32),
        ),
        in_specs=[vmem, vmem, pl.BlockSpec(memory_space=pltpu.SMEM)],
        out_specs=(vmem, vmem),
        scratch_shapes=[
            pltpu.VMEM((2, ring, chunk, LANES), jnp.bfloat16),
            pltpu.VMEM((2 * DIM, HEADS * rows), jnp.bfloat16),
            pltpu.VMEM((HEADS, DIM, rows), jnp.float32),
            pltpu.VMEM((HEADS, rows), jnp.float32),
            pltpu.VMEM((HEADS, rows), jnp.float32),
        ],
        compiler_params=pltpu.CompilerParams(vmem_limit_bytes=limit),
        name="attend",
    )(queries, kv, doc_lengths)
    return pl.pallas_call(
        functools.partial(merge_kernel, lanes),
        out_shape=jax.ShapeDtypeStruct((own, HEADS * DIM), jnp.bfloat16),
        in_specs=[vmem, vmem],
        out_specs=vmem,
        scratch_shapes=[
            pltpu.VMEM((lanes, own, HEADS * DIM), jnp.bfloat16),
            pltpu.VMEM((lanes, HEADS, rows), jnp.float32),
            pltpu.VMEM((rows, LANES), jnp.float32),
            pltpu.VMEM((own, HEADS * DIM), jnp.bfloat16),
            sems((lanes, HEADS // 2)), sems((lanes, HEADS // 2)),
            sems((lanes,)), sems((lanes,)),
            sems((HEADS // 2,)), sems((HEADS // 2,)),
        ],
        compiler_params=pltpu.CompilerParams(collective_id=2, has_side_effects=True, vmem_limit_bytes=limit),
        name="merge",
    )(parts, logs)


def per_device(ring, lanes, queries, keys, values, doc_lengths):
    args = (queries, keys, values, doc_lengths)
    out, bound = swift(ring, lanes, *args)
    fits = bound[0] <= (SAFE / FACTOR) ** 2
    return lax.cond(fits, lambda *_: out, functools.partial(steady, ring, lanes), *args)


def solution(mesh):
    ring = math.isqrt(mesh.shape["pb"] // 2)
    return jax.shard_map(
        functools.partial(per_device, ring, mesh.shape["ka"]),
        mesh=mesh,
        in_specs=(P("pb", None), P(("pb", "ka"), None), P(("pb", "ka"), None), P()),
        out_specs=P(("pb", "ka"), None),
        check_vma=False,
    )
```

```python
import functools
import math

import jax
import jax.numpy as jnp
from jax import lax
from jax.experimental import pallas as pl
from jax.experimental.pallas import tpu as pltpu
from jax.sharding import PartitionSpec as P

HEADS = 8
DIM = 128
DOCS = 8
MOST = 24576
LANES = 128
FACTOR = math.log2(math.e) / math.sqrt(DIM)
MASK = 131072.0
EMPTY = -65536.0
NOTHING = -1e30
EXTRA = 16
SAFE = 100.0
MESH = pl.DeviceIdType.MESH


def place(c, first, second):
    z = second * (1 - c) + first * c
    y = first * (1 - c) + second * c
    return z, y


def swift_kernel(
    ring, lanes, q_hbm, k_hbm, v_hbm, len_hbm, out_ref, bound_ref,
    q_in, k_in, v_in, lens, stage, kv, kfeat, qcat, acc, tot, obuf, rbuf, sums, most, mixing,
    s_in, s_one, r_one, s_fwd, r_fwd, s_bwd, r_bwd, s_sib, r_sib, s_cross, r_cross, s_out, r_out, s_sum, r_sum, s_most, r_most,
):
    half = ring // 2
    rows = q_in.shape[0]
    own = k_in.shape[0]
    chunk = ring * own
    plane = ring * 2 * rows
    me = lax.axis_index("pb")
    x = lax.axis_index("ka")
    c = lax.rem(me, 2)
    z = me // (2 * ring)
    y = lax.rem(me // 2, ring)
    p1 = y * (1 - c) + z * c
    p2 = z * (1 - c) + y * c

    def wrap(value):
        return lax.rem(value + 2 * ring, ring)

    def device(first, second, core=c):
        zz, yy = place(c, wrap(first), wrap(second))
        return {"pb": (zz * ring + yy) * 2 + core}

    sibling = {"pb": me + 1 - 2 * c}

    barrier = pltpu.get_barrier_semaphore()
    partners = [device(p1 + d, p2) for d in range(1, ring)]
    partners += [device(p1, p2 + d, core) for d in (1, -1) for core in (c, 1 - c)]
    partners += [device(p1 + d, p2, 1 - c) for d in (1, -1)]
    partners += [sibling] + [{"ka": lax.rem(x + d, lanes)} for d in range(1, lanes)]
    for partner in partners:
        pl.semaphore_signal(barrier, inc=1, device_id=partner, device_id_type=MESH)
    moves = [
        pltpu.make_async_copy(src, dst, s_in.at[n])
        for n, (src, dst) in enumerate(((k_hbm, k_in), (v_hbm, v_in), (len_hbm, lens), (q_hbm, q_in)))
    ]
    for move in moves:
        move.start()
    moves[0].wait()
    moves[1].wait()
    stage[p1, :own] = k_in[...]
    stage[p1, own : 2 * own] = v_in[...]
    wide = k_in[...].astype(jnp.float32)
    longest = jnp.max(jnp.sum(wide * wide, axis=1, keepdims=True), axis=0, keepdims=True)
    k_most = longest
    moves[3].wait()
    longest = jnp.zeros((rows, 1), jnp.float32)
    for h in range(HEADS):
        wide = q_in[:, h * DIM : (h + 1) * DIM].astype(jnp.float32)
        longest = jnp.maximum(longest, jnp.sum(wide * wide, axis=1, keepdims=True))
    longest = jnp.max(longest, axis=0, keepdims=True)
    upper = lax.broadcasted_iota(jnp.int32, (EXTRA, DIM), 0) < EXTRA // 2
    stage[p1, 2 * own :] = (jnp.where(upper, k_most, longest) * 1.01).astype(jnp.bfloat16)
    pl.semaphore_wait(barrier, len(partners))

    def copy(ref, send, recv, where):
        return pltpu.make_async_remote_copy(
            src_ref=ref, dst_ref=ref, send_sem=send, recv_sem=recv, device_id=where, device_id_type=MESH
        )

    def one_copy(d, b1):
        return copy(stage.at[wrap(b1)], s_one.at[d - 1], r_one.at[d - 1], device(p1 + d, p2))

    def piece(cc, b, i):
        return kv.at[cc, wrap(b), i]

    def fwd_copy(s, b, i):
        return copy(piece(c, b, i), s_fwd.at[s - 1, i], r_fwd.at[s - 1, i], device(p1, p2 + 1))

    def bwd_copy(s, b, i):
        return copy(piece(c, b, i), s_bwd.at[s - 1, i], r_bwd.at[s - 1, i], device(p1, p2 - 1))

    def sib_copy(k, cc, b, i):
        return copy(piece(cc, b, i), s_sib.at[k, i], r_sib.at[k, i], sibling)

    def cross_copy(cc, b, i):
        return copy(piece(cc, b, i), s_cross.at[i], r_cross.at[i], device(p1, p2 + 1 - 2 * i, 1 - c))

    def pass_on(s):
        for i in range(2):
            fwd_copy(s, p2 - s, i).wait_recv()
            if s + 1 < half or i == 0:
                fwd_copy(s + 1, p2 - s, i).start()
            bwd_copy(s, p2 + s, i).wait_recv()
            if s + 1 < half or i == 1:
                bwd_copy(s + 1, p2 + s, i).start()
            if s + 1 == half:
                cross_copy(c, p2 - s + 2 * i * s, i).start()
            sib_copy(2 * s - 1, c, p2 - s, i).start()
            sib_copy(2 * s, c, p2 + s, i).start()

    def sib_arrived(s):
        for i in range(2):
            sib_copy(2 * s - 1, 1 - c, p1 - s, i).wait_recv()
            sib_copy(2 * s, 1 - c, p1 + s, i).wait_recv()

    for d in sorted(range(1, ring), key=lambda d: abs(d - half)):
        one_copy(d, p1).start()
    moves[2].wait()

    lane = lax.broadcasted_iota(jnp.int32, (1, LANES), 1)
    line = lax.broadcasted_iota(jnp.int32, (LANES, 1), 0)
    ends = jnp.zeros((1, LANES), jnp.int32)
    begins = jnp.zeros((1, LANES), jnp.int32)
    ends_down = jnp.zeros((LANES, 1), jnp.int32)
    begins_down = jnp.zeros((LANES, 1), jnp.int32)
    for j in range(DOCS):
        length = lens[j]
        ends += jnp.where(lane >= j, length, 0)
        begins += jnp.where(lane > j, length, 0)
        ends_down += jnp.where(line >= j, length, 0)
        begins_down += jnp.where(line > j, length, 0)
    tok = lax.broadcasted_iota(jnp.int32, (LANES, rows), 1)
    col = lax.broadcasted_iota(jnp.int32, (LANES, rows), 0)
    pos = me * rows + tok
    hidden = jnp.where((col < DOCS) & ((pos < begins_down) | (pos >= ends_down)), -MASK, 0.0)
    hidden = jnp.where(col == DOCS, -MASK, hidden)
    first = col - 2 * DOCS
    later = (first >= 0) & (first < own) & (tok < x * own + first)
    hidden = jnp.where(later, -MASK, hidden).astype(jnp.bfloat16)
    for h in range(HEADS):
        at = slice(h % 2 * rows, (h % 2 + 1) * rows)
        qcat[h // 2, :DIM, at] = q_in[:, h * DIM : (h + 1) * DIM].T
        qcat[h // 2, DIM:, at] = hidden
    acc[...] = jnp.zeros_like(acc)
    tot[...] = jnp.zeros_like(tot)

    def features(n, carry):
        cc, b = n // ring, lax.rem(n, ring)
        inner = lax.broadcasted_iota(jnp.int32, (own, LANES), 0)
        lanes_of = lax.broadcasted_iota(jnp.int32, (own, LANES), 1)
        for a in range(ring):
            zz, yy = place(cc, a, b)
            block = (zz * ring + yy) * 2 + cc
            at = block * rows + x * own + inner
            mark = ((at >= begins) & (at < ends)).astype(jnp.float32)
            mark = jnp.where((lanes_of == DOCS) & (block > me), 1.0, mark)
            mark = jnp.where((lanes_of == inner + 2 * DOCS) & (block == me), 1.0, mark)
            kfeat[cc, b, a * own : (a + 1) * own, :] = mark.astype(jnp.bfloat16)
        return carry

    lax.fori_loop(0, 2 * ring, features, 0)

    ones = jnp.ones((16, chunk), jnp.bfloat16)

    def scores(g, cc, b, size):
        keys = jnp.concatenate([kv[cc, b, 0, :size], kfeat[cc, b, :size]], axis=1)
        return jnp.dot(keys, qcat[g], preferred_element_type=jnp.float32)

    def fold(g, cc, b, size, s):
        p = jnp.exp2(s * FACTOR).astype(jnp.bfloat16)
        vals = jnp.concatenate([kv[cc, b, 1, n : n + LANES] for n in range(0, size, LANES)], axis=1)
        both = jnp.dot(jnp.concatenate([vals, ones[:, :size]], axis=0), p, preferred_element_type=jnp.float32)
        acc[g] += both[:DIM]
        tot[g] += both[DIM : DIM + 1]

    def run(work):
        s = scores(*work[0])
        for n, item in enumerate(work):
            after = scores(*work[n + 1]) if n + 1 < len(work) else None
            fold(*item, s)
            s = after

    for d in range(1, ring):
        one_copy(d, p1 - d).wait_recv()
    for n in range(ring):
        kv[c, p2, 0, n * own : (n + 1) * own] = stage[n, :own]
    largest = functools.reduce(jnp.maximum, [stage[n, 2 * own :] for n in range(ring)])
    for i in range(2):
        kv[c, p2, i, chunk:] = largest
    fwd_copy(1, p2, 0).start()
    bwd_copy(1, p2, 0).start()
    side = LANES // own
    for n in range(ring // side):
        block = stage[n * side : (n + 1) * side, own : 2 * own].reshape(LANES, DIM)
        kv[c, p2, 1, n * LANES : (n + 1) * LANES] = block.T
    fwd_copy(1, p2, 1).start()
    bwd_copy(1, p2, 1).start()
    for i in range(2):
        sib_copy(0, c, p2, i).start()

    def seen(b):
        return (b <= z) & ((b + 1) * plane > me * rows - (MOST - 1))

    def unit(u, carry):
        v = jnp.maximum(u - 2, 0)
        s = v // 4 + 1
        r = lax.rem(v, 4)
        early = u < 2
        mine = jnp.where(early, u == 0, r < 2)
        cc = jnp.where(mine, c, 1 - c)
        shift = jnp.where(early, 0, (2 * lax.rem(r, 2) - 1) * s)
        b = wrap(jnp.where(mine, p2, p1) + shift)

        @pl.when(u == 1)
        def _():
            for i in range(2):
                sib_copy(0, 1 - c, p1, i).wait_recv()

        @pl.when((u >= 2) & (r == 2))
        def _():
            sib_arrived(s)

        short = (cc == 1) & (z < half)

        @pl.when(short)
        def _():
            run([(g, 1, b, chunk // 2) for g in range(HEADS // 2)])

        @pl.when(jnp.logical_not(short) & ((cc == 1) | seen(b)))
        def _():
            run([(g, cc, b, chunk) for g in range(HEADS // 2)])

        for step, after in ((1, 0), (2, 3), (3, 6)):
            if step < half:
                pl.when(u == after)(functools.partial(pass_on, step))
        return carry

    lax.fori_loop(0, 2 + 4 * (half - 2), unit, 0)

    def last_mine():
        fwd_copy(half, p2 - half, 0).wait_recv()
        bwd_copy(half, p2 + half, 1).wait_recv()

    def last_sib():
        sib_arrived(half - 1)

    def last_cross():
        cross_copy(1 - c, p1 - half, 0).wait_recv()
        cross_copy(1 - c, p1 + half, 1).wait_recv()

    def peer(d):
        return lax.rem(x + d, lanes)

    def out_copy(d, g):
        cols = pl.ds(pl.multiple_of(g * 2 * DIM, 2 * DIM), 2 * DIM)
        return pltpu.make_async_remote_copy(
            src_ref=obuf.at[peer(d), :, cols], dst_ref=rbuf.at[d, :, cols],
            send_sem=s_out.at[d, g], recv_sem=r_out.at[d, g], device_id={"ka": peer(d)}, device_id_type=MESH,
        )

    def sum_copy(d):
        return pltpu.make_async_remote_copy(
            src_ref=sums.at[0], dst_ref=sums.at[d],
            send_sem=s_sum.at[d], recv_sem=r_sum.at[d], device_id={"ka": peer(d)}, device_id_type=MESH,
        )

    def most_copy(d):
        return pltpu.make_async_remote_copy(
            src_ref=most.at[0], dst_ref=most.at[d],
            send_sem=s_most.at[d], recv_sem=r_most.at[d], device_id={"ka": peer(d)}, device_id_type=MESH,
        )

    shifts = (1 - half, half - 1, half)
    early_cc = [(c, p2 + d) for d in shifts[:2]] + [(1 - c, p1 + d) for d in shifts[:2]]
    late = early_cc + [(c, p2 + half), (1 - c, p1 + half)]

    def finish(work, g, carry):
        run([(g, cc, wrap(b), size) for cc, b, size in work])
        for n in range(2):
            h = 2 * g + n
            at = slice(n * rows, (n + 1) * rows)
            part = acc[g, :, at].T.astype(jnp.bfloat16)
            sums[0, h] = tot[g, :, at]
            cols = pl.ds(pl.multiple_of(h * DIM, DIM), DIM)
            for j in range(lanes):
                obuf[j, :, cols] = part[j * own : (j + 1) * own, :]
        for d in range(1, lanes):
            out_copy(d, g).start()
        return carry

    def finish_all(work):
        lax.fori_loop(0, HEADS // 2, functools.partial(finish, work), 0)
        for d in range(1, lanes):
            sum_copy(d).start()

    @pl.when(z >= half)
    def _():
        last_sib()
        last_cross()
        last_mine()
        finish_all([(cc, b, chunk) for cc, b in late])

    halves = [(1, y + d, chunk // 2) for d in shifts]

    @pl.when(z == half - 1)
    def _():
        last_sib()
        pl.when(c == 0)(last_cross)
        pl.when(c == 1)(last_mine)
        finish_all([(0, 0, chunk)] + halves)
        pl.when(c == 0)(last_mine)
        pl.when(c == 1)(last_cross)

    @pl.when(z < half - 1)
    def _():
        @pl.when(c == 0)
        def _():
            last_sib()
            last_cross()

        pl.when(c == 1)(last_mine)
        finish_all(halves)
        pl.when(c == 0)(last_mine)

        @pl.when(c == 1)
        def _():
            last_sib()
            last_cross()

    met = [kv[cc, b, i, chunk:] for cc in range(2) for b in range(ring) for i in range(2)]
    met = functools.reduce(jnp.maximum, met).astype(jnp.float32)
    for i in range(2):
        row = met[i * EXTRA // 2 : i * EXTRA // 2 + 1, :]
        most[0, i] = row
    for d in range(1, lanes):
        most_copy(d).start()
    for d in range(1, ring):
        one_copy(d, p1).wait_send()
    for i in range(2):
        sib_copy(0, c, p2, i).wait_send()
        for s in range(1, half):
            fwd_copy(s, p2 - s + 1, i).wait_send()
            bwd_copy(s, p2 + s - 1, i).wait_send()
            sib_copy(2 * s - 1, c, p2 - s, i).wait_send()
            sib_copy(2 * s, c, p2 + s, i).wait_send()
        cross_copy(c, p2 + (2 * i - 1) * (half - 1), i).wait_send()
    fwd_copy(half, p2 - half + 1, 0).wait_send()
    bwd_copy(half, p2 + half - 1, 1).wait_send()
    for d in range(1, lanes):
        sum_copy(d).wait_recv()
    whole = functools.reduce(jnp.add, [sums[d] for d in range(lanes)])
    share = [1.0 / whole[h] for h in range(HEADS)] + [jnp.zeros((LANES - HEADS, rows), jnp.float32)]
    mixing[...] = jnp.concatenate(share, axis=0).T
    mix = mixing[pl.ds(pl.multiple_of(x * own, own), own), :]
    for h in range(HEADS):
        cols = slice(h * DIM, (h + 1) * DIM)
        mixed = obuf[x, :, cols].astype(jnp.float32)
        for d in range(1, lanes):
            if h % 2 == 0:
                out_copy(d, h // 2).wait_recv()
            mixed += rbuf[d, :, cols].astype(jnp.float32)
        out_ref[:, cols] = (mixed * mix[:, h : h + 1]).astype(out_ref.dtype)

    for d in range(1, lanes):
        most_copy(d).wait_recv()
    met = functools.reduce(jnp.maximum, [most[d] for d in range(lanes)])
    bound_ref[0] = jnp.max(met[0] * met[1])
    for d in range(1, lanes):
        sum_copy(d).wait_send()
        most_copy(d).wait_send()
        for g in range(HEADS // 2):
            out_copy(d, g).wait_send()


def swift(ring, lanes, queries, keys, values, doc_lengths):
    rows, own = queries.shape[0], keys.shape[0]
    half = ring // 2
    chunk = ring * own
    vmem = pl.BlockSpec(memory_space=pltpu.VMEM)
    sems = pltpu.SemaphoreType.DMA
    parts = (lanes, own, HEADS * DIM)
    return pl.pallas_call(
        functools.partial(swift_kernel, ring, lanes),
        out_shape=(
            jax.ShapeDtypeStruct((own, HEADS * DIM), jnp.bfloat16),
            jax.ShapeDtypeStruct((1,), jnp.float32),
        ),
        in_specs=[pl.BlockSpec(memory_space=pltpu.HBM)] * 4,
        out_specs=(vmem, pl.BlockSpec(memory_space=pltpu.SMEM)),
        scratch_shapes=[
            pltpu.VMEM(queries.shape, jnp.bfloat16),
            pltpu.VMEM(keys.shape, jnp.bfloat16),
            pltpu.VMEM(values.shape, jnp.bfloat16),
            pltpu.SMEM(doc_lengths.shape, jnp.int32),
            pltpu.VMEM((ring, 2 * own + EXTRA, DIM), jnp.bfloat16),
            pltpu.VMEM((2, ring, 2, chunk + EXTRA, DIM), jnp.bfloat16),
            pltpu.VMEM((2, ring, chunk, LANES), jnp.bfloat16),
            pltpu.VMEM((HEADS // 2, 2 * DIM, 2 * rows), jnp.bfloat16),
            pltpu.VMEM((HEADS // 2, DIM, 2 * rows), jnp.float32),
            pltpu.VMEM((HEADS // 2, 1, 2 * rows), jnp.float32),
            pltpu.VMEM(parts, jnp.bfloat16),
            pltpu.VMEM(parts, jnp.bfloat16),
            pltpu.VMEM((lanes, HEADS, 1, rows), jnp.float32),
            pltpu.VMEM((lanes, 2, 1, LANES), jnp.float32),
            pltpu.VMEM((rows, LANES), jnp.float32),
            sems((4,)),
            sems((ring - 1,)), sems((ring - 1,)),
            sems((half, 2)), sems((half, 2)), sems((half, 2)), sems((half, 2)),
            sems((2 * half - 1, 2)), sems((2 * half - 1, 2)), sems((2,)), sems((2,)),
            sems((lanes, HEADS // 2)), sems((lanes, HEADS // 2)),
            sems((lanes,)), sems((lanes,)),
            sems((lanes,)), sems((lanes,)),
        ],
        compiler_params=pltpu.CompilerParams(
            collective_id=0, has_side_effects=True, vmem_limit_bytes=63 * 1024 * 1024
        ),
        cost_estimate=pl.CostEstimate(flops=10**10, bytes_accessed=10**7, transcendentals=10**7),
        name="swift",
    )(queries, keys, values, doc_lengths)


def where(ring):
    me = lax.axis_index("pb")
    x = lax.axis_index("ka")
    c = lax.rem(me, 2)
    z = me // (2 * ring)
    y = lax.rem(me // 2, ring)
    return me, x, c, z, y


def greet(partners):
    barrier = pltpu.get_barrier_semaphore()
    for partner in partners:
        pl.semaphore_signal(barrier, inc=1, device_id=partner, device_id_type=MESH)
    return lambda: pl.semaphore_wait(barrier, len(partners))


def gather_kernel(
    ring, k_ref, v_ref, kv, stage,
    s_one, r_one, s_fwd, r_fwd, s_bwd, r_bwd, s_sib, r_sib,
):
    half = ring // 2
    own = k_ref.shape[0]
    me, x, c, z, y = where(ring)
    p1 = y * (1 - c) + z * c
    p2 = z * (1 - c) + y * c

    def wrap(value):
        return lax.rem(value + 2 * ring, ring)

    def device(first, second):
        zz, yy = place(c, wrap(first), wrap(second))
        return {"pb": (zz * ring + yy) * 2 + c}

    sibling = {"pb": me + 1 - 2 * c}
    partners = [device(p1 + d, p2) for d in range(1, ring)]
    partners += [device(p1, p2 + d) for d in ((1, ring - 1) if ring > 2 else (1,))]
    ready = greet(partners + [sibling])
    stage[p1, :, :DIM] = k_ref[...]
    stage[p1, :, DIM:] = v_ref[...]
    ready()

    def copy(ref, send, recv, to):
        return pltpu.make_async_remote_copy(
            src_ref=ref, dst_ref=ref, send_sem=send, recv_sem=recv, device_id=to, device_id_type=MESH
        )

    def one_copy(d, b1):
        return copy(stage.at[wrap(b1)], s_one.at[d - 1], r_one.at[d - 1], device(p1 + d, p2))

    def piece(cc, b, p):
        size = ring * own // 2
        return kv.at[cc, wrap(b), p // 2, pl.ds((p % 2) * size, size)]

    def fwd_copy(s, b, p):
        return copy(piece(c, b, p), s_fwd.at[s - 1, p], r_fwd.at[s - 1, p], device(p1, p2 + 1))

    def bwd_copy(s, b, p):
        return copy(piece(c, b, p), s_bwd.at[s - 1, p], r_bwd.at[s - 1, p], device(p1, p2 - 1))

    def sib_copy(n, cc, b, p):
        return copy(piece(cc, b, p), s_sib.at[n, p], r_sib.at[n, p], sibling)

    def travels(s, p):
        return s < half or (s == half and p < 2), s < half or (s == half and p >= 2)

    for d in sorted(range(1, ring), key=lambda d: abs(d - half)):
        one_copy(d, p1).start()
    for d in range(1, ring):
        one_copy(d, p1 - d).wait_recv()
    for n in range(ring):
        kv[c, p2, 0, n * own : (n + 1) * own] = stage[n, :, :DIM]
    side = LANES // own
    for n in range(ring // side):
        block = stage[n * side : (n + 1) * side, :, DIM:].reshape(LANES, DIM)
        kv[c, p2, 1, n * LANES : (n + 1) * LANES] = block.T
    for p in range(4):
        if travels(1, p)[0]:
            fwd_copy(1, p2, p).start()
        if travels(1, p)[1]:
            bwd_copy(1, p2, p).start()
    for p in range(4):
        sib_copy(0, c, p2, p).start()
    for s in range(1, half + 1):
        for p in range(4):
            if travels(s, p)[0]:
                fwd_copy(s, p2 - s, p).wait_recv()
                if travels(s + 1, p)[0]:
                    fwd_copy(s + 1, p2 - s, p).start()
            if travels(s, p)[1]:
                bwd_copy(s, p2 + s, p).wait_recv()
                if travels(s + 1, p)[1]:
                    bwd_copy(s + 1, p2 + s, p).start()
        for p in range(4):
            if travels(s, p)[0]:
                sib_copy(2 * s - 1, c, p2 - s, p).start()
            if travels(s, p)[1]:
                sib_copy(2 * s, c, p2 + s, p).start()
    for p in range(4):
        sib_copy(0, 1 - c, p1, p).wait_recv()
    for s in range(1, half + 1):
        for p in range(4):
            if travels(s, p)[0]:
                sib_copy(2 * s - 1, 1 - c, p1 - s, p).wait_recv()
            if travels(s, p)[1]:
                sib_copy(2 * s, 1 - c, p1 + s, p).wait_recv()
    for d in range(1, ring):
        one_copy(d, p1).wait_send()
    for p in range(4):
        sib_copy(0, c, p2, p).wait_send()
    for s in range(1, half + 1):
        for p in range(4):
            if travels(s, p)[0]:
                fwd_copy(s, p2 - s + 1, p).wait_send()
                sib_copy(2 * s - 1, c, p2 - s, p).wait_send()
            if travels(s, p)[1]:
                bwd_copy(s, p2 + s - 1, p).wait_send()
                sib_copy(2 * s, c, p2 + s, p).wait_send()


def attend_kernel(ring, lanes, q_ref, kv, lens, obuf, lbuf, kfeat, qcat, acc, tot, top):
    rows = q_ref.shape[0]
    own = rows // lanes
    chunk = ring * own
    plane = ring * 2 * rows
    me, x, c, z, y = where(ring)

    lane = lax.broadcasted_iota(jnp.int32, (1, LANES), 1)
    line = lax.broadcasted_iota(jnp.int32, (LANES, 1), 0)
    ends = jnp.zeros((1, LANES), jnp.int32)
    begins = jnp.zeros((1, LANES), jnp.int32)
    ends_down = jnp.zeros((LANES, 1), jnp.int32)
    begins_down = jnp.zeros((LANES, 1), jnp.int32)
    for j in range(DOCS):
        length = lens[j]
        ends += jnp.where(lane >= j, length, 0)
        begins += jnp.where(lane > j, length, 0)
        ends_down += jnp.where(line >= j, length, 0)
        begins_down += jnp.where(line > j, length, 0)
    tok = lax.broadcasted_iota(jnp.int32, (LANES, rows), 1)
    col = lax.broadcasted_iota(jnp.int32, (LANES, rows), 0)
    pos = me * rows + tok
    hidden = jnp.where((col < DOCS) & ((pos < begins_down) | (pos >= ends_down)), -MASK, 0.0)
    hidden = jnp.where(col == DOCS, -MASK, hidden)
    first = col - 2 * DOCS
    later = (first >= 0) & (first < own) & (tok < x * own + first)
    hidden = jnp.where(later, -MASK, hidden).astype(jnp.bfloat16)
    for h in range(HEADS):
        turned = q_ref[:, h * DIM : (h + 1) * DIM].T
        qcat[:DIM, h * rows : (h + 1) * rows] = turned
        qcat[DIM:, h * rows : (h + 1) * rows] = hidden
    acc[...] = jnp.zeros_like(acc)
    tot[...] = jnp.zeros_like(tot)
    top[...] = jnp.full_like(top, EMPTY)

    def features(n, carry):
        cc, b = n // ring, lax.rem(n, ring)
        inner = lax.broadcasted_iota(jnp.int32, (own, LANES), 0)
        lanes_of = lax.broadcasted_iota(jnp.int32, (own, LANES), 1)
        for a in range(ring):
            zz, yy = place(cc, a, b)
            block = (zz * ring + yy) * 2 + cc
            at = block * rows + x * own + inner
            mark = ((at >= begins) & (at < ends)).astype(jnp.float32)
            mark = jnp.where((lanes_of == DOCS) & (block > me), 1.0, mark)
            mark = jnp.where((lanes_of == inner + 2 * DOCS) & (block == me), 1.0, mark)
            kfeat[cc, b, a * own : (a + 1) * own, :] = mark.astype(jnp.bfloat16)
        return carry

    lax.fori_loop(0, 2 * ring, features, 0)
    ones = jnp.ones((16, chunk), jnp.bfloat16)

    def scores(h, cc, b):
        keys = jnp.concatenate([kv[cc, b, 0], kfeat[cc, b]], axis=1)
        return jnp.dot(keys, qcat[:, h * rows : (h + 1) * rows], preferred_element_type=jnp.float32)

    def weighted(cc, b, p):
        vals = jnp.concatenate([kv[cc, b, 1, n : n + LANES] for n in range(0, chunk, LANES)], axis=1)
        return jnp.dot(jnp.concatenate([vals, ones], axis=0), p, preferred_element_type=jnp.float32)

    def fold(h, cc, b, s):
        old = top[h : h + 1, :]
        new = jnp.maximum(old, jnp.max(s, axis=0, keepdims=True))
        both = weighted(cc, b, jnp.exp2((s - new) * FACTOR).astype(jnp.bfloat16))
        alpha = jnp.exp2((old - new) * FACTOR)
        acc[h] = acc[h] * alpha + both[:DIM]
        tot[h : h + 1, :] = tot[h : h + 1, :] * alpha + both[DIM : DIM + 1]
        top[h : h + 1, :] = new

    def sweep(fold):
        def body(n, carry):
            cc, b = n // ring, lax.rem(n, ring)
            seen = (b <= z) & ((b + 1) * plane > me * rows - (MOST - 1))

            @pl.when((cc == 1) | seen)
            def _():
                s = scores(0, cc, b)
                for h in range(HEADS):
                    after = scores(h + 1, cc, b) if h + 1 < HEADS else None
                    fold(h, cc, b, s)
                    s = after

            return carry

        lax.fori_loop(0, 2 * ring, body, 0)

    sweep(fold)
    logs = []
    for h in range(HEADS):
        total = tot[h : h + 1, :]
        some = total > 0.0
        safe = jnp.where(some, total, 1.0)
        part = (acc[h] / safe).T.astype(jnp.bfloat16)
        logs.append(jnp.where(some, top[h : h + 1, :] * FACTOR + jnp.log2(safe), NOTHING))
        for j in range(lanes):
            obuf[j, :, h * DIM : (h + 1) * DIM] = part[j * own : (j + 1) * own, :]
    lbuf[...] = jnp.concatenate(logs, axis=0)


def merge_kernel(lanes, obuf, lbuf, out_ref, rbuf, logs, mixing, relay, s_out, r_out, s_log, r_log, s_rel, r_rel):
    x = lax.axis_index("ka")
    own = out_ref.shape[0]
    rows = lbuf.shape[1]
    near = [d for d in range(1, lanes) if lanes != 4 or d != 2]

    def peer(d):
        return lax.rem(x + d, lanes)

    def copy(src, dst, send, recv, d):
        return pltpu.make_async_remote_copy(
            src_ref=src, dst_ref=dst, send_sem=send, recv_sem=recv, device_id={"ka": peer(d)}, device_id_type=MESH
        )

    def cols_of(g):
        return pl.ds(g * 2 * DIM, 2 * DIM)

    def out_copy(d, g):
        cols = cols_of(g)
        return copy(obuf.at[peer(d), :, cols], rbuf.at[d, :, cols], s_out.at[d, g], r_out.at[d, g], d)

    def way(g):
        return 1 if g < HEADS // 4 else 3

    def relay_copy(g):
        cols = cols_of(g)
        return copy(obuf.at[peer(2), :, cols], relay.at[:, cols], s_rel.at[g], r_rel.at[g], way(g))

    def onward_copy(g):
        cols = cols_of(g)
        return copy(relay.at[:, cols], rbuf.at[2, :, cols], s_out.at[2, g], r_out.at[2, g], way(g))

    def log_copy(d):
        return copy(lbuf, logs.at[d], s_log.at[d], r_log.at[d], d)

    greet([{"ka": peer(d)} for d in range(1, lanes)])()
    groups = range(HEADS // 2)
    for d in range(1, lanes):
        log_copy(d).start()
    if lanes == 4:
        for g in (0, 2, 1, 3):
            relay_copy(g).start()
    for g in groups:
        for d in near:
            out_copy(d, g).start()
    if lanes == 4:
        for g in (0, 2, 1, 3):
            relay_copy(g).wait_recv()
            onward_copy(g).start()
    for d in range(1, lanes):
        log_copy(d).wait_recv()
    sizes = [lbuf[...]] + [logs[d] for d in range(1, lanes)]
    highest = functools.reduce(jnp.maximum, sizes)
    shares = [jnp.exp2(size - highest) for size in sizes]
    whole = functools.reduce(jnp.add, shares)
    shares = [share / whole for share in shares]
    shares.append(jnp.zeros((LANES - HEADS * lanes, rows), jnp.float32))
    mixing[...] = jnp.concatenate(shares, axis=0).T
    mix = mixing[pl.ds(pl.multiple_of(x * own, own), own), :]
    for g in groups:
        for d in range(1, lanes):
            out_copy(d, g).wait_recv()
        for h in (2 * g, 2 * g + 1):
            cols = slice(h * DIM, (h + 1) * DIM)
            mixed = mix[:, h : h + 1] * obuf[x, :, cols].astype(jnp.float32)
            for d in range(1, lanes):
                at = d * HEADS + h
                mixed += mix[:, at : at + 1] * rbuf[d, :, cols].astype(jnp.float32)
            out_ref[:, cols] = mixed.astype(out_ref.dtype)
    for d in range(1, lanes):
        log_copy(d).wait_send()
    for g in groups:
        for d in near:
            out_copy(d, g).wait_send()
        if lanes == 4:
            relay_copy(g).wait_send()
            onward_copy(g).wait_send()


def steady(ring, lanes, queries, keys, values, doc_lengths):
    rows, own = queries.shape[0], keys.shape[0]
    half = ring // 2
    chunk = ring * own
    vmem = pl.BlockSpec(memory_space=pltpu.VMEM)
    sems = pltpu.SemaphoreType.DMA
    limit = 48 * 1024 * 1024
    kv = pl.pallas_call(
        functools.partial(gather_kernel, ring),
        out_shape=jax.ShapeDtypeStruct((2, ring, 2, chunk, DIM), jnp.bfloat16),
        in_specs=[vmem, vmem],
        out_specs=vmem,
        scratch_shapes=[
            pltpu.VMEM((ring, own, 2 * DIM), jnp.bfloat16),
            sems((ring - 1,)), sems((ring - 1,)),
            sems((half, 4)), sems((half, 4)), sems((half, 4)), sems((half, 4)),
            sems((2 * half + 1, 4)), sems((2 * half + 1, 4)),
        ],
        compiler_params=pltpu.CompilerParams(collective_id=1, has_side_effects=True, vmem_limit_bytes=limit),
        name="gather",
    )(keys, values)
    parts, logs = pl.pallas_call(
        functools.partial(attend_kernel, ring, lanes),
        out_shape=(
            jax.ShapeDtypeStruct((lanes, own, HEADS * DIM), jnp.bfloat16),
            jax.ShapeDtypeStruct((HEADS, rows), jnp.float32),
        ),
        in_specs=[vmem, vmem, pl.BlockSpec(memory_space=pltpu.SMEM)],
        out_specs=(vmem, vmem),
        scratch_shapes=[
            pltpu.VMEM((2, ring, chunk, LANES), jnp.bfloat16),
            pltpu.VMEM((2 * DIM, HEADS * rows), jnp.bfloat16),
            pltpu.VMEM((HEADS, DIM, rows), jnp.float32),
            pltpu.VMEM((HEADS, rows), jnp.float32),
            pltpu.VMEM((HEADS, rows), jnp.float32),
        ],
        compiler_params=pltpu.CompilerParams(vmem_limit_bytes=limit),
        name="attend",
    )(queries, kv, doc_lengths)
    return pl.pallas_call(
        functools.partial(merge_kernel, lanes),
        out_shape=jax.ShapeDtypeStruct((own, HEADS * DIM), jnp.bfloat16),
        in_specs=[vmem, vmem],
        out_specs=vmem,
        scratch_shapes=[
            pltpu.VMEM((lanes, own, HEADS * DIM), jnp.bfloat16),
            pltpu.VMEM((lanes, HEADS, rows), jnp.float32),
            pltpu.VMEM((rows, LANES), jnp.float32),
            pltpu.VMEM((own, HEADS * DIM), jnp.bfloat16),
            sems((lanes, HEADS // 2)), sems((lanes, HEADS // 2)),
            sems((lanes,)), sems((lanes,)),
            sems((HEADS // 2,)), sems((HEADS // 2,)),
        ],
        compiler_params=pltpu.CompilerParams(collective_id=2, has_side_effects=True, vmem_limit_bytes=limit),
        name="merge",
    )(parts, logs)


def per_device(ring, lanes, queries, keys, values, doc_lengths):
    args = (queries, keys, values, doc_lengths)
    out, bound = swift(ring, lanes, *args)
    fits = bound[0] <= (SAFE / FACTOR) ** 2
    return lax.cond(fits, lambda *_: out, functools.partial(steady, ring, lanes), *args)


def solution(mesh):
    ring = math.isqrt(mesh.shape["pb"] // 2)
    return jax.shard_map(
        functools.partial(per_device, ring, mesh.shape["ka"]),
        mesh=mesh,
        in_specs=(P("pb", None), P(("pb", "ka"), None), P(("pb", "ka"), None), P()),
        out_specs=P(("pb", "ka"), None),
        check_vma=False,
    )
```

```python
import functools
import math

import jax
import jax.numpy as jnp
from jax import lax
from jax.experimental import pallas as pl
from jax.experimental.pallas import tpu as pltpu
from jax.sharding import PartitionSpec as P

HEADS = 8
DIM = 128
DOCS = 8
MOST = 24576
LANES = 128
FACTOR = math.log2(math.e) / math.sqrt(DIM)
MASK = 131072.0
EMPTY = -65536.0
NOTHING = -1e30
EXTRA = 16
SAFE = 100.0
MESH = pl.DeviceIdType.MESH


def place(c, first, second):
    z = second * (1 - c) + first * c
    y = first * (1 - c) + second * c
    return z, y


def swift_kernel(
    ring, lanes, q_hbm, k_hbm, v_hbm, len_hbm, out_ref, bound_ref,
    q_in, k_in, v_in, lens, stage, kv, kfeat, qcat, acc, tot, obuf, rbuf, sums, most, mixing,
    s_in, s_one, r_one, s_fwd, r_fwd, s_bwd, r_bwd, s_sib, r_sib, s_cross, r_cross, s_out, r_out, s_sum, r_sum, s_most, r_most,
):
    half = ring // 2
    rows = q_in.shape[0]
    own = k_in.shape[0]
    chunk = ring * own
    plane = ring * 2 * rows
    me = lax.axis_index("pb")
    x = lax.axis_index("ka")
    c = lax.rem(me, 2)
    z = me // (2 * ring)
    y = lax.rem(me // 2, ring)
    p1 = y * (1 - c) + z * c
    p2 = z * (1 - c) + y * c

    def wrap(value):
        return lax.rem(value + 2 * ring, ring)

    def device(first, second, core=c):
        zz, yy = place(c, wrap(first), wrap(second))
        return {"pb": (zz * ring + yy) * 2 + core}

    sibling = {"pb": me + 1 - 2 * c}

    moves = [
        pltpu.make_async_copy(src, dst, s_in.at[n])
        for n, (src, dst) in enumerate(((k_hbm, k_in), (v_hbm, v_in), (len_hbm, lens), (q_hbm, q_in)))
    ]
    for move in moves:
        move.start()

    barrier = pltpu.get_barrier_semaphore()
    partners = [device(p1 + d, p2) for d in range(1, ring)]
    partners += [device(p1, p2 + d, core) for d in (1, -1) for core in (c, 1 - c)]
    partners += [device(p1 + d, p2, 1 - c) for d in (1, -1)]
    partners += [sibling] + [{"ka": lax.rem(x + d, lanes)} for d in range(1, lanes)]
    for partner in partners:
        pl.semaphore_signal(barrier, inc=1, device_id=partner, device_id_type=MESH)
    moves[0].wait()
    moves[1].wait()
    stage[p1, :own] = k_in[...]
    stage[p1, own : 2 * own] = v_in[...]
    wide = k_in[...].astype(jnp.float32)
    longest = jnp.max(jnp.sum(wide * wide, axis=1, keepdims=True), axis=0, keepdims=True)
    k_most = longest
    moves[3].wait()
    longest = jnp.zeros((rows, 1), jnp.float32)
    for h in range(HEADS):
        wide = q_in[:, h * DIM : (h + 1) * DIM].astype(jnp.float32)
        longest = jnp.maximum(longest, jnp.sum(wide * wide, axis=1, keepdims=True))
    longest = jnp.max(longest, axis=0, keepdims=True)
    upper = lax.broadcasted_iota(jnp.int32, (EXTRA, DIM), 0) < EXTRA // 2
    stage[p1, 2 * own :] = (jnp.where(upper, k_most, longest) * 1.01).astype(jnp.bfloat16)
    pl.semaphore_wait(barrier, len(partners))

    def copy(ref, send, recv, where):
        return pltpu.make_async_remote_copy(
            src_ref=ref, dst_ref=ref, send_sem=send, recv_sem=recv, device_id=where, device_id_type=MESH
        )

    def one_copy(d, b1):
        return copy(stage.at[wrap(b1)], s_one.at[d - 1], r_one.at[d - 1], device(p1 + d, p2))

    def piece(cc, b, i):
        return kv.at[cc, wrap(b), i]

    def fwd_copy(s, b, i):
        return copy(piece(c, b, i), s_fwd.at[s - 1, i], r_fwd.at[s - 1, i], device(p1, p2 + 1))

    def bwd_copy(s, b, i):
        return copy(piece(c, b, i), s_bwd.at[s - 1, i], r_bwd.at[s - 1, i], device(p1, p2 - 1))

    def sib_copy(k, cc, b, i):
        return copy(piece(cc, b, i), s_sib.at[k, i], r_sib.at[k, i], sibling)

    def cross_copy(cc, b, i):
        return copy(piece(cc, b, i), s_cross.at[i], r_cross.at[i], device(p1, p2 + 1 - 2 * i, 1 - c))

    def pass_on(s):
        for i in range(2):
            fwd_copy(s, p2 - s, i).wait_recv()
            if s + 1 < half or i == 0:
                fwd_copy(s + 1, p2 - s, i).start()
            bwd_copy(s, p2 + s, i).wait_recv()
            if s + 1 < half or i == 1:
                bwd_copy(s + 1, p2 + s, i).start()
            if s + 1 == half:
                cross_copy(c, p2 - s + 2 * i * s, i).start()
            sib_copy(2 * s - 1, c, p2 - s, i).start()
            sib_copy(2 * s, c, p2 + s, i).start()

    def sib_arrived(s):
        for i in range(2):
            sib_copy(2 * s - 1, 1 - c, p1 - s, i).wait_recv()
            sib_copy(2 * s, 1 - c, p1 + s, i).wait_recv()

    for d in sorted(range(1, ring), key=lambda d: abs(d - half)):
        one_copy(d, p1).start()
    moves[2].wait()

    lane = lax.broadcasted_iota(jnp.int32, (1, LANES), 1)
    line = lax.broadcasted_iota(jnp.int32, (LANES, 1), 0)
    ends = jnp.zeros((1, LANES), jnp.int32)
    begins = jnp.zeros((1, LANES), jnp.int32)
    ends_down = jnp.zeros((LANES, 1), jnp.int32)
    begins_down = jnp.zeros((LANES, 1), jnp.int32)
    for j in range(DOCS):
        length = lens[j]
        ends += jnp.where(lane >= j, length, 0)
        begins += jnp.where(lane > j, length, 0)
        ends_down += jnp.where(line >= j, length, 0)
        begins_down += jnp.where(line > j, length, 0)
    tok = lax.broadcasted_iota(jnp.int32, (LANES, rows), 1)
    col = lax.broadcasted_iota(jnp.int32, (LANES, rows), 0)
    pos = me * rows + tok
    hidden = jnp.where((col < DOCS) & ((pos < begins_down) | (pos >= ends_down)), -MASK, 0.0)
    hidden = jnp.where(col == DOCS, -MASK, hidden)
    first = col - 2 * DOCS
    later = (first >= 0) & (first < own) & (tok < x * own + first)
    hidden = jnp.where(later, -MASK, hidden).astype(jnp.bfloat16)
    for h in range(HEADS):
        at = slice(h % 2 * rows, (h % 2 + 1) * rows)
        qcat[h // 2, :DIM, at] = q_in[:, h * DIM : (h + 1) * DIM].T
        qcat[h // 2, DIM:, at] = hidden
    acc[...] = jnp.zeros_like(acc)
    tot[...] = jnp.zeros_like(tot)

    def features(n, carry):
        cc, b = n // ring, lax.rem(n, ring)
        inner = lax.broadcasted_iota(jnp.int32, (own, LANES), 0)
        lanes_of = lax.broadcasted_iota(jnp.int32, (own, LANES), 1)
        for a in range(ring):
            zz, yy = place(cc, a, b)
            block = (zz * ring + yy) * 2 + cc
            at = block * rows + x * own + inner
            mark = ((at >= begins) & (at < ends)).astype(jnp.float32)
            mark = jnp.where((lanes_of == DOCS) & (block > me), 1.0, mark)
            mark = jnp.where((lanes_of == inner + 2 * DOCS) & (block == me), 1.0, mark)
            kfeat[cc, b, a * own : (a + 1) * own, :] = mark.astype(jnp.bfloat16)
        return carry

    lax.fori_loop(0, 2 * ring, features, 0)

    ones = jnp.ones((16, chunk), jnp.bfloat16)

    def scores(g, cc, b, size):
        keys = jnp.concatenate([kv[cc, b, 0, :size], kfeat[cc, b, :size]], axis=1)
        return jnp.dot(keys, qcat[g], preferred_element_type=jnp.float32)

    def fold(g, cc, b, size, s):
        p = jnp.exp2(s * FACTOR).astype(jnp.bfloat16)
        vals = jnp.concatenate([kv[cc, b, 1, n : n + LANES] for n in range(0, size, LANES)], axis=1)
        both = jnp.dot(jnp.concatenate([vals, ones[:, :size]], axis=0), p, preferred_element_type=jnp.float32)
        acc[g] += both[:DIM]
        tot[g] += both[DIM : DIM + 1]

    def run(work):
        s = scores(*work[0])
        for n, item in enumerate(work):
            after = scores(*work[n + 1]) if n + 1 < len(work) else None
            fold(*item, s)
            s = after

    for d in range(1, ring):
        one_copy(d, p1 - d).wait_recv()
    for n in range(ring):
        kv[c, p2, 0, n * own : (n + 1) * own] = stage[n, :own]
    largest = functools.reduce(jnp.maximum, [stage[n, 2 * own :] for n in range(ring)])
    for i in range(2):
        kv[c, p2, i, chunk:] = largest
    fwd_copy(1, p2, 0).start()
    bwd_copy(1, p2, 0).start()
    side = LANES // own
    for n in range(ring // side):
        block = stage[n * side : (n + 1) * side, own : 2 * own].reshape(LANES, DIM)
        kv[c, p2, 1, n * LANES : (n + 1) * LANES] = block.T
    fwd_copy(1, p2, 1).start()
    bwd_copy(1, p2, 1).start()
    for i in range(2):
        sib_copy(0, c, p2, i).start()

    def seen(b):
        return (b <= z) & ((b + 1) * plane > me * rows - (MOST - 1))

    def unit(u, carry):
        v = jnp.maximum(u - 2, 0)
        s = v // 4 + 1
        r = lax.rem(v, 4)
        early = u < 2
        mine = jnp.where(early, u == 0, r < 2)
        cc = jnp.where(mine, c, 1 - c)
        shift = jnp.where(early, 0, (2 * lax.rem(r, 2) - 1) * s)
        b = wrap(jnp.where(mine, p2, p1) + shift)

        @pl.when(u == 1)
        def _():
            for i in range(2):
                sib_copy(0, 1 - c, p1, i).wait_recv()

        @pl.when((u >= 2) & (r == 2))
        def _():
            sib_arrived(s)

        short = (cc == 1) & (z < half)

        @pl.when(short)
        def _():
            run([(g, 1, b, chunk // 2) for g in range(HEADS // 2)])

        @pl.when(jnp.logical_not(short) & ((cc == 1) | seen(b)))
        def _():
            run([(g, cc, b, chunk) for g in range(HEADS // 2)])

        for step, after in ((1, 0), (2, 3), (3, 6)):
            if step < half:
                pl.when(u == after)(functools.partial(pass_on, step))
        return carry

    lax.fori_loop(0, 2 + 4 * (half - 2), unit, 0)

    def last_mine():
        fwd_copy(half, p2 - half, 0).wait_recv()
        bwd_copy(half, p2 + half, 1).wait_recv()

    def last_sib():
        sib_arrived(half - 1)

    def last_cross():
        cross_copy(1 - c, p1 - half, 0).wait_recv()
        cross_copy(1 - c, p1 + half, 1).wait_recv()

    def peer(d):
        return lax.rem(x + d, lanes)

    def out_copy(d, g):
        cols = pl.ds(pl.multiple_of(g * 2 * DIM, 2 * DIM), 2 * DIM)
        return pltpu.make_async_remote_copy(
            src_ref=obuf.at[peer(d), :, cols], dst_ref=rbuf.at[d, :, cols],
            send_sem=s_out.at[d, g], recv_sem=r_out.at[d, g], device_id={"ka": peer(d)}, device_id_type=MESH,
        )

    def sum_copy(d):
        return pltpu.make_async_remote_copy(
            src_ref=sums.at[0], dst_ref=sums.at[d],
            send_sem=s_sum.at[d], recv_sem=r_sum.at[d], device_id={"ka": peer(d)}, device_id_type=MESH,
        )

    def most_copy(d):
        return pltpu.make_async_remote_copy(
            src_ref=most.at[0], dst_ref=most.at[d],
            send_sem=s_most.at[d], recv_sem=r_most.at[d], device_id={"ka": peer(d)}, device_id_type=MESH,
        )

    shifts = (1 - half, half - 1, half)
    early_cc = [(c, p2 + d) for d in shifts[:2]] + [(1 - c, p1 + d) for d in shifts[:2]]
    late = early_cc + [(c, p2 + half), (1 - c, p1 + half)]

    def finish(work, g, carry):
        run([(g, cc, wrap(b), size) for cc, b, size in work])
        for n in range(2):
            h = 2 * g + n
            at = slice(n * rows, (n + 1) * rows)
            part = acc[g, :, at].T.astype(jnp.bfloat16)
            sums[0, h] = tot[g, :, at]
            cols = pl.ds(pl.multiple_of(h * DIM, DIM), DIM)
            for j in range(lanes):
                obuf[j, :, cols] = part[j * own : (j + 1) * own, :]
        for d in range(1, lanes):
            out_copy(d, g).start()
        return carry

    def finish_all(work):
        lax.fori_loop(0, HEADS // 2, functools.partial(finish, work), 0)
        for d in range(1, lanes):
            sum_copy(d).start()

    @pl.when(z >= half)
    def _():
        last_sib()
        last_cross()
        last_mine()
        finish_all([(cc, b, chunk) for cc, b in late])

    halves = [(1, y + d, chunk // 2) for d in shifts]

    @pl.when(z == half - 1)
    def _():
        last_sib()
        pl.when(c == 0)(last_cross)
        pl.when(c == 1)(last_mine)
        finish_all([(0, 0, chunk)] + halves)
        pl.when(c == 0)(last_mine)
        pl.when(c == 1)(last_cross)

    @pl.when(z < half - 1)
    def _():
        @pl.when(c == 0)
        def _():
            last_sib()
            last_cross()

        pl.when(c == 1)(last_mine)
        finish_all(halves)
        pl.when(c == 0)(last_mine)

        @pl.when(c == 1)
        def _():
            last_sib()
            last_cross()

    met = [kv[cc, b, i, chunk:] for cc in range(2) for b in range(ring) for i in range(2)]
    met = functools.reduce(jnp.maximum, met).astype(jnp.float32)
    for i in range(2):
        row = met[i * EXTRA // 2 : i * EXTRA // 2 + 1, :]
        most[0, i] = row
    for d in range(1, lanes):
        most_copy(d).start()
    for d in range(1, ring):
        one_copy(d, p1).wait_send()
    for i in range(2):
        sib_copy(0, c, p2, i).wait_send()
        for s in range(1, half):
            fwd_copy(s, p2 - s + 1, i).wait_send()
            bwd_copy(s, p2 + s - 1, i).wait_send()
            sib_copy(2 * s - 1, c, p2 - s, i).wait_send()
            sib_copy(2 * s, c, p2 + s, i).wait_send()
        cross_copy(c, p2 + (2 * i - 1) * (half - 1), i).wait_send()
    fwd_copy(half, p2 - half + 1, 0).wait_send()
    bwd_copy(half, p2 + half - 1, 1).wait_send()
    for d in range(1, lanes):
        sum_copy(d).wait_recv()
    whole = functools.reduce(jnp.add, [sums[d] for d in range(lanes)])
    share = [1.0 / whole[h] for h in range(HEADS)] + [jnp.zeros((LANES - HEADS, rows), jnp.float32)]
    mixing[...] = jnp.concatenate(share, axis=0).T
    mix = mixing[pl.ds(pl.multiple_of(x * own, own), own), :]
    for h in range(HEADS):
        cols = slice(h * DIM, (h + 1) * DIM)
        mixed = obuf[x, :, cols].astype(jnp.float32)
        for d in range(1, lanes):
            if h % 2 == 0:
                out_copy(d, h // 2).wait_recv()
            mixed += rbuf[d, :, cols].astype(jnp.float32)
        out_ref[:, cols] = (mixed * mix[:, h : h + 1]).astype(out_ref.dtype)

    for d in range(1, lanes):
        most_copy(d).wait_recv()
    met = functools.reduce(jnp.maximum, [most[d] for d in range(lanes)])
    bound_ref[0] = jnp.max(met[0] * met[1])
    for d in range(1, lanes):
        sum_copy(d).wait_send()
        most_copy(d).wait_send()
        for g in range(HEADS // 2):
            out_copy(d, g).wait_send()


def swift(ring, lanes, queries, keys, values, doc_lengths):
    rows, own = queries.shape[0], keys.shape[0]
    half = ring // 2
    chunk = ring * own
    vmem = pl.BlockSpec(memory_space=pltpu.VMEM)
    sems = pltpu.SemaphoreType.DMA
    parts = (lanes, own, HEADS * DIM)
    return pl.pallas_call(
        functools.partial(swift_kernel, ring, lanes),
        out_shape=(
            jax.ShapeDtypeStruct((own, HEADS * DIM), jnp.bfloat16),
            jax.ShapeDtypeStruct((1,), jnp.float32),
        ),
        in_specs=[pl.BlockSpec(memory_space=pltpu.HBM)] * 4,
        out_specs=(vmem, pl.BlockSpec(memory_space=pltpu.SMEM)),
        scratch_shapes=[
            pltpu.VMEM(queries.shape, jnp.bfloat16),
            pltpu.VMEM(keys.shape, jnp.bfloat16),
            pltpu.VMEM(values.shape, jnp.bfloat16),
            pltpu.SMEM(doc_lengths.shape, jnp.int32),
            pltpu.VMEM((ring, 2 * own + EXTRA, DIM), jnp.bfloat16),
            pltpu.VMEM((2, ring, 2, chunk + EXTRA, DIM), jnp.bfloat16),
            pltpu.VMEM((2, ring, chunk, LANES), jnp.bfloat16),
            pltpu.VMEM((HEADS // 2, 2 * DIM, 2 * rows), jnp.bfloat16),
            pltpu.VMEM((HEADS // 2, DIM, 2 * rows), jnp.float32),
            pltpu.VMEM((HEADS // 2, 1, 2 * rows), jnp.float32),
            pltpu.VMEM(parts, jnp.bfloat16),
            pltpu.VMEM(parts, jnp.bfloat16),
            pltpu.VMEM((lanes, HEADS, 1, rows), jnp.float32),
            pltpu.VMEM((lanes, 2, 1, LANES), jnp.float32),
            pltpu.VMEM((rows, LANES), jnp.float32),
            sems((4,)),
            sems((ring - 1,)), sems((ring - 1,)),
            sems((half, 2)), sems((half, 2)), sems((half, 2)), sems((half, 2)),
            sems((2 * half - 1, 2)), sems((2 * half - 1, 2)), sems((2,)), sems((2,)),
            sems((lanes, HEADS // 2)), sems((lanes, HEADS // 2)),
            sems((lanes,)), sems((lanes,)),
            sems((lanes,)), sems((lanes,)),
        ],
        compiler_params=pltpu.CompilerParams(
            collective_id=0, has_side_effects=True, vmem_limit_bytes=63 * 1024 * 1024
        ),
        cost_estimate=pl.CostEstimate(flops=10**10, bytes_accessed=10**7, transcendentals=10**7),
        name="swift",
    )(queries, keys, values, doc_lengths)


def where(ring):
    me = lax.axis_index("pb")
    x = lax.axis_index("ka")
    c = lax.rem(me, 2)
    z = me // (2 * ring)
    y = lax.rem(me // 2, ring)
    return me, x, c, z, y


def greet(partners):
    barrier = pltpu.get_barrier_semaphore()
    for partner in partners:
        pl.semaphore_signal(barrier, inc=1, device_id=partner, device_id_type=MESH)
    return lambda: pl.semaphore_wait(barrier, len(partners))


def gather_kernel(
    ring, k_ref, v_ref, kv, stage,
    s_one, r_one, s_fwd, r_fwd, s_bwd, r_bwd, s_sib, r_sib,
):
    half = ring // 2
    own = k_ref.shape[0]
    me, x, c, z, y = where(ring)
    p1 = y * (1 - c) + z * c
    p2 = z * (1 - c) + y * c

    def wrap(value):
        return lax.rem(value + 2 * ring, ring)

    def device(first, second):
        zz, yy = place(c, wrap(first), wrap(second))
        return {"pb": (zz * ring + yy) * 2 + c}

    sibling = {"pb": me + 1 - 2 * c}
    partners = [device(p1 + d, p2) for d in range(1, ring)]
    partners += [device(p1, p2 + d) for d in ((1, ring - 1) if ring > 2 else (1,))]
    ready = greet(partners + [sibling])
    stage[p1, :, :DIM] = k_ref[...]
    stage[p1, :, DIM:] = v_ref[...]
    ready()

    def copy(ref, send, recv, to):
        return pltpu.make_async_remote_copy(
            src_ref=ref, dst_ref=ref, send_sem=send, recv_sem=recv, device_id=to, device_id_type=MESH
        )

    def one_copy(d, b1):
        return copy(stage.at[wrap(b1)], s_one.at[d - 1], r_one.at[d - 1], device(p1 + d, p2))

    def piece(cc, b, p):
        size = ring * own // 2
        return kv.at[cc, wrap(b), p // 2, pl.ds((p % 2) * size, size)]

    def fwd_copy(s, b, p):
        return copy(piece(c, b, p), s_fwd.at[s - 1, p], r_fwd.at[s - 1, p], device(p1, p2 + 1))

    def bwd_copy(s, b, p):
        return copy(piece(c, b, p), s_bwd.at[s - 1, p], r_bwd.at[s - 1, p], device(p1, p2 - 1))

    def sib_copy(n, cc, b, p):
        return copy(piece(cc, b, p), s_sib.at[n, p], r_sib.at[n, p], sibling)

    def travels(s, p):
        return s < half or (s == half and p < 2), s < half or (s == half and p >= 2)

    for d in sorted(range(1, ring), key=lambda d: abs(d - half)):
        one_copy(d, p1).start()
    for d in range(1, ring):
        one_copy(d, p1 - d).wait_recv()
    for n in range(ring):
        kv[c, p2, 0, n * own : (n + 1) * own] = stage[n, :, :DIM]
    side = LANES // own
    for n in range(ring // side):
        block = stage[n * side : (n + 1) * side, :, DIM:].reshape(LANES, DIM)
        kv[c, p2, 1, n * LANES : (n + 1) * LANES] = block.T
    for p in range(4):
        if travels(1, p)[0]:
            fwd_copy(1, p2, p).start()
        if travels(1, p)[1]:
            bwd_copy(1, p2, p).start()
    for p in range(4):
        sib_copy(0, c, p2, p).start()
    for s in range(1, half + 1):
        for p in range(4):
            if travels(s, p)[0]:
                fwd_copy(s, p2 - s, p).wait_recv()
                if travels(s + 1, p)[0]:
                    fwd_copy(s + 1, p2 - s, p).start()
            if travels(s, p)[1]:
                bwd_copy(s, p2 + s, p).wait_recv()
                if travels(s + 1, p)[1]:
                    bwd_copy(s + 1, p2 + s, p).start()
        for p in range(4):
            if travels(s, p)[0]:
                sib_copy(2 * s - 1, c, p2 - s, p).start()
            if travels(s, p)[1]:
                sib_copy(2 * s, c, p2 + s, p).start()
    for p in range(4):
        sib_copy(0, 1 - c, p1, p).wait_recv()
    for s in range(1, half + 1):
        for p in range(4):
            if travels(s, p)[0]:
                sib_copy(2 * s - 1, 1 - c, p1 - s, p).wait_recv()
            if travels(s, p)[1]:
                sib_copy(2 * s, 1 - c, p1 + s, p).wait_recv()
    for d in range(1, ring):
        one_copy(d, p1).wait_send()
    for p in range(4):
        sib_copy(0, c, p2, p).wait_send()
    for s in range(1, half + 1):
        for p in range(4):
            if travels(s, p)[0]:
                fwd_copy(s, p2 - s + 1, p).wait_send()
                sib_copy(2 * s - 1, c, p2 - s, p).wait_send()
            if travels(s, p)[1]:
                bwd_copy(s, p2 + s - 1, p).wait_send()
                sib_copy(2 * s, c, p2 + s, p).wait_send()


def attend_kernel(ring, lanes, q_ref, kv, lens, obuf, lbuf, kfeat, qcat, acc, tot, top):
    rows = q_ref.shape[0]
    own = rows // lanes
    chunk = ring * own
    plane = ring * 2 * rows
    me, x, c, z, y = where(ring)

    lane = lax.broadcasted_iota(jnp.int32, (1, LANES), 1)
    line = lax.broadcasted_iota(jnp.int32, (LANES, 1), 0)
    ends = jnp.zeros((1, LANES), jnp.int32)
    begins = jnp.zeros((1, LANES), jnp.int32)
    ends_down = jnp.zeros((LANES, 1), jnp.int32)
    begins_down = jnp.zeros((LANES, 1), jnp.int32)
    for j in range(DOCS):
        length = lens[j]
        ends += jnp.where(lane >= j, length, 0)
        begins += jnp.where(lane > j, length, 0)
        ends_down += jnp.where(line >= j, length, 0)
        begins_down += jnp.where(line > j, length, 0)
    tok = lax.broadcasted_iota(jnp.int32, (LANES, rows), 1)
    col = lax.broadcasted_iota(jnp.int32, (LANES, rows), 0)
    pos = me * rows + tok
    hidden = jnp.where((col < DOCS) & ((pos < begins_down) | (pos >= ends_down)), -MASK, 0.0)
    hidden = jnp.where(col == DOCS, -MASK, hidden)
    first = col - 2 * DOCS
    later = (first >= 0) & (first < own) & (tok < x * own + first)
    hidden = jnp.where(later, -MASK, hidden).astype(jnp.bfloat16)
    for h in range(HEADS):
        turned = q_ref[:, h * DIM : (h + 1) * DIM].T
        qcat[:DIM, h * rows : (h + 1) * rows] = turned
        qcat[DIM:, h * rows : (h + 1) * rows] = hidden
    acc[...] = jnp.zeros_like(acc)
    tot[...] = jnp.zeros_like(tot)
    top[...] = jnp.full_like(top, EMPTY)

    def features(n, carry):
        cc, b = n // ring, lax.rem(n, ring)
        inner = lax.broadcasted_iota(jnp.int32, (own, LANES), 0)
        lanes_of = lax.broadcasted_iota(jnp.int32, (own, LANES), 1)
        for a in range(ring):
            zz, yy = place(cc, a, b)
            block = (zz * ring + yy) * 2 + cc
            at = block * rows + x * own + inner
            mark = ((at >= begins) & (at < ends)).astype(jnp.float32)
            mark = jnp.where((lanes_of == DOCS) & (block > me), 1.0, mark)
            mark = jnp.where((lanes_of == inner + 2 * DOCS) & (block == me), 1.0, mark)
            kfeat[cc, b, a * own : (a + 1) * own, :] = mark.astype(jnp.bfloat16)
        return carry

    lax.fori_loop(0, 2 * ring, features, 0)
    ones = jnp.ones((16, chunk), jnp.bfloat16)

    def scores(h, cc, b):
        keys = jnp.concatenate([kv[cc, b, 0], kfeat[cc, b]], axis=1)
        return jnp.dot(keys, qcat[:, h * rows : (h + 1) * rows], preferred_element_type=jnp.float32)

    def weighted(cc, b, p):
        vals = jnp.concatenate([kv[cc, b, 1, n : n + LANES] for n in range(0, chunk, LANES)], axis=1)
        return jnp.dot(jnp.concatenate([vals, ones], axis=0), p, preferred_element_type=jnp.float32)

    def fold(h, cc, b, s):
        old = top[h : h + 1, :]
        new = jnp.maximum(old, jnp.max(s, axis=0, keepdims=True))
        both = weighted(cc, b, jnp.exp2((s - new) * FACTOR).astype(jnp.bfloat16))
        alpha = jnp.exp2((old - new) * FACTOR)
        acc[h] = acc[h] * alpha + both[:DIM]
        tot[h : h + 1, :] = tot[h : h + 1, :] * alpha + both[DIM : DIM + 1]
        top[h : h + 1, :] = new

    def sweep(fold):
        def body(n, carry):
            cc, b = n // ring, lax.rem(n, ring)
            seen = (b <= z) & ((b + 1) * plane > me * rows - (MOST - 1))

            @pl.when((cc == 1) | seen)
            def _():
                s = scores(0, cc, b)
                for h in range(HEADS):
                    after = scores(h + 1, cc, b) if h + 1 < HEADS else None
                    fold(h, cc, b, s)
                    s = after

            return carry

        lax.fori_loop(0, 2 * ring, body, 0)

    sweep(fold)
    logs = []
    for h in range(HEADS):
        total = tot[h : h + 1, :]
        some = total > 0.0
        safe = jnp.where(some, total, 1.0)
        part = (acc[h] / safe).T.astype(jnp.bfloat16)
        logs.append(jnp.where(some, top[h : h + 1, :] * FACTOR + jnp.log2(safe), NOTHING))
        for j in range(lanes):
            obuf[j, :, h * DIM : (h + 1) * DIM] = part[j * own : (j + 1) * own, :]
    lbuf[...] = jnp.concatenate(logs, axis=0)


def merge_kernel(lanes, obuf, lbuf, out_ref, rbuf, logs, mixing, relay, s_out, r_out, s_log, r_log, s_rel, r_rel):
    x = lax.axis_index("ka")
    own = out_ref.shape[0]
    rows = lbuf.shape[1]
    near = [d for d in range(1, lanes) if lanes != 4 or d != 2]

    def peer(d):
        return lax.rem(x + d, lanes)

    def copy(src, dst, send, recv, d):
        return pltpu.make_async_remote_copy(
            src_ref=src, dst_ref=dst, send_sem=send, recv_sem=recv, device_id={"ka": peer(d)}, device_id_type=MESH
        )

    def cols_of(g):
        return pl.ds(g * 2 * DIM, 2 * DIM)

    def out_copy(d, g):
        cols = cols_of(g)
        return copy(obuf.at[peer(d), :, cols], rbuf.at[d, :, cols], s_out.at[d, g], r_out.at[d, g], d)

    def way(g):
        return 1 if g < HEADS // 4 else 3

    def relay_copy(g):
        cols = cols_of(g)
        return copy(obuf.at[peer(2), :, cols], relay.at[:, cols], s_rel.at[g], r_rel.at[g], way(g))

    def onward_copy(g):
        cols = cols_of(g)
        return copy(relay.at[:, cols], rbuf.at[2, :, cols], s_out.at[2, g], r_out.at[2, g], way(g))

    def log_copy(d):
        return copy(lbuf, logs.at[d], s_log.at[d], r_log.at[d], d)

    greet([{"ka": peer(d)} for d in range(1, lanes)])()
    groups = range(HEADS // 2)
    for d in range(1, lanes):
        log_copy(d).start()
    if lanes == 4:
        for g in (0, 2, 1, 3):
            relay_copy(g).start()
    for g in groups:
        for d in near:
            out_copy(d, g).start()
    if lanes == 4:
        for g in (0, 2, 1, 3):
            relay_copy(g).wait_recv()
            onward_copy(g).start()
    for d in range(1, lanes):
        log_copy(d).wait_recv()
    sizes = [lbuf[...]] + [logs[d] for d in range(1, lanes)]
    highest = functools.reduce(jnp.maximum, sizes)
    shares = [jnp.exp2(size - highest) for size in sizes]
    whole = functools.reduce(jnp.add, shares)
    shares = [share / whole for share in shares]
    shares.append(jnp.zeros((LANES - HEADS * lanes, rows), jnp.float32))
    mixing[...] = jnp.concatenate(shares, axis=0).T
    mix = mixing[pl.ds(pl.multiple_of(x * own, own), own), :]
    for g in groups:
        for d in range(1, lanes):
            out_copy(d, g).wait_recv()
        for h in (2 * g, 2 * g + 1):
            cols = slice(h * DIM, (h + 1) * DIM)
            mixed = mix[:, h : h + 1] * obuf[x, :, cols].astype(jnp.float32)
            for d in range(1, lanes):
                at = d * HEADS + h
                mixed += mix[:, at : at + 1] * rbuf[d, :, cols].astype(jnp.float32)
            out_ref[:, cols] = mixed.astype(out_ref.dtype)
    for d in range(1, lanes):
        log_copy(d).wait_send()
    for g in groups:
        for d in near:
            out_copy(d, g).wait_send()
        if lanes == 4:
            relay_copy(g).wait_send()
            onward_copy(g).wait_send()


def steady(ring, lanes, queries, keys, values, doc_lengths):
    rows, own = queries.shape[0], keys.shape[0]
    half = ring // 2
    chunk = ring * own
    vmem = pl.BlockSpec(memory_space=pltpu.VMEM)
    sems = pltpu.SemaphoreType.DMA
    limit = 48 * 1024 * 1024
    kv = pl.pallas_call(
        functools.partial(gather_kernel, ring),
        out_shape=jax.ShapeDtypeStruct((2, ring, 2, chunk, DIM), jnp.bfloat16),
        in_specs=[vmem, vmem],
        out_specs=vmem,
        scratch_shapes=[
            pltpu.VMEM((ring, own, 2 * DIM), jnp.bfloat16),
            sems((ring - 1,)), sems((ring - 1,)),
            sems((half, 4)), sems((half, 4)), sems((half, 4)), sems((half, 4)),
            sems((2 * half + 1, 4)), sems((2 * half + 1, 4)),
        ],
        compiler_params=pltpu.CompilerParams(collective_id=1, has_side_effects=True, vmem_limit_bytes=limit),
        name="gather",
    )(keys, values)
    parts, logs = pl.pallas_call(
        functools.partial(attend_kernel, ring, lanes),
        out_shape=(
            jax.ShapeDtypeStruct((lanes, own, HEADS * DIM), jnp.bfloat16),
            jax.ShapeDtypeStruct((HEADS, rows), jnp.float32),
        ),
        in_specs=[vmem, vmem, pl.BlockSpec(memory_space=pltpu.SMEM)],
        out_specs=(vmem, vmem),
        scratch_shapes=[
            pltpu.VMEM((2, ring, chunk, LANES), jnp.bfloat16),
            pltpu.VMEM((2 * DIM, HEADS * rows), jnp.bfloat16),
            pltpu.VMEM((HEADS, DIM, rows), jnp.float32),
            pltpu.VMEM((HEADS, rows), jnp.float32),
            pltpu.VMEM((HEADS, rows), jnp.float32),
        ],
        compiler_params=pltpu.CompilerParams(vmem_limit_bytes=limit),
        name="attend",
    )(queries, kv, doc_lengths)
    return pl.pallas_call(
        functools.partial(merge_kernel, lanes),
        out_shape=jax.ShapeDtypeStruct((own, HEADS * DIM), jnp.bfloat16),
        in_specs=[vmem, vmem],
        out_specs=vmem,
        scratch_shapes=[
            pltpu.VMEM((lanes, own, HEADS * DIM), jnp.bfloat16),
            pltpu.VMEM((lanes, HEADS, rows), jnp.float32),
            pltpu.VMEM((rows, LANES), jnp.float32),
            pltpu.VMEM((own, HEADS * DIM), jnp.bfloat16),
            sems((lanes, HEADS // 2)), sems((lanes, HEADS // 2)),
            sems((lanes,)), sems((lanes,)),
            sems((HEADS // 2,)), sems((HEADS // 2,)),
        ],
        compiler_params=pltpu.CompilerParams(collective_id=2, has_side_effects=True, vmem_limit_bytes=limit),
        name="merge",
    )(parts, logs)


def per_device(ring, lanes, queries, keys, values, doc_lengths):
    args = (queries, keys, values, doc_lengths)
    out, bound = swift(ring, lanes, *args)
    fits = bound[0] <= (SAFE / FACTOR) ** 2
    return lax.cond(fits, lambda *_: out, functools.partial(steady, ring, lanes), *args)


def solution(mesh):
    ring = math.isqrt(mesh.shape["pb"] // 2)
    return jax.shard_map(
        functools.partial(per_device, ring, mesh.shape["ka"]),
        mesh=mesh,
        in_specs=(P("pb", None), P(("pb", "ka"), None), P(("pb", "ka"), None), P()),
        out_specs=P(("pb", "ka"), None),
        check_vma=False,
    )
```
